32 devices in a mesh: term: 16 (over z, y, core), wave: 2 (over x).
Axes of the slice: x: 2, y: 2, z: 4, core: 2. Of those that a mesh axis runs over, the one named last changes fastest.
Arguments:
- spectral_state: bfloat16 [8, 512, 1280], P('wave', 'term'), may hold values from -6 to 6
- inverse: bfloat16 [16, 8, 2, 640, 640], P('term', 'wave'), may hold values from -0.15625 to 0.15625
- term_weights: float32 [16, 2], P('term'), may hold values from -4 to 4
- legendre: bfloat16 [8, 640, 1280], P('wave'), may hold values from -0.25 to 0.25
- slot_column: int32 [8], replicated, may hold values from 0 to 7, each once
Outputs:
- fourier: float32 [8, 2, 512, 1280], P(None, None, 'term', 'wave')
The draws below stay inside these ranges and needn't reach their ends.
Inputs may be any that keep to these rules, and one draw needn't show every extreme that they name: `slot_column`: each column appears in exactly one slot.
All inputs are finite; a program needn't handle non-finite values.
Results may differ from the reference program's by a relative error of at most 0.0003.
Values may be sent and summed in bfloat16 or wider, within the bound.
No kernel may reach another device: no remote copies, remote signals or barrier semaphores. Data moves between devices by JAX's collectives and lax.ppermute only.
A program may use at most 128 MiB of HBM per device.

```python
import jax
import jax.numpy as jnp
from jax import lax

NDEG = 640
NLAT = 1280
COLS = 512
M_TOT = 8
TERMS = 16


def block_scale(own_key, dims, shards, least, top_value):
    def one(axis_at, shards_of):
        heights = jax.random.uniform(jax.random.fold_in(jax.random.fold_in(own_key, 6), axis_at), (shards_of,), jnp.float32, least / len(shards), top_value / len(shards))
        return jnp.repeat(jnp.exp(heights), dims[axis_at] // shards_of).reshape((-1,) + (1,) * (len(dims) - axis_at - 1))

    level = one(*shards[0])
    for cut in shards[1:]:
        level = level * one(*cut)
    return level


def bell_draw(own_key, shape, deviation, limit, cuts=(), kind=jnp.bfloat16):
    values = deviation * jax.random.normal(own_key, shape, jnp.float32)
    if cuts:
        values = values * block_scale(own_key, shape, cuts, -0.22, 0.18)
    return jnp.clip(values, -limit, limit).astype(kind)


def setup_inputs(seed: int = 0) -> dict:
    streams_of = jax.random.split(jax.random.key(seed), 6)
    spectral_state = bell_draw(streams_of[0], (M_TOT, COLS, 2 * NDEG), 1.0, 6.0, ((0, 2), (1, 16)))
    inverse = bell_draw(streams_of[1], (TERMS, M_TOT, 2, NDEG, NDEG), (2 * NDEG) ** -0.5, 0.15625, ((0, 16), (1, 2)))
    term_weights = bell_draw(streams_of[2], (TERMS, 2), (TERMS ** -0.5), 4.0, ((0, 16),), jnp.float32)
    legendre = bell_draw(streams_of[3], (M_TOT, NDEG, NLAT), NDEG ** -0.5, 0.25, ((0, 2),))
    slot_column = jax.random.permutation(streams_of[4], M_TOT).astype(jnp.int32)
    return {"spectral_state": spectral_state, "inverse": inverse, "term_weights": term_weights, "legendre": legendre, "slot_column": slot_column}


def reference(spectral_state, inverse, term_weights, legendre, slot_column):
    highest = lax.Precision.HIGHEST

    def one_slot(slot_index):
        values = lax.dynamic_index_in_dim(spectral_state, slot_index, 0, keepdims=False)
        blocks = lax.dynamic_index_in_dim(inverse, slot_index, 1, keepdims=False)
        table = lax.dynamic_index_in_dim(legendre, slot_index, 0, keepdims=False)
        middle = values.shape[1] // 2
        real_in = values[:, :middle].astype(jnp.float32)
        imag_in = values[:, middle:].astype(jnp.float32)
        real_block = blocks[:, 0].astype(jnp.float32)
        imag_block = blocks[:, 1].astype(jnp.float32)
        real_real = jnp.einsum("cn,kno->kco", real_in, real_block, precision=highest)
        imag_imag = jnp.einsum("cn,kno->kco", imag_in, imag_block, precision=highest)
        real_imag = jnp.einsum("cn,kno->kco", real_in, imag_block, precision=highest)
        imag_real = jnp.einsum("cn,kno->kco", imag_in, real_block, precision=highest)
        solved_re = real_real - imag_imag
        solved_im = real_imag + imag_real
        weight_re = term_weights[:, 0][:, None, None]
        weight_im = term_weights[:, 1][:, None, None]
        total_re = jnp.sum(weight_re * solved_re - weight_im * solved_im, axis=0)
        total_im = jnp.sum(weight_re * solved_im + weight_im * solved_re, axis=0)
        total = jnp.stack([total_re, total_im], axis=0)
        return jnp.einsum("pcn,nl->pcl", total, table.astype(jnp.float32), precision=highest)

    slot_count = spectral_state.shape[0]
    grids = lax.map(one_slot, jnp.arange(slot_count, dtype=jnp.int32))
    fourier = jnp.zeros(grids.shape, jnp.float32).at[slot_column].set(grids)
    return fourier
```

```python
import functools

import jax
import jax.numpy as jnp
from jax import lax
from jax.experimental import pallas as pl
from jax.experimental.pallas import tpu as pltpu
from jax.sharding import PartitionSpec as P

F32, BF16, I16, I32 = jnp.float32, jnp.bfloat16, jnp.int16, jnp.int32
LANES = 128
STEPS = 64.0
TOP = 32000.0
TINY = 1e-30


def params(mib=40):
    return pltpu.CompilerParams(vmem_limit_bytes=mib * 2**20)


def split(x):
    hi = x.astype(BF16)
    return hi, (x - hi.astype(F32)).astype(BF16)


def lane_block(width):
    return 256 if width % 256 == 0 else LANES


def encode(x):
    top = jnp.maximum(jnp.max(jnp.abs(x), axis=1, keepdims=True), TINY)
    step = jnp.ceil(jnp.log2(top / TOP) * STEPS)
    code = jnp.round(x * jnp.exp2(step * (-1.0 / STEPS)))
    return code.astype(I32).astype(I16), step


def put_steps(steps, rows):
    lane = lax.broadcasted_iota(I32, (rows, LANES), 1)
    out = jnp.zeros((rows, LANES), F32)
    for n, step in enumerate(steps):
        out = jnp.where(lane == n, step, out)
    return out.astype(I32).astype(I16)


def encode_rows(x):
    rows, width = x.shape
    nb = lane_block(width)
    pairs = [encode(x[:, i : i + nb]) for i in range(0, width, nb)]
    return [p[0] for p in pairs] + [put_steps([p[1] for p in pairs], rows)]


def decode_rows(coded, width):
    nb = lane_block(width)
    scale = jnp.exp2(coded[:, width:].astype(I32).astype(F32) * (1.0 / STEPS))
    return [
        coded[:, i : i + nb].astype(I32).astype(F32) * scale[:, n : n + 1]
        for n, i in enumerate(range(0, width, nb))
    ]


def operator_kernel(pos, w_own, w_got, own, got, out):
    size = own.shape[-1]
    real = jnp.zeros(own.shape[-2:], F32)
    imag = jnp.zeros(own.shape[-2:], F32)
    for k in range(own.shape[0]):
        for w, block in ((w_own, own[k, 0]), (w_got, got[k])):
            r, j = block[0].astype(F32), block[1].astype(F32)
            real += w[k, 0] * r - w[k, 1] * j
            imag += w[k, 0] * j + w[k, 1] * r
    for level, (r, j) in enumerate(zip(split(real), split(imag))):
        out[level, 0, :, :size] = r
        out[level, 0, :, size:] = j
        out[level, 1, :, :size] = -j
        out[level, 1, :, size:] = r


def make_operator(at, w_own, w_got, inverse, got):
    terms, _, _, size, _ = inverse.shape
    rows = LANES
    smem = pl.BlockSpec(memory_space=pltpu.SMEM)
    out = pl.pallas_call(
        operator_kernel,
        out_shape=jax.ShapeDtypeStruct((2, 2, size, 2 * size), BF16),
        grid_spec=pltpu.PrefetchScalarGridSpec(
            num_scalar_prefetch=1,
            grid=(size // rows,),
            in_specs=[
                smem,
                smem,
                pl.BlockSpec((terms, 1, 2, rows, size), lambda i, pos: (0, pos[0], 0, i, 0)),
                pl.BlockSpec((terms, 2, rows, size), lambda i, pos: (0, 0, i, 0)),
            ],
            out_specs=pl.BlockSpec((2, 2, rows, 2 * size), lambda i, pos: (0, 0, i, 0)),
        ),
        compiler_params=params(),
        cost_estimate=pl.CostEstimate(
            flops=16 * terms * size * size, bytes_accessed=24 * size * size, transcendentals=0
        ),
        name="operator",
    )(at, w_own, w_got, inverse, got)
    return out.reshape(2, 2 * size, 2 * size)


def product_kernel(coded, count, *refs):
    parts, op, out, full = refs[:count], refs[count], refs[count + 1], refs[count + 2]
    rows = parts[0].shape[0]
    n = pl.program_id(0)

    @pl.when(n == 0)
    def _():
        for i, part in enumerate(parts):
            full[i * rows : (i + 1) * rows, :] = part[...]

    x = full[...]
    acc = jnp.dot(x, op[0], preferred_element_type=F32)
    acc += jnp.dot(x, op[1], preferred_element_type=F32)
    if not coded:
        out[...] = acc
        return
    steps = refs[count + 3]
    width, nb = x.shape[1], op.shape[2]
    code, step = encode(acc)
    out[:, pl.ds(pl.multiple_of(n * nb, nb), nb)] = code
    lane = lax.broadcasted_iota(I32, steps.shape, 1)
    steps[...] = jnp.where(lane == n, step, steps[...])

    @pl.when(n == pl.num_programs(0) - 1)
    def _():
        out[:, width:] = steps[...].astype(I32).astype(I16)


def product(parts, op, coded):
    count = len(parts)
    part_rows, width = parts[0].shape
    rows = count * part_rows
    nb = lane_block(width)
    scratch = [pltpu.VMEM((rows, width), BF16)]
    if coded:
        out_shape = jax.ShapeDtypeStruct((rows, width + LANES), I16)
        out_spec = pl.BlockSpec((rows, width + LANES), lambda n: (0, 0))
        scratch.append(pltpu.VMEM((rows, LANES), F32))
    else:
        out_shape = jax.ShapeDtypeStruct((rows, width), F32)
        out_spec = pl.BlockSpec((rows, nb), lambda n: (0, n))
    return pl.pallas_call(
        functools.partial(product_kernel, coded, count),
        out_shape=out_shape,
        grid=(width // nb,),
        in_specs=[pl.BlockSpec((part_rows, width), lambda n: (0, 0))] * count
        + [pl.BlockSpec((2, width, nb), lambda n: (0, 0, n))],
        out_specs=out_spec,
        scratch_shapes=scratch,
        compiler_params=params(),
        cost_estimate=pl.CostEstimate(
            flops=4 * rows * width * width,
            bytes_accessed=4 * width * width + 4 * rows * width,
            transcendentals=0,
        ),
        name="product",
    )(*parts, op)


def fold_kernel(count, own, got, *outs):
    rows, width = outs[0].shape
    nb = lane_block(width)
    for q in range(count):
        at = slice(q * rows, (q + 1) * rows)
        pieces = decode_rows(got[at, :], width)
        total = [own[at, n * nb : (n + 1) * nb] + piece for n, piece in enumerate(pieces)]
        if q == 0:
            for n, piece in enumerate(total):
                outs[0][:, n * nb : (n + 1) * nb] = piece
        else:
            pairs = [encode(piece) for piece in total]
            for n, pair in enumerate(pairs):
                outs[q][:, n * nb : (n + 1) * nb] = pair[0]
            outs[q][:, width:] = put_steps([p[1] for p in pairs], rows)


def fold(own, got, count):
    rows, width = own.shape[0] // count, own.shape[1]
    return pl.pallas_call(
        functools.partial(fold_kernel, count),
        out_shape=[jax.ShapeDtypeStruct((rows, width), F32)]
        + [jax.ShapeDtypeStruct((rows, width + LANES), I16)] * (count - 1),
        compiler_params=params(),
        cost_estimate=pl.CostEstimate(
            flops=10 * own.size, bytes_accessed=10 * own.size, transcendentals=0
        ),
        name="fold",
    )(own, got)


def total_rows(own, got):
    width = own.shape[1]
    nb = lane_block(width)
    pieces = [own[:, i : i + nb] for i in range(0, width, nb)]
    for part in got:
        pieces = [a + b for a, b in zip(pieces, decode_rows(part[...], width))]
    return jnp.concatenate(pieces, axis=1)


def synthesis_kernel(bands, count, pos, own, *refs):
    got, table, outs, values = refs[:count], refs[count], refs[count + 1 : -1], refs[-1]
    rows, width = own.shape
    size = width // 2
    half = rows // 2
    band = pl.program_id(0)

    @pl.when(band == 0)
    def _():
        total = total_rows(own, got)
        for part in range(2):
            hi, lo = split(total[:, part * size : (part + 1) * size])
            values[0, part * rows : (part + 1) * rows, :] = hi
            values[1, part * rows : (part + 1) * rows, :] = lo

    grid = jnp.dot(values[0], table[0], preferred_element_type=F32)
    grid += jnp.dot(values[1], table[0], preferred_element_type=F32)
    for d in range(bands):

        @pl.when(band == d)
        def _():
            for side in range(2):
                for part in range(2):
                    start = part * rows + side * half
                    outs[2 * d + side][part] = grid[start : start + half]


def synthesis(at, own, got, legendre, bands):
    rows, width = own.shape
    size, nlat = legendre.shape[1:]
    band = nlat // bands
    piece = (2, rows // 2, band)
    return pl.pallas_call(
        functools.partial(synthesis_kernel, bands, len(got)),
        out_shape=[jax.ShapeDtypeStruct(piece, F32)] * (2 * bands),
        grid_spec=pltpu.PrefetchScalarGridSpec(
            num_scalar_prefetch=1,
            grid=(bands,),
            in_specs=[pl.BlockSpec((rows, width), lambda b, pos: (0, 0))]
            + [pl.BlockSpec((rows, width + LANES), lambda b, pos: (0, 0))] * len(got)
            + [pl.BlockSpec((1, size, band), lambda b, pos: (pos[0], 0, pos[1] ^ b))],
            out_specs=[pl.BlockSpec(piece, lambda b, pos: (0, 0, 0))] * (2 * bands),
            scratch_shapes=[pltpu.VMEM((2, 2 * rows, size), BF16)],
        ),
        compiler_params=params(),
        cost_estimate=pl.CostEstimate(
            flops=8 * rows * size * nlat,
            bytes_accessed=2 * size * nlat + 8 * rows * nlat,
            transcendentals=0,
        ),
        name="synthesis",
    )(at, own, *got, legendre)


def sum_kernel(own, *refs):
    refs[-1][...] = total_rows(own, refs[:-1])


def plain_synthesis(at, own, got, legendre, bands):
    rows, width = own.shape
    size, nlat = legendre.shape[1:]
    total = pl.pallas_call(
        sum_kernel, out_shape=jax.ShapeDtypeStruct(own.shape, F32), name="total"
    )(own, *got)
    table = lax.dynamic_index_in_dim(legendre, at[0], 0, keepdims=False)
    values = jnp.stack([total[:, :size], total[:, size:]])
    grid = sum(
        jnp.einsum("pcn,nl->pcl", v, table, preferred_element_type=F32) for v in split(values)
    )
    half, band = rows // 2, nlat // bands
    return [
        lax.dynamic_slice(
            grid, (0, side * half, (at[1] ^ d) * band), (2, half, band)
        )
        for d in range(bands)
        for side in range(2)
    ]


def place_kernel(count, dst, *refs):
    pieces, out = refs[:count], refs[count]
    for i in range(count):

        @pl.when(pl.program_id(0) == i)
        def _():
            out[0] = pieces[i][...]


def place(dst, pieces):
    count = len(pieces)
    shape = pieces[0].shape
    return pl.pallas_call(
        functools.partial(place_kernel, count),
        out_shape=jax.ShapeDtypeStruct((count,) + shape, F32),
        grid_spec=pltpu.PrefetchScalarGridSpec(
            num_scalar_prefetch=1,
            grid=(count,),
            in_specs=[pl.BlockSpec(shape, lambda i, dst: (0, 0, 0))] * count,
            out_specs=pl.BlockSpec((1,) + shape, lambda i, dst: (dst[i], 0, 0, 0)),
        ),
        compiler_params=params(),
        name="place",
    )(dst, *pieces)


def shards(mesh, spectral_state, inverse, term_weights, legendre, slot_column):
    terms, waves = mesh.shape["term"], mesh.shape["wave"]
    slots, cols, width = spectral_state.shape
    mine = slots // 2
    outer = terms // 4
    me, wave = lax.axis_index("term"), lax.axis_index("wave")
    core = me % 2

    def swap(x, term_bits, wave_bits=0):
        pairs = [
            (t * waves + w, (t ^ term_bits) * waves + (w ^ wave_bits))
            for t in range(terms)
            for w in range(waves)
        ]
        return lax.ppermute(x, ("term", "wave"), pairs)

    def half_of(x, which, dim):
        return lax.dynamic_slice_in_dim(x, which * mine, mine, dim)

    state_got = swap(half_of(spectral_state, 1 - core, 0), 1)
    state_own = half_of(spectral_state, core, 0)
    weights_got = swap(term_weights, 1)
    away = half_of(inverse, 1 - core, 1)
    blocks = [jnp.concatenate([state_own[j], state_got[j]], axis=0) for j in range(mine)]
    inverse_got = [swap(away[:, j], 1) for j in range(mine)]

    pieces = []
    for j in range(mine):
        at = jnp.stack([core * mine + j, wave]).astype(I32)
        op = make_operator(at, term_weights, weights_got, inverse, inverse_got[j])
        near = [blocks[j]] + [swap(blocks[j], q * 4) for q in range(1, outer)]
        far = [swap(block, 2) for block in near]
        sent = swap(product(far, op, True), 2)
        own = product(near, op, False)
        folded = fold(own, sent, outer)
        got = [swap(folded[q], q * 4) for q in range(1, outer)]
        make = synthesis if legendre.shape[2] // waves % LANES == 0 else plain_synthesis
        grid = make(at, folded[0], got, legendre, waves)
        for d in range(waves):
            for side in range(2):
                piece = grid[2 * d + side]
                if d or side:
                    piece = swap(piece, side, d)
                slot = (wave ^ d) * slots + (core ^ side) * mine + j
                pieces.append((slot, piece))

    dst = jnp.stack([slot_column[slot] for slot, _ in pieces])
    return place(dst, [piece for _, piece in pieces])


def solution(mesh):
    return jax.shard_map(
        functools.partial(shards, mesh),
        mesh=mesh,
        in_specs=(
            P("wave", "term", None),
            P("term", "wave", None, None, None),
            P("term", None),
            P("wave", None, None),
            P(),
        ),
        out_specs=P(None, None, "term", "wave"),
        check_vma=False,
    )
```

```python
import functools

import jax
import jax.numpy as jnp
from jax import lax
from jax.experimental import pallas as pl
from jax.experimental.pallas import tpu as pltpu
from jax.sharding import PartitionSpec as P

F32, BF16, I16, I32 = jnp.float32, jnp.bfloat16, jnp.int16, jnp.int32
LANES = 128
TAIL = 16
STEPS = 64.0
TOP = 32000.0
TINY = 1e-30


def params(mib=48):
    return pltpu.CompilerParams(vmem_limit_bytes=mib * 2**20)


def split(x):
    hi = x.astype(BF16)
    return hi, (x - hi.astype(F32)).astype(BF16)


def encode(x):
    top = jnp.maximum(jnp.max(jnp.abs(x), axis=0, keepdims=True), TINY)
    step = jnp.ceil(jnp.log2(top * (1.0 / TOP)) * STEPS)
    code = jnp.round(x * jnp.exp2(step * (-1.0 / STEPS)))
    return code.astype(I32).astype(I16), step


def put_row(tail, row, values):
    at = lax.broadcasted_iota(I32, tail.shape, 0)
    return jnp.where(at == row, values, tail)


def scales(tail):
    return jnp.exp2(tail.astype(I32).astype(F32) * (1.0 / STEPS))


def take_row(table, row):
    at = lax.broadcasted_iota(I32, table.shape, 0)
    return jnp.sum(jnp.where(at == row, table, 0.0), axis=0, keepdims=True)


def message(strips, rows):
    return jax.ShapeDtypeStruct((strips * rows + TAIL, LANES), I16)


def whole(shape):
    return pl.BlockSpec(shape, lambda *_: (0,) * len(shape))


def weighted(w_own, w_got, own, got):
    real = imag = 0.0
    for k in range(own.shape[0]):
        for w, block in ((w_own, own[k, 0]), (w_got, got[k])):
            r, j = block[0].astype(F32), block[1].astype(F32)
            real += w[k, 0] * r - w[k, 1] * j
            imag += w[k, 0] * j + w[k, 1] * r
    return real, imag


def share_kernel(pos, w_own, w_got, own, got, out, tail):
    t = pl.program_id(0)
    size = own.shape[3]
    end = out.shape[0] - TAIL

    @pl.when(t == 0)
    def _():
        tail[...] = jnp.zeros_like(tail)

    for part, value in enumerate(weighted(w_own, w_got, own, got)):
        strip = 2 * t + part
        code, step = encode(value)
        out[pl.ds(pl.multiple_of(strip * size, TAIL), size), :] = code
        tail[...] = put_row(tail[...], strip, step)

    @pl.when(t == pl.num_programs(0) - 1)
    def _():
        out[end:, :] = tail[...].astype(I32).astype(I16)


def own_kernel(pos, w_own, w_got, own, got, out):
    for part, value in enumerate(weighted(w_own, w_got, own, got)):
        out[0, part] = value


def operator(slot, w_own, w_got, inverse, got, first, count, coded):
    terms, _, _, size, _ = inverse.shape
    smem = pl.BlockSpec(memory_space=pltpu.SMEM)
    if coded:
        out_shape = message(2 * count, size)
        out_spec = whole(out_shape.shape)
    else:
        out_shape = jax.ShapeDtypeStruct((count, 2, size, LANES), F32)
        out_spec = pl.BlockSpec((1, 2, size, LANES), lambda t, slot: (t, 0, 0, 0))
    return pl.pallas_call(
        share_kernel if coded else own_kernel,
        out_shape=out_shape,
        grid_spec=pltpu.PrefetchScalarGridSpec(
            num_scalar_prefetch=1,
            grid=(count,),
            in_specs=[
                smem,
                smem,
                pl.BlockSpec(
                    (terms, 1, 2, size, LANES), lambda t, slot: (0, slot[0], 0, 0, t + first)
                ),
                pl.BlockSpec((terms, 2, size, LANES), lambda t, slot: (0, 0, 0, t + first)),
            ],
            out_specs=out_spec,
            scratch_shapes=[pltpu.VMEM((TAIL, LANES), F32)] if coded else [],
        ),
        compiler_params=params(),
        cost_estimate=pl.CostEstimate(
            flops=32 * terms * size * LANES * count,
            bytes_accessed=16 * size * LANES * count,
            transcendentals=0,
        ),
        name="share" if coded else "operator",
    )(slot, w_own, w_got, inverse, got)


def product_kernel(count, tiles, *refs):
    parts, own, got = refs[:count], refs[count], refs[count + 1]
    near, sends = refs[count + 2], refs[count + 3 : 2 * count + 2]
    full, op, tails = refs[2 * count + 2 :]
    rows, width = parts[0].shape
    size = width // 2
    t = pl.program_id(0)

    @pl.when(t == 0)
    def _():
        tails[...] = jnp.zeros_like(tails)
        for i, part in enumerate(parts):
            full[i * rows : (i + 1) * rows, :] = part[...]

    table = scales(got[2 * tiles * size :, :])
    pair = []
    for part in range(2):
        strip = 2 * t + part
        code = got[pl.ds(pl.multiple_of(strip * size, TAIL), size), :]
        pair.append(own[0, part] + code.astype(I32).astype(F32) * take_row(table, strip))
    for level, (r, j) in enumerate(zip(split(pair[0]), split(pair[1]))):
        op[level, :size, :LANES] = r
        op[level, :size, LANES:] = j
        op[level, size:, :LANES] = -j
        op[level, size:, LANES:] = r
    x = full[...]
    acc = jnp.dot(x, op[0], preferred_element_type=F32)
    acc += jnp.dot(x, op[1], preferred_element_type=F32)
    near[0] = acc[:rows]
    for q in range(1, count):
        for part in range(2):
            strip = 2 * t + part
            block = acc[q * rows : (q + 1) * rows, part * LANES : (part + 1) * LANES]
            code, step = encode(block)
            sends[q - 1][pl.ds(pl.multiple_of(strip * rows, TAIL), rows), :] = code
            tails[q - 1] = put_row(tails[q - 1], strip, step)

    @pl.when(t == tiles - 1)
    def _():
        for q in range(1, count):
            sends[q - 1][2 * tiles * rows :, :] = tails[q - 1].astype(I32).astype(I16)


def product(parts, own, got, first, tiles):
    count = len(parts)
    rows, width = parts[0].shape
    size = width // 2
    send = message(2 * tiles, rows)
    return pl.pallas_call(
        functools.partial(product_kernel, count, tiles),
        out_shape=[jax.ShapeDtypeStruct((tiles, rows, 2 * LANES), F32)] + [send] * (count - 1),
        grid=(tiles,),
        in_specs=[whole((rows, width))] * count
        + [
            pl.BlockSpec((1, 2, size, LANES), lambda t: (t + first, 0, 0, 0)),
            whole(got.shape),
        ],
        out_specs=[pl.BlockSpec((1, rows, 2 * LANES), lambda t: (t, 0, 0))]
        + [whole(send.shape)] * (count - 1),
        scratch_shapes=[
            pltpu.VMEM((count * rows, width), BF16),
            pltpu.VMEM((2, width, 2 * LANES), BF16),
            pltpu.VMEM((count - 1, TAIL, LANES), F32),
        ],
        compiler_params=params(),
        cost_estimate=pl.CostEstimate(
            flops=8 * count * rows * width * tiles * LANES,
            bytes_accessed=12 * size * LANES * tiles + 2 * count * rows * width,
            transcendentals=0,
        ),
        name="product",
    )(*parts, own, got)


def add_up(near, got, write):
    base = 0
    for own, parts in zip(near, got):
        tiles, rows, _ = own.shape
        tables = [scales(part[2 * tiles * rows :, :]) for part in parts]
        for t in range(tiles):
            for part in range(2):
                strip = 2 * t + part
                total = own[t, :, part * LANES : (part + 1) * LANES]
                for ref, table in zip(parts, tables):
                    code = ref[strip * rows : (strip + 1) * rows, :]
                    total += code.astype(I32).astype(F32) * table[strip : strip + 1, :]
                write(base + t, part, total)
        base += tiles


def unpack(refs, chunks, count):
    near = refs[:chunks]
    got = [refs[chunks + i * count : chunks + (i + 1) * count] for i in range(chunks)]
    return near, got, refs[chunks * (1 + count) :]


def synthesis_kernel(bands, chunks, count, pos, *refs):
    near, got, rest = unpack(refs, chunks, count)
    table, outs, values = rest[0], rest[1:-1], rest[-1]
    rows = near[0].shape[1]
    band = pl.program_id(0)

    @pl.when(band == 0)
    def _():
        def write(tile, part, total):
            for level, value in enumerate(split(total)):
                values[
                    level, part * rows : (part + 1) * rows, tile * LANES : (tile + 1) * LANES
                ] = value

        add_up(near, got, write)

    grid = jnp.dot(values[0], table[0], preferred_element_type=F32)
    grid += jnp.dot(values[1], table[0], preferred_element_type=F32)
    quarter = rows // 4
    for d in range(bands):

        @pl.when(band == d)
        def _():
            for side in range(4):
                for part in range(2):
                    start = part * rows + side * quarter
                    outs[4 * d + side][part] = grid[start : start + quarter]


def synthesis(pos, near, got, legendre, bands):
    rows = near[0].shape[1]
    size, nlat = legendre.shape[1:]
    band = nlat // bands
    piece = (2, rows // 4, band)
    operands = list(near) + [part for parts in got for part in parts]
    return pl.pallas_call(
        functools.partial(synthesis_kernel, bands, len(near), len(got[0])),
        out_shape=[jax.ShapeDtypeStruct(piece, F32)] * (4 * bands),
        grid_spec=pltpu.PrefetchScalarGridSpec(
            num_scalar_prefetch=1,
            grid=(bands,),
            in_specs=[whole(x.shape) for x in operands]
            + [pl.BlockSpec((1, size, band), lambda b, pos: (pos[0], 0, pos[1] ^ b))],
            out_specs=[whole(piece)] * (4 * bands),
            scratch_shapes=[pltpu.VMEM((2, 2 * rows, size), BF16)],
        ),
        compiler_params=params(),
        cost_estimate=pl.CostEstimate(
            flops=8 * rows * size * nlat,
            bytes_accessed=2 * size * nlat + 8 * rows * nlat,
            transcendentals=0,
        ),
        name="synthesis",
    )(pos, *operands, legendre)


def total_kernel(chunks, count, *refs):
    near, got, (out,) = unpack(refs, chunks, count)

    def write(tile, part, total):
        out[part, :, tile * LANES : (tile + 1) * LANES] = total

    add_up(near, got, write)


def plain_synthesis(pos, near, got, legendre, bands):
    rows = near[0].shape[1]
    size, nlat = legendre.shape[1:]
    total = pl.pallas_call(
        functools.partial(total_kernel, len(near), len(got[0])),
        out_shape=jax.ShapeDtypeStruct((2, rows, size), F32),
        compiler_params=params(),
        name="total",
    )(*near, *[part for parts in got for part in parts])
    table = lax.dynamic_index_in_dim(legendre, pos[0], 0, keepdims=False)
    grid = sum(
        jnp.einsum("pcn,nl->pcl", v, table, preferred_element_type=F32) for v in split(total)
    )
    quarter, band = rows // 4, nlat // bands
    return [
        lax.dynamic_slice(grid, (0, side * quarter, (pos[1] ^ d) * band), (2, quarter, band))
        for d in range(bands)
        for side in range(4)
    ]


def place_kernel(count, dst, *refs):
    pieces, out = refs[:count], refs[count]
    for i in range(count):

        @pl.when(pl.program_id(0) == i)
        def _():
            out[0] = pieces[i][...]


def place(dst, pieces):
    count = len(pieces)
    shape = pieces[0].shape
    return pl.pallas_call(
        functools.partial(place_kernel, count),
        out_shape=jax.ShapeDtypeStruct((count,) + shape, F32),
        grid_spec=pltpu.PrefetchScalarGridSpec(
            num_scalar_prefetch=1,
            grid=(count,),
            in_specs=[whole(shape)] * count,
            out_specs=pl.BlockSpec((1,) + shape, lambda i, dst: (dst[i], 0, 0, 0)),
        ),
        compiler_params=params(),
        name="place",
    )(dst, *pieces)


def shards(mesh, spectral_state, inverse, term_weights, legendre, slot_column):
    terms, waves = mesh.shape["term"], mesh.shape["wave"]
    slots, cols, width = spectral_state.shape
    size = width // 2
    outer = terms // 4
    me, wave = lax.axis_index("term"), lax.axis_index("wave")
    place_of = me % 4
    turn = slots // 4

    def swap(x, term_bits, wave_bits=0):
        pairs = [
            (t * waves + w, (t ^ term_bits) * waves + (w ^ wave_bits))
            for t in range(terms)
            for w in range(waves)
        ]
        return lax.ppermute(x, ("term", "wave"), pairs)

    tiles = size // LANES
    cut = (tiles + 1) // 2
    chunks = [(0, cut), (cut, tiles - cut)] if tiles > 1 else [(0, tiles)]

    pieces = []
    for j in range(turn):
        slot_of = lambda bits: (place_of ^ bits) * turn + j
        state_of = lambda bits: lax.dynamic_index_in_dim(
            spectral_state, slot_of(bits), 0, keepdims=False
        )
        block = jnp.concatenate(
            [state_of(0)] + [swap(state_of(bits), bits) for bits in range(1, 4)], axis=0
        )
        parts = [block] + [swap(block, q * 4) for q in range(1, outer)]

        w_got = swap(term_weights, 1)
        from_core = lambda bits: swap(
            lax.dynamic_index_in_dim(inverse, slot_of(bits ^ 1), 1, keepdims=False), 1
        )
        far, own = from_core(2), from_core(0)
        scalar = lambda x: jnp.reshape(x, (1,)).astype(I32)
        shares = [
            swap(
                operator(scalar(slot_of(2)), term_weights, w_got, inverse, far, *chunk, True), 2
            )
            for chunk in chunks
        ]
        mine = operator(scalar(slot_of(0)), term_weights, w_got, inverse, own, 0, tiles, False)
        near, got = [], []
        for chunk, share in zip(chunks, shares):
            made = product(parts, mine, share, *chunk)
            near.append(made[0])
            got.append([swap(made[q], q * 4) for q in range(1, outer)])
        pos = jnp.stack([slot_of(0), wave]).astype(I32)
        make = synthesis if legendre.shape[2] // waves % LANES == 0 else plain_synthesis
        grid = make(pos, near, got, legendre, waves)
        for d in range(waves):
            for bits in range(4):
                piece = grid[4 * d + bits]
                if d or bits:
                    piece = swap(piece, bits, d)
                pieces.append(((wave ^ d) * slots + slot_of(bits), piece))

    at = jnp.stack([slot for slot, _ in pieces])
    return place(slot_column[at], [piece for _, piece in pieces])


def solution(mesh):
    return jax.shard_map(
        functools.partial(shards, mesh),
        mesh=mesh,
        in_specs=(
            P("wave", "term", None),
            P("term", "wave", None, None, None),
            P("term", None),
            P("wave", None, None),
            P(),
        ),
        out_specs=P(None, None, "term", "wave"),
        check_vma=False,
    )
```

```python
import functools

import jax
import jax.numpy as jnp
from jax import lax
from jax.experimental import pallas as pl
from jax.experimental.pallas import tpu as pltpu
from jax.sharding import PartitionSpec as P

F32, BF16, I16, I32 = jnp.float32, jnp.bfloat16, jnp.int16, jnp.int32
LANES = 128
TAIL = 16
STEPS = 64.0
TOP = 32000.0
TINY = 1e-30


def params(mib=48):
    return pltpu.CompilerParams(vmem_limit_bytes=mib * 2**20)


def split(x):
    hi = x.astype(BF16)
    return hi, (x - hi.astype(F32)).astype(BF16)


def encode(x):
    top = jnp.maximum(jnp.max(jnp.abs(x), axis=0, keepdims=True), TINY)
    step = jnp.ceil(jnp.log2(top * (1.0 / TOP)) * STEPS)
    code = jnp.round(x * jnp.exp2(step * (-1.0 / STEPS)))
    return code.astype(I32).astype(I16), step


def put_row(tail, row, values):
    at = lax.broadcasted_iota(I32, tail.shape, 0)
    return jnp.where(at == row, values, tail)


def scales(tail):
    return jnp.exp2(tail.astype(I32).astype(F32) * (1.0 / STEPS))


def message(strips, rows):
    return jax.ShapeDtypeStruct((strips * rows + TAIL, LANES), I16)


def whole(shape):
    return pl.BlockSpec(shape, lambda *_: (0,) * len(shape))


def weighted(w_own, w_got, own, got):
    real = imag = 0.0
    for k in range(own.shape[0]):
        for w, block in ((w_own, own[k, 0]), (w_got, got[k])):
            r, j = block[0].astype(F32), block[1].astype(F32)
            real += w[k, 0] * r - w[k, 1] * j
            imag += w[k, 0] * j + w[k, 1] * r
    return real, imag


def share_kernel(after, where, w_own, w_got, own, got, *refs):
    out, tail = refs[after:]
    t = pl.program_id(0)
    size = own.shape[3]
    end = out.shape[0] - TAIL

    @pl.when(t == 0)
    def _():
        tail[...] = jnp.zeros_like(tail)

    for part, value in enumerate(weighted(w_own, w_got, own, got)):
        strip = 2 * t + part
        code, step = encode(value)
        out[pl.ds(pl.multiple_of(strip * size, TAIL), size), :] = code
        tail[...] = put_row(tail[...], strip, step)

    @pl.when(t == pl.num_programs(0) - 1)
    def _():
        out[end:, :] = tail[...].astype(I32).astype(I16)


def own_kernel(where, w_own, w_got, own, got, out):
    for part, value in enumerate(weighted(w_own, w_got, own, got)):
        out[0, part] = value


def operator(where, bits, w_own, w_got, inverse, got, first, count, coded, after=()):
    terms, _, _, size, _ = inverse.shape
    smem = pl.BlockSpec(memory_space=pltpu.SMEM)
    if coded:
        out_shape = message(2 * count, size)
        out_spec = whole(out_shape.shape)
    else:
        out_shape = jax.ShapeDtypeStruct((count, 2, size, LANES), F32)
        out_spec = pl.BlockSpec((1, 2, size, LANES), lambda t, where: (t, 0, 0, 0))
    return pl.pallas_call(
        functools.partial(share_kernel, len(after)) if coded else own_kernel,
        out_shape=out_shape,
        grid_spec=pltpu.PrefetchScalarGridSpec(
            num_scalar_prefetch=1,
            grid=(count,),
            in_specs=[
                smem,
                smem,
                pl.BlockSpec(
                    (terms, 1, 2, size, LANES),
                    lambda t, where: (0, where[bits], 0, 0, t + first),
                ),
                pl.BlockSpec((terms, 2, size, LANES), lambda t, where: (0, 0, 0, t + first)),
            ]
            + [pl.BlockSpec(memory_space=pl.ANY)] * len(after),
            out_specs=out_spec,
            scratch_shapes=[pltpu.VMEM((TAIL, LANES), F32)] if coded else [],
        ),
        compiler_params=params(),
        cost_estimate=pl.CostEstimate(
            flops=32 * terms * size * LANES * count,
            bytes_accessed=16 * size * LANES * count,
            transcendentals=0,
        ),
        name="share" if coded else "operator",
    )(where, w_own, w_got, inverse, got, *after)


def product_kernel(count, tiles, after, *refs):
    parts, own, got = refs[:count], refs[count], refs[count + 1 : count + 1 + tiles]
    refs = refs[count + 1 + tiles + after :]
    near, sends = refs[0], refs[1:count]
    full, op, tails = refs[count:]
    rows, width = parts[0].shape
    size = width // 2
    t = pl.program_id(0)

    @pl.when(t == 0)
    def _():
        tails[...] = jnp.zeros_like(tails)
        for i, part in enumerate(parts):
            full[i * rows : (i + 1) * rows, :] = part[...]

    for i in range(tiles):

        @pl.when(t == i)
        def _():
            table = scales(got[i][2 * size :, :])
            real, imag = (
                own[0, part]
                + got[i][part * size : (part + 1) * size, :].astype(I32).astype(F32)
                * table[part : part + 1, :]
                for part in range(2)
            )
            for level, (r, j) in enumerate(zip(split(real), split(imag))):
                op[level, :size, :LANES] = r
                op[level, :size, LANES:] = j
                op[level, size:, :LANES] = -j
                op[level, size:, LANES:] = r

    x = full[...]
    acc = jnp.dot(x, op[0], preferred_element_type=F32)
    acc += jnp.dot(x, op[1], preferred_element_type=F32)
    near[0] = acc[:rows]
    for q in range(1, count):
        for part in range(2):
            strip = 2 * t + part
            block = acc[q * rows : (q + 1) * rows, part * LANES : (part + 1) * LANES]
            code, step = encode(block)
            sends[q - 1][pl.ds(pl.multiple_of(strip * rows, TAIL), rows), :] = code
            tails[q - 1] = put_row(tails[q - 1], strip, step)

    @pl.when(t == tiles - 1)
    def _():
        for q in range(1, count):
            sends[q - 1][2 * tiles * rows :, :] = tails[q - 1].astype(I32).astype(I16)


def product(parts, own, got, first, after):
    count, tiles = len(parts), len(got)
    rows, width = parts[0].shape
    size = width // 2
    send = message(2 * tiles, rows)
    return pl.pallas_call(
        functools.partial(product_kernel, count, tiles, len(after)),
        out_shape=[jax.ShapeDtypeStruct((tiles, rows, 2 * LANES), F32)] + [send] * (count - 1),
        grid=(tiles,),
        in_specs=[whole((rows, width))] * count
        + [
            pl.BlockSpec((1, 2, size, LANES), lambda t: (t + first, 0, 0, 0)),
        ]
        + [whole(x.shape) for x in got]
        + [pl.BlockSpec(memory_space=pl.ANY)] * len(after),
        out_specs=[pl.BlockSpec((1, rows, 2 * LANES), lambda t: (t, 0, 0))]
        + [whole(send.shape)] * (count - 1),
        scratch_shapes=[
            pltpu.VMEM((count * rows, width), BF16),
            pltpu.VMEM((2, width, 2 * LANES), BF16),
            pltpu.VMEM((count - 1, TAIL, LANES), F32),
        ],
        compiler_params=params(),
        cost_estimate=pl.CostEstimate(
            flops=8 * count * rows * width * tiles * LANES,
            bytes_accessed=12 * size * LANES * tiles + 2 * count * rows * width,
            transcendentals=0,
        ),
        name="product",
    )(*parts, own, *got, *after)


def add_up(near, got, write):
    base = 0
    for own, parts in zip(near, got):
        tiles, rows, _ = own.shape
        tables = [scales(part[2 * tiles * rows :, :]) for part in parts]
        for t in range(tiles):
            for part in range(2):
                strip = 2 * t + part
                total = own[t, :, part * LANES : (part + 1) * LANES]
                for ref, table in zip(parts, tables):
                    code = ref[strip * rows : (strip + 1) * rows, :]
                    total += code.astype(I32).astype(F32) * table[strip : strip + 1, :]
                write(base + t, part, total)
        base += tiles


def unpack(refs, chunks, count):
    near = refs[:chunks]
    got = [refs[chunks + i * count : chunks + (i + 1) * count] for i in range(chunks)]
    return near, got, refs[chunks * (1 + count) :]


def synthesis_kernel(bands, chunks, count, where, *refs):
    near, got, rest = unpack(refs, chunks, count)
    table, outs, values = rest[0], rest[1:-1], rest[-1]
    rows = near[0].shape[1]
    band = pl.program_id(0)

    @pl.when(band == 0)
    def _():
        def write(tile, part, total):
            for level, value in enumerate(split(total)):
                values[
                    level, part * rows : (part + 1) * rows, tile * LANES : (tile + 1) * LANES
                ] = value

        add_up(near, got, write)

    grid = jnp.dot(values[0], table[0], preferred_element_type=F32)
    grid += jnp.dot(values[1], table[0], preferred_element_type=F32)
    quarter = rows // 4
    for d in range(bands):

        @pl.when(band == d)
        def _():
            for side in range(4):
                out = outs[4 * d + side]
                if len(out.shape) == 3:
                    for part in range(2):
                        start = part * rows + side * quarter
                        out[part] = grid[start : start + quarter]
                    continue
                tail = jnp.zeros((TAIL, LANES), F32)
                for part in range(2):
                    start = part * rows + side * quarter
                    for k in range(grid.shape[1] // LANES):
                        strip = 2 * k + part
                        code, step = encode(
                            grid[start : start + quarter, k * LANES : (k + 1) * LANES]
                        )
                        out[strip * quarter : (strip + 1) * quarter, :] = code
                        tail = put_row(tail, strip, step)
                out[out.shape[0] - TAIL :, :] = tail.astype(I32).astype(I16)


def synthesis(where, near, got, legendre, bands):
    rows = near[0].shape[1]
    size, nlat = legendre.shape[1:]
    band = nlat // bands
    send = message(2 * band // LANES, rows // 4)
    outs = [jax.ShapeDtypeStruct((2, rows // 4, band), F32)] + [send] * (4 * bands - 1)
    operands = list(near) + [part for parts in got for part in parts]
    return pl.pallas_call(
        functools.partial(synthesis_kernel, bands, len(near), len(got[0])),
        out_shape=outs,
        grid_spec=pltpu.PrefetchScalarGridSpec(
            num_scalar_prefetch=1,
            grid=(bands,),
            in_specs=[whole(x.shape) for x in operands]
            + [pl.BlockSpec((1, size, band), lambda b, where: (where[0], 0, where[4] ^ b))],
            out_specs=[whole(out.shape) for out in outs],
            scratch_shapes=[pltpu.VMEM((2, 2 * rows, size), BF16)],
        ),
        compiler_params=params(),
        cost_estimate=pl.CostEstimate(
            flops=8 * rows * size * nlat,
            bytes_accessed=2 * size * nlat + 8 * rows * nlat,
            transcendentals=0,
        ),
        name="synthesis",
    )(where, *operands, legendre)


def total_kernel(chunks, count, *refs):
    near, got, (out,) = unpack(refs, chunks, count)

    def write(tile, part, total):
        out[part, :, tile * LANES : (tile + 1) * LANES] = total

    add_up(near, got, write)


def plain_synthesis(where, near, got, legendre, bands):
    rows = near[0].shape[1]
    size, nlat = legendre.shape[1:]
    total = pl.pallas_call(
        functools.partial(total_kernel, len(near), len(got[0])),
        out_shape=jax.ShapeDtypeStruct((2, rows, size), F32),
        compiler_params=params(),
        name="total",
    )(*near, *[part for parts in got for part in parts])
    table = lax.dynamic_index_in_dim(legendre, where[0], 0, keepdims=False)
    grid = sum(
        jnp.einsum("pcn,nl->pcl", v, table, preferred_element_type=F32) for v in split(total)
    )
    quarter, band = rows // 4, nlat // bands
    return [
        lax.dynamic_slice(grid, (0, side * quarter, (where[4] ^ d) * band), (2, quarter, band))
        for d in range(bands)
        for side in range(4)
    ]


def place_kernel(count, where, column, *refs):
    pieces, out = refs[:count], refs[count]
    _, _, rows, lanes = out.shape
    for i in range(count):

        @pl.when(pl.program_id(0) == i)
        def _():
            piece = pieces[i]
            if len(piece.shape) == 3:
                out[0] = piece[...]
                return
            strips = 2 * lanes // LANES
            table = scales(piece[strips * rows :, :])
            for strip in range(strips):
                code = piece[strip * rows : (strip + 1) * rows, :]
                at = strip // 2 * LANES
                out[0, strip % 2, :, at : at + LANES] = (
                    code.astype(I32).astype(F32) * table[strip : strip + 1, :]
                )


def place(where, column, slots, pieces):
    count = len(pieces)
    shape = pieces[0].shape
    return pl.pallas_call(
        functools.partial(place_kernel, count),
        out_shape=jax.ShapeDtypeStruct((count,) + shape, F32),
        grid_spec=pltpu.PrefetchScalarGridSpec(
            num_scalar_prefetch=2,
            grid=(count,),
            in_specs=[whole(piece.shape) for piece in pieces],
            out_specs=pl.BlockSpec(
                (1,) + shape,
                lambda i, where, column: (
                    column[(where[4] ^ (i // 4)) * slots + where[i % 4]],
                    0,
                    0,
                    0,
                ),
            ),
        ),
        compiler_params=params(),
        name="place",
    )(where, column, *pieces)


def pick_kernel(where, *refs):
    count = len(refs) // 2
    for i in range(count):
        refs[count + i][...] = refs[i][0]


def pick(where, state):
    shape = state.shape[1:]
    block = lambda i: pl.BlockSpec((1,) + shape, lambda _, where: (where[i], 0, 0))
    return pl.pallas_call(
        pick_kernel,
        out_shape=[jax.ShapeDtypeStruct(shape, state.dtype)] * 4,
        grid_spec=pltpu.PrefetchScalarGridSpec(
            num_scalar_prefetch=1,
            grid=(1,),
            in_specs=[block(i) for i in range(4)],
            out_specs=[whole(shape)] * 4,
        ),
        compiler_params=params(),
        name="pick",
    )(where, *[state] * 4)


def shards(mesh, spectral_state, inverse, term_weights, legendre, slot_column):
    terms, waves = mesh.shape["term"], mesh.shape["wave"]
    slots, cols, width = spectral_state.shape
    size = width // 2
    outer = terms // 4
    me, wave = lax.axis_index("term"), lax.axis_index("wave")
    place_of = me % 4

    def swap(x, term_bits, wave_bits=0):
        pairs = [
            (t * waves + w, (t ^ term_bits) * waves + (w ^ wave_bits))
            for t in range(terms)
            for w in range(waves)
        ]
        return lax.ppermute(x, ("term", "wave"), pairs)

    tiles = size // LANES
    cut = (tiles + 1) // 2
    chunks = [(0, cut), (cut, tiles - cut)] if tiles > 1 else [(0, tiles)]

    assert slots == 4
    where = jnp.stack([place_of ^ bits for bits in range(4)] + [wave]).astype(I32)
    states = pick(where, spectral_state)
    block = jnp.concatenate(
        [states[0]] + [swap(states[bits], bits) for bits in range(1, 4)], axis=0
    )
    parts = [block] + [swap(block, q * 4) for q in range(1, outer)]

    w_got = swap(term_weights, 1)
    far, own = (
        swap(lax.dynamic_index_in_dim(inverse, place_of ^ bits, 1, keepdims=False), 1)
        for bits in (3, 1)
    )
    mine = operator(where, 0, term_weights, w_got, inverse, own, 0, tiles, False)
    shares = []
    for t in range(tiles):
        after = (block,) if t < tiles - 1 else (*parts[1:], mine)
        share = operator(where, 2, term_weights, w_got, inverse, far, t, 1, True, after)
        shares.append(swap(share, 2))
    near, got = [], []
    for first, count in chunks:
        after = [near[-1], got[-1][0]] if near else []
        made = product(parts, mine, shares[first : first + count], first, after)
        near.append(made[0])
        got.append([swap(made[q], q * 4) for q in range(1, outer)])
    make = synthesis if legendre.shape[2] // waves % LANES == 0 else plain_synthesis
    grid = make(where, near, got, legendre, waves)
    pieces = [
        swap(grid[4 * d + bits], bits, d) if d or bits else grid[0]
        for d in range(waves)
        for bits in range(4)
    ]
    return place(where, slot_column, slots, pieces)


def solution(mesh):
    return jax.shard_map(
        functools.partial(shards, mesh),
        mesh=mesh,
        in_specs=(
            P("wave", "term", None),
            P("term", "wave", None, None, None),
            P("term", None),
            P("wave", None, None),
            P(),
        ),
        out_specs=P(None, None, "term", "wave"),
        check_vma=False,
    )
```

```python
import functools

import jax
import jax.numpy as jnp
from jax import lax
from jax.experimental import pallas as pl
from jax.experimental.pallas import tpu as pltpu
from jax.sharding import PartitionSpec as P

F32, BF16, I16, I32 = jnp.float32, jnp.bfloat16, jnp.int16, jnp.int32
LANES = 128
TAIL = 16
STEPS = 64.0
TOP = 32000.0
TINY = 1e-30


def params(mib=48):
    return pltpu.CompilerParams(vmem_limit_bytes=mib * 2**20)


def split(x):
    hi = x.astype(BF16)
    return hi, (x - hi.astype(F32)).astype(BF16)


def encode(x):
    top = jnp.maximum(jnp.max(jnp.abs(x), axis=0, keepdims=True), TINY)
    step = jnp.ceil(jnp.log2(top * (1.0 / TOP)) * STEPS)
    code = jnp.round(x * jnp.exp2(step * (-1.0 / STEPS)))
    return code.astype(I32).astype(I16), step


def put_row(tail, row, values):
    at = lax.broadcasted_iota(I32, tail.shape, 0)
    return jnp.where(at == row, values, tail)


def scales(tail):
    return jnp.exp2(tail.astype(I32).astype(F32) * (1.0 / STEPS))


def message(strips, rows):
    return jax.ShapeDtypeStruct((strips * rows + TAIL, LANES), I16)


def whole(shape):
    return pl.BlockSpec(shape, lambda *_: (0,) * len(shape))


def weighted(w_own, w_got, own, got):
    real = imag = 0.0
    for k in range(own.shape[0]):
        for w, block in ((w_own, own[k, 0]), (w_got, got[k])):
            r, j = block[0].astype(F32), block[1].astype(F32)
            real += w[k, 0] * r - w[k, 1] * j
            imag += w[k, 0] * j + w[k, 1] * r
    return real, imag


def share_kernel(after, where, w_own, w_got, own, got, *refs):
    out, tail = refs[after:]
    t = pl.program_id(0)
    size = own.shape[3]
    end = out.shape[0] - TAIL

    @pl.when(t == 0)
    def _():
        tail[...] = jnp.zeros_like(tail)

    for part, value in enumerate(weighted(w_own, w_got, own, got)):
        strip = 2 * t + part
        code, step = encode(value)
        out[pl.ds(pl.multiple_of(strip * size, TAIL), size), :] = code
        tail[...] = put_row(tail[...], strip, step)

    @pl.when(t == pl.num_programs(0) - 1)
    def _():
        out[end:, :] = tail[...].astype(I32).astype(I16)


def own_kernel(where, w_own, w_got, own, got, out):
    for part, value in enumerate(weighted(w_own, w_got, own, got)):
        out[0, part] = value


def operator(where, bits, w_own, w_got, inverse, got, first, count, coded, after=()):
    terms, _, _, size, _ = inverse.shape
    smem = pl.BlockSpec(memory_space=pltpu.SMEM)
    if coded:
        out_shape = message(2 * count, size)
        out_spec = whole(out_shape.shape)
    else:
        out_shape = jax.ShapeDtypeStruct((count, 2, size, LANES), F32)
        out_spec = pl.BlockSpec((1, 2, size, LANES), lambda t, where: (t, 0, 0, 0))
    return pl.pallas_call(
        functools.partial(share_kernel, len(after)) if coded else own_kernel,
        out_shape=out_shape,
        grid_spec=pltpu.PrefetchScalarGridSpec(
            num_scalar_prefetch=1,
            grid=(count,),
            in_specs=[
                smem,
                smem,
                pl.BlockSpec(
                    (terms, 1, 2, size, LANES),
                    lambda t, where: (0, where[bits], 0, 0, t + first),
                ),
                pl.BlockSpec((terms, 2, size, LANES), lambda t, where: (0, 0, 0, t + first)),
            ]
            + [pl.BlockSpec(memory_space=pl.ANY)] * len(after),
            out_specs=out_spec,
            scratch_shapes=[pltpu.VMEM((TAIL, LANES), F32)] if coded else [],
        ),
        compiler_params=params(),
        cost_estimate=pl.CostEstimate(
            flops=32 * terms * size * LANES * count,
            bytes_accessed=16 * size * LANES * count,
            transcendentals=0,
        ),
        name="share" if coded else "operator",
    )(where, w_own, w_got, inverse, got, *after)


def product_kernel(count, tiles, after, *refs):
    parts, own, got = refs[:count], refs[count], refs[count + 1]
    refs = refs[count + 2 + after :]
    near, sends = refs[0], refs[1:count]
    full, op, tails = refs[count:]
    rows, width = parts[0].shape
    size = width // 2
    t = pl.program_id(0)

    @pl.when(t == 0)
    def _():
        tails[...] = jnp.zeros_like(tails)
        for i, part in enumerate(parts):
            full[i * rows : (i + 1) * rows, :] = part[...]

    for i in range(tiles):

        @pl.when(t == i)
        def _():
            table = scales(got[2 * tiles * size :, :])
            real, imag = (
                own[0, strip % 2]
                + got[strip * size : (strip + 1) * size, :].astype(I32).astype(F32)
                * table[strip : strip + 1, :]
                for strip in (2 * i, 2 * i + 1)
            )
            for level, (r, j) in enumerate(zip(split(real), split(imag))):
                op[level, :size, :LANES] = r
                op[level, :size, LANES:] = j
                op[level, size:, :LANES] = -j
                op[level, size:, LANES:] = r

    x = full[...]
    acc = jnp.dot(x, op[0], preferred_element_type=F32)
    acc += jnp.dot(x, op[1], preferred_element_type=F32)
    near[0] = acc[:rows]
    for q in range(1, count):
        for part in range(2):
            strip = 2 * t + part
            block = acc[q * rows : (q + 1) * rows, part * LANES : (part + 1) * LANES]
            code, step = encode(block)
            sends[q - 1][pl.ds(pl.multiple_of(strip * rows, TAIL), rows), :] = code
            tails[q - 1] = put_row(tails[q - 1], strip, step)

    @pl.when(t == tiles - 1)
    def _():
        for q in range(1, count):
            sends[q - 1][2 * tiles * rows :, :] = tails[q - 1].astype(I32).astype(I16)


def product(parts, own, got, first, tiles, after):
    count = len(parts)
    rows, width = parts[0].shape
    size = width // 2
    send = message(2 * tiles, rows)
    return pl.pallas_call(
        functools.partial(product_kernel, count, tiles, len(after)),
        out_shape=[jax.ShapeDtypeStruct((tiles, rows, 2 * LANES), F32)] + [send] * (count - 1),
        grid=(tiles,),
        in_specs=[whole((rows, width))] * count
        + [
            pl.BlockSpec((1, 2, size, LANES), lambda t: (t + first, 0, 0, 0)),
        ]
        + [whole(got.shape)]
        + [pl.BlockSpec(memory_space=pl.ANY)] * len(after),
        out_specs=[pl.BlockSpec((1, rows, 2 * LANES), lambda t: (t, 0, 0))]
        + [whole(send.shape)] * (count - 1),
        scratch_shapes=[
            pltpu.VMEM((count * rows, width), BF16),
            pltpu.VMEM((2, width, 2 * LANES), BF16),
            pltpu.VMEM((count - 1, TAIL, LANES), F32),
        ],
        compiler_params=params(),
        cost_estimate=pl.CostEstimate(
            flops=8 * count * rows * width * tiles * LANES,
            bytes_accessed=12 * size * LANES * tiles + 2 * count * rows * width,
            transcendentals=0,
        ),
        name="product",
    )(*parts, own, got, *after)


def add_up(near, got, write):
    base = 0
    for own, parts in zip(near, got):
        tiles, rows, _ = own.shape
        tables = [scales(part[2 * tiles * rows :, :]) for part in parts]
        for t in range(tiles):
            for part in range(2):
                strip = 2 * t + part
                total = own[t, :, part * LANES : (part + 1) * LANES]
                for ref, table in zip(parts, tables):
                    code = ref[strip * rows : (strip + 1) * rows, :]
                    total += code.astype(I32).astype(F32) * table[strip : strip + 1, :]
                write(base + t, part, total)
        base += tiles


def unpack(refs, chunks, count):
    near = refs[:chunks]
    got = [refs[chunks + i * count : chunks + (i + 1) * count] for i in range(chunks)]
    return near, got, refs[chunks * (1 + count) :]


def synthesis_kernel(bands, chunks, count, where, *refs):
    near, got, rest = unpack(refs, chunks, count)
    table, outs, values = rest[0], rest[1:-1], rest[-1]
    rows = near[0].shape[1]
    band = pl.program_id(0)

    @pl.when(band == 0)
    def _():
        def write(tile, part, total):
            for level, value in enumerate(split(total)):
                values[
                    level, part * rows : (part + 1) * rows, tile * LANES : (tile + 1) * LANES
                ] = value

        add_up(near, got, write)

    grid = jnp.dot(values[0], table[0], preferred_element_type=F32)
    grid += jnp.dot(values[1], table[0], preferred_element_type=F32)
    quarter = rows // 4
    for d in range(bands):

        @pl.when(band == d)
        def _():
            for side in range(4):
                out = outs[4 * d + side]
                if len(out.shape) == 3:
                    for part in range(2):
                        start = part * rows + side * quarter
                        out[part] = grid[start : start + quarter]
                    continue
                tail = jnp.zeros((TAIL, LANES), F32)
                for part in range(2):
                    start = part * rows + side * quarter
                    for k in range(grid.shape[1] // LANES):
                        strip = 2 * k + part
                        code, step = encode(
                            grid[start : start + quarter, k * LANES : (k + 1) * LANES]
                        )
                        out[strip * quarter : (strip + 1) * quarter, :] = code
                        tail = put_row(tail, strip, step)
                out[out.shape[0] - TAIL :, :] = tail.astype(I32).astype(I16)


def synthesis(where, near, got, legendre, bands):
    rows = near[0].shape[1]
    size, nlat = legendre.shape[1:]
    band = nlat // bands
    send = message(2 * band // LANES, rows // 4)
    outs = [jax.ShapeDtypeStruct((2, rows // 4, band), F32)] + [send] * (4 * bands - 1)
    operands = list(near) + [part for parts in got for part in parts]
    return pl.pallas_call(
        functools.partial(synthesis_kernel, bands, len(near), len(got[0])),
        out_shape=outs,
        grid_spec=pltpu.PrefetchScalarGridSpec(
            num_scalar_prefetch=1,
            grid=(bands,),
            in_specs=[whole(x.shape) for x in operands]
            + [pl.BlockSpec((1, size, band), lambda b, where: (where[0], 0, where[4] ^ b))],
            out_specs=[whole(out.shape) for out in outs],
            scratch_shapes=[pltpu.VMEM((2, 2 * rows, size), BF16)],
        ),
        compiler_params=params(),
        cost_estimate=pl.CostEstimate(
            flops=8 * rows * size * nlat,
            bytes_accessed=2 * size * nlat + 8 * rows * nlat,
            transcendentals=0,
        ),
        name="synthesis",
    )(where, *operands, legendre)


def total_kernel(chunks, count, *refs):
    near, got, (out,) = unpack(refs, chunks, count)

    def write(tile, part, total):
        out[part, :, tile * LANES : (tile + 1) * LANES] = total

    add_up(near, got, write)


def plain_synthesis(where, near, got, legendre, bands):
    rows = near[0].shape[1]
    size, nlat = legendre.shape[1:]
    total = pl.pallas_call(
        functools.partial(total_kernel, len(near), len(got[0])),
        out_shape=jax.ShapeDtypeStruct((2, rows, size), F32),
        compiler_params=params(),
        name="total",
    )(*near, *[part for parts in got for part in parts])
    table = lax.dynamic_index_in_dim(legendre, where[0], 0, keepdims=False)
    grid = sum(
        jnp.einsum("pcn,nl->pcl", v, table, preferred_element_type=F32) for v in split(total)
    )
    quarter, band = rows // 4, nlat // bands
    return [
        lax.dynamic_slice(grid, (0, side * quarter, (where[4] ^ d) * band), (2, quarter, band))
        for d in range(bands)
        for side in range(4)
    ]


def place_kernel(count, where, column, *refs):
    pieces, out = refs[:count], refs[count]
    _, _, rows, lanes = out.shape
    for i in range(count):

        @pl.when(pl.program_id(0) == i)
        def _():
            piece = pieces[i]
            if len(piece.shape) == 3:
                out[0] = piece[...]
                return
            strips = 2 * lanes // LANES
            table = scales(piece[strips * rows :, :])
            for strip in range(strips):
                code = piece[strip * rows : (strip + 1) * rows, :]
                at = strip // 2 * LANES
                out[0, strip % 2, :, at : at + LANES] = (
                    code.astype(I32).astype(F32) * table[strip : strip + 1, :]
                )


def place(where, column, slots, pieces):
    count = len(pieces)
    shape = pieces[0].shape
    return pl.pallas_call(
        functools.partial(place_kernel, count),
        out_shape=jax.ShapeDtypeStruct((count,) + shape, F32),
        grid_spec=pltpu.PrefetchScalarGridSpec(
            num_scalar_prefetch=2,
            grid=(count,),
            in_specs=[whole(piece.shape) for piece in pieces],
            out_specs=pl.BlockSpec(
                (1,) + shape,
                lambda i, where, column: (
                    column[(where[4] ^ (i // 4)) * slots + where[i % 4]],
                    0,
                    0,
                    0,
                ),
            ),
        ),
        compiler_params=params(),
        name="place",
    )(where, column, *pieces)


def pick_kernel(where, *refs):
    count = len(refs) // 2
    for i in range(count):
        refs[count + i][...] = refs[i][0]


def pick(where, state):
    shape = state.shape[1:]
    block = lambda i: pl.BlockSpec((1,) + shape, lambda _, where: (where[i], 0, 0))
    return pl.pallas_call(
        pick_kernel,
        out_shape=[jax.ShapeDtypeStruct(shape, state.dtype)] * 4,
        grid_spec=pltpu.PrefetchScalarGridSpec(
            num_scalar_prefetch=1,
            grid=(1,),
            in_specs=[block(i) for i in range(4)],
            out_specs=[whole(shape)] * 4,
        ),
        compiler_params=params(),
        name="pick",
    )(where, *[state] * 4)


def shards(mesh, spectral_state, inverse, term_weights, legendre, slot_column):
    terms, waves = mesh.shape["term"], mesh.shape["wave"]
    slots, cols, width = spectral_state.shape
    size = width // 2
    outer = terms // 4
    me, wave = lax.axis_index("term"), lax.axis_index("wave")
    place_of = me % 4

    def swap(x, term_bits, wave_bits=0):
        pairs = [
            (t * waves + w, (t ^ term_bits) * waves + (w ^ wave_bits))
            for t in range(terms)
            for w in range(waves)
        ]
        return lax.ppermute(x, ("term", "wave"), pairs)

    tiles = size // LANES
    cut = (tiles + 1) // 2
    chunks = [(0, cut), (cut, tiles - cut)] if tiles > 1 else [(0, tiles)]

    assert slots == 4
    where = jnp.stack([place_of ^ bits for bits in range(4)] + [wave]).astype(I32)
    states = pick(where, spectral_state)
    block = jnp.concatenate(
        [states[0]] + [swap(states[bits], bits) for bits in range(1, 4)], axis=0
    )
    parts = [block] + [swap(block, q * 4) for q in range(1, outer)]

    w_got = swap(term_weights, 1)
    far, own = (
        swap(lax.dynamic_index_in_dim(inverse, place_of ^ bits, 1, keepdims=False), 1)
        for bits in (3, 1)
    )
    mine = operator(where, 0, term_weights, w_got, inverse, own, 0, tiles, False)
    behind = [(block,), (mine,)]
    shares = [
        swap(operator(where, 2, term_weights, w_got, inverse, far, *chunk, True, after), 2)
        for chunk, after in zip(chunks, behind)
    ]
    near, got = [], []
    for chunk, share in zip(chunks, shares):
        after = [near[-1], got[-1][0]] if near else []
        made = product(parts, mine, share, *chunk, after)
        near.append(made[0])
        got.append([swap(made[q], q * 4) for q in range(1, outer)])
    make = synthesis if legendre.shape[2] // waves % LANES == 0 else plain_synthesis
    grid = make(where, near, got, legendre, waves)
    pieces = [
        swap(grid[4 * d + bits], bits, d) if d or bits else grid[0]
        for d in range(waves)
        for bits in range(4)
    ]
    return place(where, slot_column, slots, pieces)


def solution(mesh):
    return jax.shard_map(
        functools.partial(shards, mesh),
        mesh=mesh,
        in_specs=(
            P("wave", "term", None),
            P("term", "wave", None, None, None),
            P("term", None),
            P("wave", None, None),
            P(),
        ),
        out_specs=P(None, None, "term", "wave"),
        check_vma=False,
    )
```

```python
import functools

import jax
import jax.numpy as jnp
from jax import lax
from jax.experimental import pallas as pl
from jax.experimental.pallas import tpu as pltpu
from jax.sharding import PartitionSpec as P

F32, BF16, I16, I32 = jnp.float32, jnp.bfloat16, jnp.int16, jnp.int32
LANES = 128
TAIL = 16
STEPS = 64.0
TOP = 32000.0
TINY = 1e-30


def params(mib=48):
    return pltpu.CompilerParams(vmem_limit_bytes=mib * 2**20)


def split(x):
    hi = x.astype(BF16)
    return hi, (x - hi.astype(F32)).astype(BF16)


def encode(x):
    top = jnp.maximum(jnp.max(jnp.abs(x), axis=0, keepdims=True), TINY)
    step = jnp.ceil(jnp.log2(top * (1.0 / TOP)) * STEPS)
    code = jnp.round(x * jnp.exp2(step * (-1.0 / STEPS)))
    return code.astype(I32).astype(I16), step


def put_row(tail, row, values):
    at = lax.broadcasted_iota(I32, tail.shape, 0)
    return jnp.where(at == row, values, tail)


def scales(tail):
    return jnp.exp2(tail.astype(I32).astype(F32) * (1.0 / STEPS))


def message(strips, rows):
    return jax.ShapeDtypeStruct((strips * rows + TAIL, LANES), I16)


def whole(shape):
    return pl.BlockSpec(shape, lambda *_: (0,) * len(shape))


def weighted(w_own, w_got, own, got):
    real = imag = 0.0
    for k in range(own.shape[0]):
        for w, block in ((w_own, own[k, 0]), (w_got, got[k])):
            r, j = block[0].astype(F32), block[1].astype(F32)
            real += w[k, 0] * r - w[k, 1] * j
            imag += w[k, 0] * j + w[k, 1] * r
    return real, imag


def share_kernel(after, where, w_own, w_got, own, got, *refs):
    out, tail = refs[after:]
    t = pl.program_id(0)
    size = own.shape[3]
    end = out.shape[0] - TAIL

    @pl.when(t == 0)
    def _():
        tail[...] = jnp.zeros_like(tail)

    for part, value in enumerate(weighted(w_own, w_got, own, got)):
        strip = 2 * t + part
        code, step = encode(value)
        out[pl.ds(pl.multiple_of(strip * size, TAIL), size), :] = code
        tail[...] = put_row(tail[...], strip, step)

    @pl.when(t == pl.num_programs(0) - 1)
    def _():
        out[end:, :] = tail[...].astype(I32).astype(I16)


def own_kernel(where, w_own, w_got, own, got, out):
    for part, value in enumerate(weighted(w_own, w_got, own, got)):
        out[0, part] = value


def operator(where, bits, w_own, w_got, inverse, got, first, count, coded, after=()):
    terms, _, _, size, _ = inverse.shape
    smem = pl.BlockSpec(memory_space=pltpu.SMEM)
    if coded:
        out_shape = message(2 * count, size)
        out_spec = whole(out_shape.shape)
    else:
        out_shape = jax.ShapeDtypeStruct((count, 2, size, LANES), F32)
        out_spec = pl.BlockSpec((1, 2, size, LANES), lambda t, where: (t, 0, 0, 0))
    return pl.pallas_call(
        functools.partial(share_kernel, len(after)) if coded else own_kernel,
        out_shape=out_shape,
        grid_spec=pltpu.PrefetchScalarGridSpec(
            num_scalar_prefetch=1,
            grid=(count,),
            in_specs=[
                smem,
                smem,
                pl.BlockSpec(
                    (terms, 1, 2, size, LANES),
                    lambda t, where: (0, where[bits], 0, 0, t + first),
                ),
                pl.BlockSpec((terms, 2, size, LANES), lambda t, where: (0, 0, 0, t + first)),
            ]
            + [pl.BlockSpec(memory_space=pl.ANY)] * len(after),
            out_specs=out_spec,
            scratch_shapes=[pltpu.VMEM((TAIL, LANES), F32)] if coded else [],
        ),
        compiler_params=params(),
        cost_estimate=pl.CostEstimate(
            flops=32 * terms * size * LANES * count,
            bytes_accessed=16 * size * LANES * count,
            transcendentals=0,
        ),
        name="share" if coded else "operator",
    )(where, w_own, w_got, inverse, got, *after)


def product_kernel(pieces, count, held, after, *refs):
    tiles = sum(held)
    parts, own, got = refs[:pieces], refs[pieces], refs[pieces + 1 : pieces + 1 + len(held)]
    refs = refs[pieces + 1 + len(held) + after :]
    near, sends = refs[0], refs[1:count]
    full, op, tails = refs[count:]
    rows, width = parts[0].shape
    size = width // 2
    t = pl.program_id(0)

    @pl.when(t == 0)
    def _():
        tails[...] = jnp.zeros_like(tails)
        start = 0
        for part in parts:
            full[start : start + part.shape[0], :] = part[...]
            start += part.shape[0]

    sources = [(ref, i) for ref, n in zip(got, held) for i in range(n)]
    for at, (ref, i) in enumerate(sources):

        @pl.when(t == at)
        def _():
            table = scales(ref[ref.shape[0] - TAIL :, :])
            real, imag = (
                own[0, strip % 2]
                + ref[strip * size : (strip + 1) * size, :].astype(I32).astype(F32)
                * table[strip : strip + 1, :]
                for strip in (2 * i, 2 * i + 1)
            )
            for level, (r, j) in enumerate(zip(split(real), split(imag))):
                op[level, :size, :LANES] = r
                op[level, :size, LANES:] = j
                op[level, size:, :LANES] = -j
                op[level, size:, LANES:] = r

    x = full[...]
    acc = jnp.dot(x, op[0], preferred_element_type=F32)
    acc += jnp.dot(x, op[1], preferred_element_type=F32)
    near[0] = acc[:rows]
    for q in range(1, count):
        for part in range(2):
            strip = 2 * t + part
            block = acc[q * rows : (q + 1) * rows, part * LANES : (part + 1) * LANES]
            code, step = encode(block)
            sends[q - 1][pl.ds(pl.multiple_of(strip * rows, TAIL), rows), :] = code
            tails[q - 1] = put_row(tails[q - 1], strip, step)

    @pl.when(t == tiles - 1)
    def _():
        for q in range(1, count):
            sends[q - 1][2 * tiles * rows :, :] = tails[q - 1].astype(I32).astype(I16)


def product(parts, own, got, first, held, after):
    tiles = sum(held)
    rows, width = parts[0].shape
    count = sum(part.shape[0] for part in parts) // rows
    size = width // 2
    send = message(2 * tiles, rows)
    return pl.pallas_call(
        functools.partial(product_kernel, len(parts), count, held, len(after)),
        out_shape=[jax.ShapeDtypeStruct((tiles, rows, 2 * LANES), F32)] + [send] * (count - 1),
        grid=(tiles,),
        in_specs=[whole(part.shape) for part in parts]
        + [
            pl.BlockSpec((1, 2, size, LANES), lambda t: (t + first, 0, 0, 0)),
        ]
        + [whole(x.shape) for x in got]
        + [pl.BlockSpec(memory_space=pl.ANY)] * len(after),
        out_specs=[pl.BlockSpec((1, rows, 2 * LANES), lambda t: (t, 0, 0))]
        + [whole(send.shape)] * (count - 1),
        scratch_shapes=[
            pltpu.VMEM((count * rows, width), BF16),
            pltpu.VMEM((2, width, 2 * LANES), BF16),
            pltpu.VMEM((count - 1, TAIL, LANES), F32),
        ],
        compiler_params=params(),
        cost_estimate=pl.CostEstimate(
            flops=8 * count * rows * width * tiles * LANES,
            bytes_accessed=12 * size * LANES * tiles + 2 * count * rows * width,
            transcendentals=0,
        ),
        name="product",
    )(*parts, own, *got, *after)


def add_up(near, got, write):
    base = 0
    for own, parts in zip(near, got):
        tiles, rows, _ = own.shape
        tables = [scales(part[2 * tiles * rows :, :]) for part in parts]
        for t in range(tiles):
            for part in range(2):
                strip = 2 * t + part
                total = own[t, :, part * LANES : (part + 1) * LANES]
                for ref, table in zip(parts, tables):
                    code = ref[strip * rows : (strip + 1) * rows, :]
                    total += code.astype(I32).astype(F32) * table[strip : strip + 1, :]
                write(base + t, part, total)
        base += tiles


def unpack(refs, chunks, count):
    near = refs[:chunks]
    got = [refs[chunks + i * count : chunks + (i + 1) * count] for i in range(chunks)]
    return near, got, refs[chunks * (1 + count) :]


def synthesis_kernel(bands, chunks, count, where, *refs):
    near, got, rest = unpack(refs, chunks, count)
    table, outs, values = rest[0], rest[1:-1], rest[-1]
    rows = near[0].shape[1]
    band = pl.program_id(0)

    @pl.when(band == 0)
    def _():
        def write(tile, part, total):
            for level, value in enumerate(split(total)):
                values[
                    level, part * rows : (part + 1) * rows, tile * LANES : (tile + 1) * LANES
                ] = value

        add_up(near, got, write)

    grid = jnp.dot(values[0], table[0], preferred_element_type=F32)
    grid += jnp.dot(values[1], table[0], preferred_element_type=F32)
    quarter = rows // 4
    for d in range(bands):

        @pl.when(band == d)
        def _():
            for side in range(4):
                out = outs[4 * d + side]
                if len(out.shape) == 3:
                    for part in range(2):
                        start = part * rows + side * quarter
                        out[part] = grid[start : start + quarter]
                    continue
                tail = jnp.zeros((TAIL, LANES), F32)
                for part in range(2):
                    start = part * rows + side * quarter
                    for k in range(grid.shape[1] // LANES):
                        strip = 2 * k + part
                        code, step = encode(
                            grid[start : start + quarter, k * LANES : (k + 1) * LANES]
                        )
                        out[strip * quarter : (strip + 1) * quarter, :] = code
                        tail = put_row(tail, strip, step)
                out[out.shape[0] - TAIL :, :] = tail.astype(I32).astype(I16)


def synthesis(where, near, got, legendre, bands):
    rows = near[0].shape[1]
    size, nlat = legendre.shape[1:]
    band = nlat // bands
    send = message(2 * band // LANES, rows // 4)
    outs = [jax.ShapeDtypeStruct((2, rows // 4, band), F32)] + [send] * (4 * bands - 1)
    operands = list(near) + [part for parts in got for part in parts]
    return pl.pallas_call(
        functools.partial(synthesis_kernel, bands, len(near), len(got[0])),
        out_shape=outs,
        grid_spec=pltpu.PrefetchScalarGridSpec(
            num_scalar_prefetch=1,
            grid=(bands,),
            in_specs=[whole(x.shape) for x in operands]
            + [pl.BlockSpec((1, size, band), lambda b, where: (where[0], 0, where[4] ^ b))],
            out_specs=[whole(out.shape) for out in outs],
            scratch_shapes=[pltpu.VMEM((2, 2 * rows, size), BF16)],
        ),
        compiler_params=params(),
        cost_estimate=pl.CostEstimate(
            flops=8 * rows * size * nlat,
            bytes_accessed=2 * size * nlat + 8 * rows * nlat,
            transcendentals=0,
        ),
        name="synthesis",
    )(where, *operands, legendre)


def total_kernel(chunks, count, *refs):
    near, got, (out,) = unpack(refs, chunks, count)

    def write(tile, part, total):
        out[part, :, tile * LANES : (tile + 1) * LANES] = total

    add_up(near, got, write)


def plain_synthesis(where, near, got, legendre, bands):
    rows = near[0].shape[1]
    size, nlat = legendre.shape[1:]
    total = pl.pallas_call(
        functools.partial(total_kernel, len(near), len(got[0])),
        out_shape=jax.ShapeDtypeStruct((2, rows, size), F32),
        compiler_params=params(),
        name="total",
    )(*near, *[part for parts in got for part in parts])
    table = lax.dynamic_index_in_dim(legendre, where[0], 0, keepdims=False)
    grid = sum(
        jnp.einsum("pcn,nl->pcl", v, table, preferred_element_type=F32) for v in split(total)
    )
    quarter, band = rows // 4, nlat // bands
    return [
        lax.dynamic_slice(grid, (0, side * quarter, (where[4] ^ d) * band), (2, quarter, band))
        for d in range(bands)
        for side in range(4)
    ]


def place_kernel(count, where, column, *refs):
    pieces, out = refs[:count], refs[count]
    _, _, rows, lanes = out.shape
    for i in range(count):

        @pl.when(pl.program_id(0) == i)
        def _():
            piece = pieces[i]
            if len(piece.shape) == 3:
                out[0] = piece[...]
                return
            strips = 2 * lanes // LANES
            table = scales(piece[strips * rows :, :])
            for strip in range(strips):
                code = piece[strip * rows : (strip + 1) * rows, :]
                at = strip // 2 * LANES
                out[0, strip % 2, :, at : at + LANES] = (
                    code.astype(I32).astype(F32) * table[strip : strip + 1, :]
                )


def place(where, column, slots, pieces):
    count = len(pieces)
    shape = pieces[0].shape
    return pl.pallas_call(
        functools.partial(place_kernel, count),
        out_shape=jax.ShapeDtypeStruct((count,) + shape, F32),
        grid_spec=pltpu.PrefetchScalarGridSpec(
            num_scalar_prefetch=2,
            grid=(count,),
            in_specs=[whole(piece.shape) for piece in pieces],
            out_specs=pl.BlockSpec(
                (1,) + shape,
                lambda i, where, column: (
                    column[(where[4] ^ (i // 4)) * slots + where[i % 4]],
                    0,
                    0,
                    0,
                ),
            ),
        ),
        compiler_params=params(),
        name="place",
    )(where, column, *pieces)


def pick_kernel(where, *refs):
    count = len(refs) // 2
    for i in range(count):
        refs[count + i][...] = refs[i][0]


def pick(where, state):
    shape = state.shape[1:]
    block = lambda i: pl.BlockSpec((1,) + shape, lambda _, where: (where[i], 0, 0))
    return pl.pallas_call(
        pick_kernel,
        out_shape=[jax.ShapeDtypeStruct(shape, state.dtype)] * 4,
        grid_spec=pltpu.PrefetchScalarGridSpec(
            num_scalar_prefetch=1,
            grid=(1,),
            in_specs=[block(i) for i in range(4)],
            out_specs=[whole(shape)] * 4,
        ),
        compiler_params=params(),
        name="pick",
    )(where, *[state] * 4)


def shards(mesh, spectral_state, inverse, term_weights, legendre, slot_column):
    terms, waves = mesh.shape["term"], mesh.shape["wave"]
    slots, cols, width = spectral_state.shape
    size = width // 2
    outer = terms // 4
    me, wave = lax.axis_index("term"), lax.axis_index("wave")
    place_of = me % 4

    def swap(x, term_bits, wave_bits=0):
        pairs = [
            (t * waves + w, (t ^ term_bits) * waves + (w ^ wave_bits))
            for t in range(terms)
            for w in range(waves)
        ]
        return lax.ppermute(x, ("term", "wave"), pairs)

    tiles = size // LANES
    assert slots == 4
    where = jnp.stack([place_of ^ bits for bits in range(4)] + [wave]).astype(I32)
    states = pick(where, spectral_state)
    received = [swap(states[bits], bits) for bits in range(1, 4)]
    turned, received[0] = lax.optimization_barrier((place_of, received[0]))
    block = jnp.concatenate([states[0]] + received, axis=0)
    steps = [q for q in range(1, outer) if q != 2] + [2]
    parts = [block] + [swap(block, q * 4) for q in steps[:-1]]
    half = block.shape[0] // 2
    parts += [swap(parts[1][:half], 3 * 4), swap(parts[2][half:], 1 * 4)]

    w_got = swap(term_weights, 1)
    far, own = (
        swap(lax.dynamic_index_in_dim(inverse, turned ^ bits, 1, keepdims=False), 1)
        for bits in (3, 1)
    )
    mine = operator(where, 0, term_weights, w_got, inverse, own, 0, tiles, False)
    groups = ((2, 1), (2,))
    shares, near, got = [], [], []
    first = 0
    for group in groups:
        start, messages = first, []
        for n in group:
            after = (block,) if not shares else (shares[-1], mine)
            shares.append(
                operator(where, 2, term_weights, w_got, inverse, far, first, n, True, after)
            )
            messages.append(swap(shares[-1], 2))
            first += n
        after = [near[-1], got[-1][0]] if near else []
        made = product(parts, mine, messages, start, group, after)
        near.append(made[0])
        got.append([swap(send, q * 4) for send, q in zip(made[1:], steps)])
    make = synthesis if legendre.shape[2] // waves % LANES == 0 else plain_synthesis
    grid = make(where, near, got, legendre, waves)
    pieces = [
        swap(grid[4 * d + bits], bits, d) if d or bits else grid[0]
        for d in range(waves)
        for bits in range(4)
    ]
    return place(where, slot_column, slots, pieces)


def solution(mesh):
    return jax.shard_map(
        functools.partial(shards, mesh),
        mesh=mesh,
        in_specs=(
            P("wave", "term", None),
            P("term", "wave", None, None, None),
            P("term", None),
            P("wave", None, None),
            P(),
        ),
        out_specs=P(None, None, "term", "wave"),
        check_vma=False,
    )
```

```python
import functools

import jax
import jax.numpy as jnp
from jax import lax
from jax.experimental import pallas as pl
from jax.experimental.pallas import tpu as pltpu
from jax.sharding import PartitionSpec as P

F32, BF16, I16, I32 = jnp.float32, jnp.bfloat16, jnp.int16, jnp.int32
LANES = 128
TAIL = 16
STEPS = 64.0
TOP = 32000.0
TINY = 1e-30


def params(mib=8):
    return pltpu.CompilerParams(vmem_limit_bytes=mib * 2**20)


def split(x):
    hi = x.astype(BF16)
    return hi, (x - hi.astype(F32)).astype(BF16)


def encode(x):
    top = jnp.maximum(jnp.max(jnp.abs(x), axis=0, keepdims=True), TINY)
    step = jnp.ceil(jnp.log2(top * (1.0 / TOP)) * STEPS)
    code = jnp.round(x * jnp.exp2(step * (-1.0 / STEPS)))
    return code.astype(I32).astype(I16), step


def put_row(tail, row, values):
    at = lax.broadcasted_iota(I32, tail.shape, 0)
    return jnp.where(at == row, values, tail)


def scales(tail):
    return jnp.exp2(tail.astype(I32).astype(F32) * (1.0 / STEPS))


def message(strips, rows):
    return jax.ShapeDtypeStruct((strips * rows + TAIL, LANES), I16)


def whole(shape):
    return pl.BlockSpec(memory_space=pltpu.VMEM)


def weighted(w_own, w_got, own, got):
    real = imag = 0.0
    for k in range(own.shape[0]):
        for w, block in ((w_own, own[k, 0]), (w_got, got[k])):
            r, j = block[0].astype(F32), block[1].astype(F32)
            real += w[k, 0] * r - w[k, 1] * j
            imag += w[k, 0] * j + w[k, 1] * r
    return real, imag


def share_kernel(after, where, w_own, w_got, own, got, *refs):
    out, tail = refs[after:]
    t = pl.program_id(0)
    size = own.shape[3]
    end = out.shape[0] - TAIL

    @pl.when(t == 0)
    def _():
        tail[...] = jnp.zeros_like(tail)

    for part, value in enumerate(weighted(w_own, w_got, own, got)):
        strip = 2 * t + part
        code, step = encode(value)
        out[pl.ds(pl.multiple_of(strip * size, TAIL), size), :] = code
        tail[...] = put_row(tail[...], strip, step)

    @pl.when(t == pl.num_programs(0) - 1)
    def _():
        out[end:, :] = tail[...].astype(I32).astype(I16)


def own_kernel(where, w_own, w_got, own, got, out):
    for part, value in enumerate(weighted(w_own, w_got, own, got)):
        out[0, part] = value


def share(where, w_own, w_got, inverse, got, first, count, after):
    terms, _, _, size, _ = inverse.shape
    smem = pl.BlockSpec(memory_space=pltpu.SMEM)
    out = message(2 * count, size)
    return pl.pallas_call(
        functools.partial(share_kernel, len(after)),
        out_shape=out,
        grid_spec=pltpu.PrefetchScalarGridSpec(
            num_scalar_prefetch=1,
            grid=(count,),
            in_specs=[smem, smem]
            + operator_specs(terms, size, 2, first)
            + [pl.BlockSpec(memory_space=pl.ANY)] * len(after),
            out_specs=whole(out.shape),
            scratch_shapes=[pltpu.VMEM((TAIL, LANES), F32)],
        ),
        compiler_params=params(),
        cost_estimate=pl.CostEstimate(
            flops=32 * terms * size * LANES * count,
            bytes_accessed=16 * size * LANES * count,
            transcendentals=0,
        ),
        name="share",
    )(where, w_own, w_got, inverse, got, *after)


def operator_specs(terms, size, bits, first):
    return [
        pl.BlockSpec(
            (terms, 1, 2, size, LANES), lambda t, where: (0, where[bits], 0, 0, t + first)
        ),
        pl.BlockSpec((terms, 2, size, LANES), lambda t, where: (0, 0, 0, t + first)),
    ]


def operator(where, w_own, w_got, inverse, got):
    terms, _, _, size, _ = inverse.shape
    tiles = size // LANES
    smem = pl.BlockSpec(memory_space=pltpu.SMEM)
    return pl.pallas_call(
        own_kernel,
        out_shape=jax.ShapeDtypeStruct((tiles, 2, size, LANES), F32),
        grid_spec=pltpu.PrefetchScalarGridSpec(
            num_scalar_prefetch=1,
            grid=(tiles,),
            in_specs=[smem, smem] + operator_specs(terms, size, 0, 0),
            out_specs=pl.BlockSpec((1, 2, size, LANES), lambda t, where: (t, 0, 0, 0)),
        ),
        compiler_params=params(),
        cost_estimate=pl.CostEstimate(
            flops=32 * terms * size * size,
            bytes_accessed=16 * size * size,
            transcendentals=0,
        ),
        name="operator",
    )(where, w_own, w_got, inverse, got)


def table_kernel(where, legendre, after, out):
    out[...] = legendre[0]


def slot_table(where, legendre, after):
    _, size, nlat = legendre.shape
    return pl.pallas_call(
        table_kernel,
        out_shape=jax.ShapeDtypeStruct((size, nlat), legendre.dtype),
        grid_spec=pltpu.PrefetchScalarGridSpec(
            num_scalar_prefetch=1,
            grid=(size // LANES,),
            in_specs=[
                pl.BlockSpec((1, LANES, nlat), lambda i, where: (where[0], i, 0)),
                pl.BlockSpec(memory_space=pl.ANY),
            ],
            out_specs=pl.BlockSpec((LANES, nlat), lambda i, where: (i, 0)),
        ),
        compiler_params=params(),
        name="table",
    )(where, legendre, after)


def build_kernel(first, held, own, *refs):
    got, op = refs[: len(held)], refs[len(held)]
    size = own.shape[2]
    sources = [(ref, i) for ref, n in zip(got, held) for i in range(n)]
    for t, (ref, i) in enumerate(sources):
        table = scales(ref[ref.shape[0] - TAIL :, :])
        real, imag = (
            own[first + t, strip % 2]
            + ref[strip * size : (strip + 1) * size, :].astype(I32).astype(F32)
            * table[strip : strip + 1, :]
            for strip in (2 * i, 2 * i + 1)
        )
        for level, (r, j) in enumerate(zip(split(real), split(imag))):
            op[t, level, :size, :LANES] = r
            op[t, level, :size, LANES:] = j
            op[t, level, size:, :LANES] = -j
            op[t, level, size:, LANES:] = r


def build(own, got, first, held):
    size = own.shape[2]
    out = jax.ShapeDtypeStruct((sum(held), 2, 2 * size, 2 * LANES), BF16)
    return pl.pallas_call(
        functools.partial(build_kernel, first, held),
        out_shape=out,
        in_specs=[whole(x.shape) for x in (own, *got)],
        out_specs=whole(out.shape),
        compiler_params=params(),
        cost_estimate=pl.CostEstimate(
            flops=8 * out.size, bytes_accessed=4 * out.size, transcendentals=0
        ),
        name="build",
    )(own, *got)


def product_kernel(pieces, count, after, *refs):
    parts, op = refs[:pieces], refs[pieces]
    refs = refs[pieces + 1 + after :]
    near, sends, full = refs[0], refs[1:count], refs[count]
    tiles = op.shape[0]
    rows = parts[0].shape[0]
    start = 0
    for part in parts:
        full[start : start + part.shape[0], :] = part[...]
        start += part.shape[0]
    tails = [jnp.zeros((TAIL, LANES), F32)] * (count - 1)
    for t in range(tiles):
        x = full[...]
        acc = jnp.dot(x, op[t, 0], preferred_element_type=F32)
        acc += jnp.dot(x, op[t, 1], preferred_element_type=F32)
        near[t] = acc[:rows]
        for q in range(1, count):
            for part in range(2):
                strip = 2 * t + part
                block = acc[q * rows : (q + 1) * rows, part * LANES : (part + 1) * LANES]
                code, step = encode(block)
                sends[q - 1][strip * rows : (strip + 1) * rows, :] = code
                tails[q - 1] = put_row(tails[q - 1], strip, step)
    for send, tail in zip(sends, tails):
        send[2 * tiles * rows :, :] = tail.astype(I32).astype(I16)


def product(parts, op, after):
    tiles = op.shape[0]
    rows, width = parts[0].shape
    count = sum(part.shape[0] for part in parts) // rows
    send = message(2 * tiles, rows)
    return pl.pallas_call(
        functools.partial(product_kernel, len(parts), count, len(after)),
        out_shape=[jax.ShapeDtypeStruct((tiles, rows, 2 * LANES), F32)] + [send] * (count - 1),
        in_specs=[whole(x.shape) for x in (*parts, op)]
        + [pl.BlockSpec(memory_space=pl.ANY)] * len(after),
        out_specs=[whole(send.shape)] * count,
        scratch_shapes=[pltpu.VMEM((count * rows, width), BF16)],
        compiler_params=params(),
        cost_estimate=pl.CostEstimate(
            flops=8 * count * rows * width * tiles * LANES,
            bytes_accessed=2 * op.size + 2 * count * rows * width,
            transcendentals=0,
        ),
        name="product",
    )(*parts, op, *after)


def add_up(near, got, write):
    base = 0
    for own, parts in zip(near, got):
        tiles, rows, _ = own.shape
        tables = [scales(part[2 * tiles * rows :, :]) for part in parts]
        for t in range(tiles):
            for part in range(2):
                strip = 2 * t + part
                total = own[t, :, part * LANES : (part + 1) * LANES]
                for ref, table in zip(parts, tables):
                    code = ref[strip * rows : (strip + 1) * rows, :]
                    total += code.astype(I32).astype(F32) * table[strip : strip + 1, :]
                write(base + t, part, total)
        base += tiles


def unpack(refs, chunks, count):
    near = refs[:chunks]
    got = [refs[chunks + i * count : chunks + (i + 1) * count] for i in range(chunks)]
    return near, got, refs[chunks * (1 + count) :]


def synthesis_kernel(bands, chunks, count, where, *refs):
    near, got, rest = unpack(refs, chunks, count)
    table, outs, values = rest[0], rest[1:-1], rest[-1]
    rows = near[0].shape[1]
    quarter = rows // 4
    band = table.shape[1] // bands

    def write(tile, part, total):
        for level, value in enumerate(split(total)):
            values[
                level, part * rows : (part + 1) * rows, tile * LANES : (tile + 1) * LANES
            ] = value

    add_up(near, got, write)
    for d in reversed(range(bands)):
        start = pl.multiple_of((where[4] ^ d) * band, LANES)
        columns = table[:, pl.ds(start, band)]
        grid = jnp.dot(values[0], columns, preferred_element_type=F32)
        grid += jnp.dot(values[1], columns, preferred_element_type=F32)
        for side in range(4):
            out = outs[4 * d + side]
            if len(out.shape) == 3:
                for part in range(2):
                    start = part * rows + side * quarter
                    out[part] = grid[start : start + quarter]
                continue
            tail = jnp.zeros((TAIL, LANES), F32)
            for part in range(2):
                start = part * rows + side * quarter
                for k in range(band // LANES):
                    strip = 2 * k + part
                    code, step = encode(
                        grid[start : start + quarter, k * LANES : (k + 1) * LANES]
                    )
                    out[strip * quarter : (strip + 1) * quarter, :] = code
                    tail = put_row(tail, strip, step)
            out[out.shape[0] - TAIL :, :] = tail.astype(I32).astype(I16)


def synthesis(where, near, got, table, bands):
    rows = near[0].shape[1]
    size, nlat = table.shape
    band = nlat // bands
    send = message(2 * band // LANES, rows // 4)
    outs = [jax.ShapeDtypeStruct((2, rows // 4, band), F32)] + [send] * (4 * bands - 1)
    operands = [*near, *[part for parts in got for part in parts], table]
    return pl.pallas_call(
        functools.partial(synthesis_kernel, bands, len(near), len(got[0])),
        out_shape=outs,
        in_specs=[pl.BlockSpec(memory_space=pltpu.SMEM)] + [whole(x.shape) for x in operands],
        out_specs=[whole(out.shape) for out in outs],
        scratch_shapes=[pltpu.VMEM((2, 2 * rows, size), BF16)],
        compiler_params=params(),
        cost_estimate=pl.CostEstimate(
            flops=8 * rows * size * nlat,
            bytes_accessed=2 * size * nlat + 8 * rows * nlat,
            transcendentals=0,
        ),
        name="synthesis",
    )(where, *operands)


def total_kernel(chunks, count, *refs):
    near, got, (out,) = unpack(refs, chunks, count)

    def write(tile, part, total):
        out[part, :, tile * LANES : (tile + 1) * LANES] = total

    add_up(near, got, write)


def plain_synthesis(where, near, got, table, bands):
    rows = near[0].shape[1]
    size, nlat = table.shape
    total = pl.pallas_call(
        functools.partial(total_kernel, len(near), len(got[0])),
        out_shape=jax.ShapeDtypeStruct((2, rows, size), F32),
        compiler_params=params(),
        name="total",
    )(*near, *[part for parts in got for part in parts])
    grid = sum(
        jnp.einsum("pcn,nl->pcl", v, table, preferred_element_type=F32) for v in split(total)
    )
    quarter, band = rows // 4, nlat // bands
    return [
        lax.dynamic_slice(grid, (0, side * quarter, (where[4] ^ d) * band), (2, quarter, band))
        for d in range(bands)
        for side in range(4)
    ]


def place_kernel(count, slots, where, column, *refs):
    pieces, out, full, sems = refs[:count], refs[count], refs[count + 1], refs[count + 2]
    _, _, rows, lanes = full.shape
    copies = []
    for i, piece in enumerate(pieces):
        if len(piece.shape) == 3:
            full[i] = piece[...]
        else:
            strips = 2 * lanes // LANES
            table = scales(piece[strips * rows :, :])
            for strip in range(strips):
                code = piece[strip * rows : (strip + 1) * rows, :]
                at = strip // 2 * LANES
                full[i, strip % 2, :, at : at + LANES] = (
                    code.astype(I32).astype(F32) * table[strip : strip + 1, :]
                )
        slot = column[(where[4] ^ (i // 4)) * slots + where[i % 4]]
        copies.append(pltpu.make_async_copy(full.at[i], out.at[slot], sems.at[i]))
        copies[-1].start()
    for copy in copies:
        copy.wait()


def place(where, column, slots, pieces):
    count = len(pieces)
    shape = (count,) + pieces[0].shape
    smem = pl.BlockSpec(memory_space=pltpu.SMEM)
    return pl.pallas_call(
        functools.partial(place_kernel, count, slots),
        out_shape=jax.ShapeDtypeStruct(shape, F32),
        in_specs=[smem, smem] + [whole(piece.shape) for piece in pieces],
        out_specs=pl.BlockSpec(memory_space=pl.ANY),
        scratch_shapes=[pltpu.VMEM(shape, F32), pltpu.SemaphoreType.DMA((count,))],
        compiler_params=params(),
        name="place",
    )(where, column, *pieces)


def pick_kernel(where, *refs):
    count = len(refs) // 2
    for i in range(count):
        refs[count + i][...] = refs[i][0]


def pick(where, state):
    shape = state.shape[1:]
    block = lambda i: pl.BlockSpec((1,) + shape, lambda _, where: (where[i], 0, 0))
    return pl.pallas_call(
        pick_kernel,
        out_shape=[jax.ShapeDtypeStruct(shape, state.dtype)] * 4,
        grid_spec=pltpu.PrefetchScalarGridSpec(
            num_scalar_prefetch=1,
            grid=(1,),
            in_specs=[block(i) for i in range(4)],
            out_specs=[whole(shape)] * 4,
        ),
        compiler_params=params(),
        name="pick",
    )(where, *[state] * 4)


def shards(mesh, spectral_state, inverse, term_weights, legendre, slot_column):
    terms, waves = mesh.shape["term"], mesh.shape["wave"]
    slots, cols, width = spectral_state.shape
    size = width // 2
    outer = terms // 4
    me, wave = lax.axis_index("term"), lax.axis_index("wave")
    place_of = me % 4

    def swap(x, term_bits, wave_bits=0):
        pairs = [
            (t * waves + w, (t ^ term_bits) * waves + (w ^ wave_bits))
            for t in range(terms)
            for w in range(waves)
        ]
        return lax.ppermute(x, ("term", "wave"), pairs)

    tiles = size // LANES
    assert slots == 4
    where = jnp.stack([place_of ^ bits for bits in range(4)] + [wave]).astype(I32)
    states = pick(where, spectral_state)
    received = [swap(states[bits], bits) for bits in range(1, 4)]
    turned, received[0] = lax.optimization_barrier((place_of, received[0]))
    block = jnp.concatenate([states[0]] + received, axis=0)
    steps = [q for q in range(1, outer) if q != 2] + [2]
    parts = [block] + [swap(block, q * 4) for q in steps[:-1]]
    half = block.shape[0] // 2
    parts += [swap(parts[1][:half], 3 * 4), swap(parts[2][half:], 1 * 4)]

    w_got = swap(term_weights, 1)
    far, own = (
        swap(lax.dynamic_index_in_dim(inverse, turned ^ bits, 1, keepdims=False), 1)
        for bits in (3, 1)
    )
    mine = operator(where, term_weights, w_got, inverse, own)
    groups = ((2, 1), (2,))
    shares, near, got = [], [], []
    first = 0
    for group in groups:
        start, messages = first, []
        for n in group:
            after = (block,) if not shares else (shares[-1], mine)
            shares.append(
                share(where, term_weights, w_got, inverse, far, first, n, after)
            )
            messages.append(swap(shares[-1], 2))
            first += n
        after = [near[-1], got[-1][0]] if near else []
        made = product(parts, build(mine, messages, start, group), after)
        near.append(made[0])
        got.append([swap(send, q * 4) for send, q in zip(made[1:], steps)])
    make = synthesis if legendre.shape[2] // waves % LANES == 0 else plain_synthesis
    table = slot_table(where, legendre, near[-1])
    grid = make(where, near, got, table, waves)
    pieces = [
        swap(grid[4 * d + bits], bits, d) if d or bits else grid[0]
        for d in range(waves)
        for bits in range(4)
    ]
    return place(where, slot_column, slots, pieces)


def solution(mesh):
    return jax.shard_map(
        functools.partial(shards, mesh),
        mesh=mesh,
        in_specs=(
            P("wave", "term", None),
            P("term", "wave", None, None, None),
            P("term", None),
            P("wave", None, None),
            P(),
        ),
        out_specs=P(None, None, "term", "wave"),
        check_vma=False,
    )
```

```python
import functools

import jax
import jax.numpy as jnp
from jax import lax
from jax.experimental import pallas as pl
from jax.experimental.pallas import tpu as pltpu
from jax.sharding import PartitionSpec as P

F32, BF16, I16, I32 = jnp.float32, jnp.bfloat16, jnp.int16, jnp.int32
LANES = 128
TAIL = 16
STEPS = 64.0
TOP = 32000.0
TINY = 1e-30


def params(mib=8):
    return pltpu.CompilerParams(vmem_limit_bytes=mib * 2**20)


def split(x):
    hi = x.astype(BF16)
    return hi, (x - hi.astype(F32)).astype(BF16)


def encode(x):
    top = jnp.maximum(jnp.max(jnp.abs(x), axis=0, keepdims=True), TINY)
    step = jnp.ceil(jnp.log2(top * (1.0 / TOP)) * STEPS)
    code = jnp.round(x * jnp.exp2(step * (-1.0 / STEPS)))
    return code.astype(I32).astype(I16), step


def put_row(tail, row, values):
    at = lax.broadcasted_iota(I32, tail.shape, 0)
    return jnp.where(at == row, values, tail)


def scales(tail):
    return jnp.exp2(tail.astype(I32).astype(F32) * (1.0 / STEPS))


def message(strips, rows):
    return jax.ShapeDtypeStruct((strips * rows + TAIL, LANES), I16)


def whole(shape):
    return pl.BlockSpec(memory_space=pltpu.VMEM)


def weighted(w_own, w_got, own, got):
    real = imag = 0.0
    for k in range(own.shape[0]):
        for w, block in ((w_own, own[k, 0]), (w_got, got[k])):
            r, j = block[0].astype(F32), block[1].astype(F32)
            real += w[k, 0] * r - w[k, 1] * j
            imag += w[k, 0] * j + w[k, 1] * r
    return real, imag


def share_kernel(after, where, w_own, w_got, own, got, *refs):
    out, tail = refs[after:]
    t = pl.program_id(0)
    size = own.shape[3]
    end = out.shape[0] - TAIL

    @pl.when(t == 0)
    def _():
        tail[...] = jnp.zeros_like(tail)

    for part, value in enumerate(weighted(w_own, w_got, own, got)):
        strip = 2 * t + part
        code, step = encode(value)
        out[pl.ds(pl.multiple_of(strip * size, TAIL), size), :] = code
        tail[...] = put_row(tail[...], strip, step)

    @pl.when(t == pl.num_programs(0) - 1)
    def _():
        out[end:, :] = tail[...].astype(I32).astype(I16)


def own_kernel(where, w_own, w_got, own, got, out):
    for part, value in enumerate(weighted(w_own, w_got, own, got)):
        out[0, part] = value


def share(where, w_own, w_got, inverse, got, first, count, after):
    terms, _, _, size, _ = inverse.shape
    smem = pl.BlockSpec(memory_space=pltpu.SMEM)
    out = message(2 * count, size)
    return pl.pallas_call(
        functools.partial(share_kernel, len(after)),
        out_shape=out,
        grid_spec=pltpu.PrefetchScalarGridSpec(
            num_scalar_prefetch=1,
            grid=(count,),
            in_specs=[smem, smem]
            + operator_specs(terms, size, 2, first)
            + [pl.BlockSpec(memory_space=pl.ANY)] * len(after),
            out_specs=whole(out.shape),
            scratch_shapes=[pltpu.VMEM((TAIL, LANES), F32)],
        ),
        compiler_params=params(),
        cost_estimate=pl.CostEstimate(
            flops=32 * terms * size * LANES * count,
            bytes_accessed=16 * size * LANES * count,
            transcendentals=0,
        ),
        name="share",
    )(where, w_own, w_got, inverse, got, *after)


def operator_specs(terms, size, bits, first):
    return [
        pl.BlockSpec(
            (terms, 1, 2, size, LANES), lambda t, where: (0, where[bits], 0, 0, t + first)
        ),
        pl.BlockSpec((terms, 2, size, LANES), lambda t, where: (0, 0, 0, t + first)),
    ]


def operator(where, w_own, w_got, inverse, got):
    terms, _, _, size, _ = inverse.shape
    tiles = size // LANES
    smem = pl.BlockSpec(memory_space=pltpu.SMEM)
    return pl.pallas_call(
        own_kernel,
        out_shape=jax.ShapeDtypeStruct((tiles, 2, size, LANES), F32),
        grid_spec=pltpu.PrefetchScalarGridSpec(
            num_scalar_prefetch=1,
            grid=(tiles,),
            in_specs=[smem, smem] + operator_specs(terms, size, 0, 0),
            out_specs=pl.BlockSpec((1, 2, size, LANES), lambda t, where: (t, 0, 0, 0)),
        ),
        compiler_params=params(),
        cost_estimate=pl.CostEstimate(
            flops=32 * terms * size * size,
            bytes_accessed=16 * size * size,
            transcendentals=0,
        ),
        name="operator",
    )(where, w_own, w_got, inverse, got)


def table_kernel(where, legendre, after, out):
    out[...] = legendre[0]


def slot_table(where, legendre, after):
    _, size, nlat = legendre.shape
    return pl.pallas_call(
        table_kernel,
        out_shape=jax.ShapeDtypeStruct((size, nlat), legendre.dtype),
        grid_spec=pltpu.PrefetchScalarGridSpec(
            num_scalar_prefetch=1,
            grid=(size // LANES,),
            in_specs=[
                pl.BlockSpec((1, LANES, nlat), lambda i, where: (where[0], i, 0)),
                pl.BlockSpec(memory_space=pl.ANY),
            ],
            out_specs=pl.BlockSpec((LANES, nlat), lambda i, where: (i, 0)),
        ),
        compiler_params=params(),
        name="table",
    )(where, legendre, after)


def build_kernel(first, held, own, *refs):
    got, op = refs[: len(held)], refs[len(held)]
    size = own.shape[2]
    sources = [(ref, i) for ref, n in zip(got, held) for i in range(n)]
    for t, (ref, i) in enumerate(sources):
        table = scales(ref[ref.shape[0] - TAIL :, :])
        real, imag = (
            own[first + t, strip % 2]
            + ref[strip * size : (strip + 1) * size, :].astype(I32).astype(F32)
            * table[strip : strip + 1, :]
            for strip in (2 * i, 2 * i + 1)
        )
        for level, (r, j) in enumerate(zip(split(real), split(imag))):
            op[t, level, :size, :LANES] = r
            op[t, level, :size, LANES:] = j
            op[t, level, size:, :LANES] = -j
            op[t, level, size:, LANES:] = r


def build(own, got, first, held):
    size = own.shape[2]
    out = jax.ShapeDtypeStruct((sum(held), 2, 2 * size, 2 * LANES), BF16)
    return pl.pallas_call(
        functools.partial(build_kernel, first, held),
        out_shape=out,
        in_specs=[whole(x.shape) for x in (own, *got)],
        out_specs=whole(out.shape),
        compiler_params=params(),
        cost_estimate=pl.CostEstimate(
            flops=8 * out.size, bytes_accessed=4 * out.size, transcendentals=0
        ),
        name="build",
    )(own, *got)


def product_kernel(pieces, kept, after, *refs):
    parts, op = refs[:pieces], refs[pieces]
    refs = refs[pieces + 1 + after :]
    outs, full = refs[:pieces], refs[pieces]
    tiles = op.shape[0]
    rows = parts[0].shape[0]
    for i, part in enumerate(parts):
        full[i * rows : (i + 1) * rows, :] = part[...]
    tails = {q: jnp.zeros((TAIL, LANES), F32) for q in range(pieces) if q not in kept}
    for t in range(tiles):
        x = full[...]
        acc = jnp.dot(x, op[t, 0], preferred_element_type=F32)
        acc += jnp.dot(x, op[t, 1], preferred_element_type=F32)
        for q in range(pieces):
            block = acc[q * rows : (q + 1) * rows]
            if q in kept:
                outs[q][t] = block
                continue
            for part in range(2):
                strip = 2 * t + part
                code, step = encode(block[:, part * LANES : (part + 1) * LANES])
                outs[q][strip * rows : (strip + 1) * rows, :] = code
                tails[q] = put_row(tails[q], strip, step)
    for q, tail in tails.items():
        outs[q][2 * tiles * rows :, :] = tail.astype(I32).astype(I16)


def product(parts, op, kept, after):
    tiles = op.shape[0]
    rows, width = parts[0].shape
    count = len(parts)
    plain = jax.ShapeDtypeStruct((tiles, rows, 2 * LANES), F32)
    send = message(2 * tiles, rows)
    return pl.pallas_call(
        functools.partial(product_kernel, count, kept, len(after)),
        out_shape=[plain if q in kept else send for q in range(count)],
        in_specs=[whole(x.shape) for x in (*parts, op)]
        + [pl.BlockSpec(memory_space=pl.ANY)] * len(after),
        out_specs=[whole(send.shape)] * count,
        scratch_shapes=[pltpu.VMEM((count * rows, width), BF16)],
        compiler_params=params(),
        cost_estimate=pl.CostEstimate(
            flops=8 * count * rows * width * tiles * LANES,
            bytes_accessed=2 * op.size + 2 * count * rows * width,
            transcendentals=0,
        ),
        name="product",
    )(*parts, op, *after)


def fold_kernel(own, got, *refs):
    out = refs[-1]
    tail = jnp.zeros((TAIL, LANES), F32)
    sums = {}

    def write(tile, part, total):
        sums[2 * tile + part] = total

    add_up([own], [[got]], write)
    rows = own.shape[1]
    for strip, total in sums.items():
        code, step = encode(total)
        out[strip * rows : (strip + 1) * rows, :] = code
        tail = put_row(tail, strip, step)
    out[out.shape[0] - TAIL :, :] = tail.astype(I32).astype(I16)


def fold(own, got, after):
    return pl.pallas_call(
        fold_kernel,
        out_shape=jax.ShapeDtypeStruct(got.shape, got.dtype),
        in_specs=[whole(own.shape), whole(got.shape)]
        + [pl.BlockSpec(memory_space=pl.ANY)] * len(after),
        out_specs=whole(got.shape),
        compiler_params=params(),
        cost_estimate=pl.CostEstimate(
            flops=12 * own.size, bytes_accessed=8 * own.size, transcendentals=0
        ),
        name="fold",
    )(own, got, *after)


def add_up(near, got, write):
    base = 0
    for own, parts in zip(near, got):
        tiles, rows, _ = own.shape
        tables = [scales(part[2 * tiles * rows :, :]) for part in parts]
        for t in range(tiles):
            for part in range(2):
                strip = 2 * t + part
                total = own[t, :, part * LANES : (part + 1) * LANES]
                for ref, table in zip(parts, tables):
                    code = ref[strip * rows : (strip + 1) * rows, :]
                    total += code.astype(I32).astype(F32) * table[strip : strip + 1, :]
                write(base + t, part, total)
        base += tiles


def unpack(refs, counts):
    near, refs, got = refs[: len(counts)], refs[len(counts) :], []
    for count in counts:
        got.append(refs[:count])
        refs = refs[count:]
    return near, got, refs


def synthesis_kernel(bands, counts, where, *refs):
    near, got, rest = unpack(refs, counts)
    table, outs, values = rest[0], rest[1:-1], rest[-1]
    rows = near[0].shape[1]
    quarter = rows // 4
    band = table.shape[1] // bands

    def write(tile, part, total):
        for level, value in enumerate(split(total)):
            values[
                level, part * rows : (part + 1) * rows, tile * LANES : (tile + 1) * LANES
            ] = value

    add_up(near, got, write)
    for d in reversed(range(bands)):
        start = pl.multiple_of((where[4] ^ d) * band, LANES)
        columns = table[:, pl.ds(start, band)]
        grid = jnp.dot(values[0], columns, preferred_element_type=F32)
        grid += jnp.dot(values[1], columns, preferred_element_type=F32)
        for side in range(4):
            out = outs[4 * d + side]
            if len(out.shape) == 3:
                for part in range(2):
                    start = part * rows + side * quarter
                    out[part] = grid[start : start + quarter]
                continue
            tail = jnp.zeros((TAIL, LANES), F32)
            for part in range(2):
                start = part * rows + side * quarter
                for k in range(band // LANES):
                    strip = 2 * k + part
                    code, step = encode(
                        grid[start : start + quarter, k * LANES : (k + 1) * LANES]
                    )
                    out[strip * quarter : (strip + 1) * quarter, :] = code
                    tail = put_row(tail, strip, step)
            out[out.shape[0] - TAIL :, :] = tail.astype(I32).astype(I16)


def synthesis(where, near, got, table, bands):
    rows = near[0].shape[1]
    size, nlat = table.shape
    band = nlat // bands
    send = message(2 * band // LANES, rows // 4)
    outs = [jax.ShapeDtypeStruct((2, rows // 4, band), F32)] + [send] * (4 * bands - 1)
    operands = [*near, *[part for parts in got for part in parts], table]
    return pl.pallas_call(
        functools.partial(synthesis_kernel, bands, [len(parts) for parts in got]),
        out_shape=outs,
        in_specs=[pl.BlockSpec(memory_space=pltpu.SMEM)] + [whole(x.shape) for x in operands],
        out_specs=[whole(out.shape) for out in outs],
        scratch_shapes=[pltpu.VMEM((2, 2 * rows, size), BF16)],
        compiler_params=params(),
        cost_estimate=pl.CostEstimate(
            flops=8 * rows * size * nlat,
            bytes_accessed=2 * size * nlat + 8 * rows * nlat,
            transcendentals=0,
        ),
        name="synthesis",
    )(where, *operands)


def total_kernel(counts, *refs):
    near, got, (out,) = unpack(refs, counts)

    def write(tile, part, total):
        out[part, :, tile * LANES : (tile + 1) * LANES] = total

    add_up(near, got, write)


def plain_synthesis(where, near, got, table, bands):
    rows = near[0].shape[1]
    size, nlat = table.shape
    total = pl.pallas_call(
        functools.partial(total_kernel, [len(parts) for parts in got]),
        out_shape=jax.ShapeDtypeStruct((2, rows, size), F32),
        compiler_params=params(),
        name="total",
    )(*near, *[part for parts in got for part in parts])
    grid = sum(
        jnp.einsum("pcn,nl->pcl", v, table, preferred_element_type=F32) for v in split(total)
    )
    quarter, band = rows // 4, nlat // bands
    return [
        lax.dynamic_slice(grid, (0, side * quarter, (where[4] ^ d) * band), (2, quarter, band))
        for d in range(bands)
        for side in range(4)
    ]


def place_kernel(count, slots, order, where, column, *refs):
    pieces, out, full, sems = refs[:count], refs[count], refs[count + 1], refs[count + 2]
    _, _, rows, lanes = full.shape
    copies = []
    for i, piece in enumerate(pieces):
        if len(piece.shape) == 3:
            full[i] = piece[...]
        else:
            strips = 2 * lanes // LANES
            table = scales(piece[strips * rows :, :])
            for strip in range(strips):
                code = piece[strip * rows : (strip + 1) * rows, :]
                at = strip // 2 * LANES
                full[i, strip % 2, :, at : at + LANES] = (
                    code.astype(I32).astype(F32) * table[strip : strip + 1, :]
                )
        d, bits = order[i]
        slot = column[(where[4] ^ d) * slots + where[bits]]
        copies.append(pltpu.make_async_copy(full.at[i], out.at[slot], sems.at[i]))
        copies[-1].start()
    for copy in copies:
        copy.wait()


def place(where, column, slots, order, pieces):
    count = len(pieces)
    shape = (count,) + pieces[order.index((0, 0))].shape
    smem = pl.BlockSpec(memory_space=pltpu.SMEM)
    return pl.pallas_call(
        functools.partial(place_kernel, count, slots, order),
        out_shape=jax.ShapeDtypeStruct(shape, F32),
        in_specs=[smem, smem] + [whole(piece.shape) for piece in pieces],
        out_specs=pl.BlockSpec(memory_space=pl.ANY),
        scratch_shapes=[pltpu.VMEM(shape, F32), pltpu.SemaphoreType.DMA((count,))],
        compiler_params=params(),
        name="place",
    )(where, column, *pieces)


def pick_kernel(where, *refs):
    count = len(refs) // 2
    for i in range(count):
        refs[count + i][...] = refs[i][0]


def pick(where, state):
    shape = state.shape[1:]
    block = lambda i: pl.BlockSpec((1,) + shape, lambda _, where: (where[i], 0, 0))
    return pl.pallas_call(
        pick_kernel,
        out_shape=[jax.ShapeDtypeStruct(shape, state.dtype)] * 4,
        grid_spec=pltpu.PrefetchScalarGridSpec(
            num_scalar_prefetch=1,
            grid=(1,),
            in_specs=[block(i) for i in range(4)],
            out_specs=[whole(shape)] * 4,
        ),
        compiler_params=params(),
        name="pick",
    )(where, *[state] * 4)


def shards(mesh, spectral_state, inverse, term_weights, legendre, slot_column):
    terms, waves = mesh.shape["term"], mesh.shape["wave"]
    slots, cols, width = spectral_state.shape
    size = width // 2
    outer = terms // 4
    me, wave = lax.axis_index("term"), lax.axis_index("wave")
    place_of = me % 4

    def swap(x, term_bits, wave_bits=0):
        pairs = [
            (t * waves + w, (t ^ term_bits) * waves + (w ^ wave_bits))
            for t in range(terms)
            for w in range(waves)
        ]
        return lax.ppermute(x, ("term", "wave"), pairs)

    tiles = size // LANES
    assert slots == 4
    where = jnp.stack([place_of ^ bits for bits in range(4)] + [wave]).astype(I32)
    states = pick(where, spectral_state)
    received = [swap(states[bits], bits) for bits in range(1, 4)]
    turned, received[0] = lax.optimization_barrier((place_of, received[0]))
    block = jnp.concatenate([states[0]] + received, axis=0)
    steps = [3, 1] + list(range(4, outer)) + [2]
    parts = [block] + [swap(block, q * 4) for q in steps[:-1]]
    parts.append(swap(parts[1], 1 * 4))

    w_got = swap(term_weights, 1)
    far, own = (
        swap(lax.dynamic_index_in_dim(inverse, turned ^ bits, 1, keepdims=False), 1)
        for bits in (3, 1)
    )
    mine = operator(where, term_weights, w_got, inverse, own)
    groups = ((2, 1), (2,))
    shares, near, got = [], [], []
    first = 0
    for group in groups:
        start, messages = first, []
        for n in group:
            after = () if not shares else (shares[-1], mine)
            shares.append(
                share(where, term_weights, w_got, inverse, far, first, n, after)
            )
            messages.append(swap(shares[-1], 2))
            first += n
        after = [near[-1], got[-1][0]] if near else []
        op = build(mine, messages, start, group)
        if group is not groups[-1]:
            made = product(parts, op, (0,), after)
            sends = made[1:]
        else:
            made = product(parts, op, (0, 1), after)
            sends = [fold(made[1], swap(made[-1], 1 * 4), got[-1][1:] if got else []), *made[2:-1]]
        near.append(made[0])
        got.append([swap(send, q * 4) for send, q in zip(sends, steps)])
    make = synthesis if legendre.shape[2] // waves % LANES == 0 else plain_synthesis
    table = slot_table(where, legendre, near[-1])
    grid = make(where, near, got, table, waves)
    order = [(d, bits) for d in reversed(range(waves)) for bits in (2, 3, 0, 1)]
    order.append(order.pop(order.index((0, 0))))
    pieces = [
        swap(grid[4 * d + bits], bits, d) if d or bits else grid[0] for d, bits in order
    ]
    return place(where, slot_column, slots, order, pieces)


def solution(mesh):
    return jax.shard_map(
        functools.partial(shards, mesh),
        mesh=mesh,
        in_specs=(
            P("wave", "term", None),
            P("term", "wave", None, None, None),
            P("term", None),
            P("wave", None, None),
            P(),
        ),
        out_specs=P(None, None, "term", "wave"),
        check_vma=False,
    )
```

```python
import functools

import jax
import jax.numpy as jnp
from jax import lax
from jax.experimental import pallas as pl
from jax.experimental.pallas import tpu as pltpu
from jax.sharding import PartitionSpec as P

F32, BF16, I16, I32 = jnp.float32, jnp.bfloat16, jnp.int16, jnp.int32
LANES = 128
TAIL = 16
STEPS = 64.0
TOP = 32000.0
TINY = 1e-30


def params(mib=8):
    return pltpu.CompilerParams(vmem_limit_bytes=mib * 2**20)


def split(x):
    hi = x.astype(BF16)
    return hi, (x - hi.astype(F32)).astype(BF16)


def encode(x):
    top = jnp.maximum(jnp.max(jnp.abs(x), axis=0, keepdims=True), TINY)
    step = jnp.ceil(jnp.log2(top * (1.0 / TOP)) * STEPS)
    code = jnp.round(x * jnp.exp2(step * (-1.0 / STEPS)))
    return code.astype(I32).astype(I16), step


def put_row(tail, row, values):
    at = lax.broadcasted_iota(I32, tail.shape, 0)
    return jnp.where(at == row, values, tail)


def scales(tail):
    return jnp.exp2(tail.astype(I32).astype(F32) * (1.0 / STEPS))


def message(strips, rows):
    return jax.ShapeDtypeStruct((strips * rows + TAIL, LANES), I16)


def whole(shape):
    return pl.BlockSpec(memory_space=pltpu.VMEM)


def weighted(w_own, w_got, own, got):
    real = imag = 0.0
    for k in range(own.shape[0]):
        for w, block in ((w_own, own[k, 0]), (w_got, got[k])):
            r, j = block[0].astype(F32), block[1].astype(F32)
            real += w[k, 0] * r - w[k, 1] * j
            imag += w[k, 0] * j + w[k, 1] * r
    return real, imag


def share_kernel(after, where, w_own, w_got, own, got, *refs):
    out, tail = refs[after:]
    t = pl.program_id(0)
    size = own.shape[3]
    end = out.shape[0] - TAIL

    @pl.when(t == 0)
    def _():
        tail[...] = jnp.zeros_like(tail)

    for part, value in enumerate(weighted(w_own, w_got, own, got)):
        strip = 2 * t + part
        code, step = encode(value)
        out[pl.ds(pl.multiple_of(strip * size, TAIL), size), :] = code
        tail[...] = put_row(tail[...], strip, step)

    @pl.when(t == pl.num_programs(0) - 1)
    def _():
        out[end:, :] = tail[...].astype(I32).astype(I16)


def own_kernel(where, w_own, w_got, own, got, out):
    for part, value in enumerate(weighted(w_own, w_got, own, got)):
        out[0, part] = value


def share(where, w_own, w_got, inverse, got, first, count, after):
    terms, _, _, size, _ = inverse.shape
    smem = pl.BlockSpec(memory_space=pltpu.SMEM)
    out = message(2 * count, size)
    return pl.pallas_call(
        functools.partial(share_kernel, len(after)),
        out_shape=out,
        grid_spec=pltpu.PrefetchScalarGridSpec(
            num_scalar_prefetch=1,
            grid=(count,),
            in_specs=[smem, smem]
            + operator_specs(terms, size, 2, first)
            + [pl.BlockSpec(memory_space=pl.ANY)] * len(after),
            out_specs=whole(out.shape),
            scratch_shapes=[pltpu.VMEM((TAIL, LANES), F32)],
        ),
        compiler_params=params(),
        cost_estimate=pl.CostEstimate(
            flops=32 * terms * size * LANES * count,
            bytes_accessed=16 * size * LANES * count,
            transcendentals=0,
        ),
        name="share",
    )(where, w_own, w_got, inverse, got, *after)


def operator_specs(terms, size, bits, first):
    return [
        pl.BlockSpec(
            (terms, 1, 2, size, LANES), lambda t, where: (0, where[bits], 0, 0, t + first)
        ),
        pl.BlockSpec((terms, 2, size, LANES), lambda t, where: (0, 0, 0, t + first)),
    ]


def operator(where, w_own, w_got, inverse, got):
    terms, _, _, size, _ = inverse.shape
    tiles = size // LANES
    smem = pl.BlockSpec(memory_space=pltpu.SMEM)
    return pl.pallas_call(
        own_kernel,
        out_shape=jax.ShapeDtypeStruct((tiles, 2, size, LANES), F32),
        grid_spec=pltpu.PrefetchScalarGridSpec(
            num_scalar_prefetch=1,
            grid=(tiles,),
            in_specs=[smem, smem] + operator_specs(terms, size, 0, 0),
            out_specs=pl.BlockSpec((1, 2, size, LANES), lambda t, where: (t, 0, 0, 0)),
        ),
        compiler_params=params(),
        cost_estimate=pl.CostEstimate(
            flops=32 * terms * size * size,
            bytes_accessed=16 * size * size,
            transcendentals=0,
        ),
        name="operator",
    )(where, w_own, w_got, inverse, got)


def table_kernel(where, legendre, after, out):
    out[...] = legendre[0]


def slot_table(where, legendre, after):
    _, size, nlat = legendre.shape
    return pl.pallas_call(
        table_kernel,
        out_shape=jax.ShapeDtypeStruct((size, nlat), legendre.dtype),
        grid_spec=pltpu.PrefetchScalarGridSpec(
            num_scalar_prefetch=1,
            grid=(size // LANES,),
            in_specs=[
                pl.BlockSpec((1, LANES, nlat), lambda i, where: (where[0], i, 0)),
                pl.BlockSpec(memory_space=pl.ANY),
            ],
            out_specs=pl.BlockSpec((LANES, nlat), lambda i, where: (i, 0)),
        ),
        compiler_params=params(),
        name="table",
    )(where, legendre, after)


def build_kernel(first, held, own, *refs):
    got, op = refs[: len(held)], refs[-1]
    size = own.shape[2]
    sources = [(ref, i) for ref, n in zip(got, held) for i in range(n)]
    for t, (ref, i) in enumerate(sources):
        table = scales(ref[ref.shape[0] - TAIL :, :])
        real, imag = (
            own[first + t, strip % 2]
            + ref[strip * size : (strip + 1) * size, :].astype(I32).astype(F32)
            * table[strip : strip + 1, :]
            for strip in (2 * i, 2 * i + 1)
        )
        for level, (r, j) in enumerate(zip(split(real), split(imag))):
            op[t, level, :size, :LANES] = r
            op[t, level, :size, LANES:] = j
            op[t, level, size:, :LANES] = -j
            op[t, level, size:, LANES:] = r


def build(own, got, first, held, after):
    size = own.shape[2]
    out = jax.ShapeDtypeStruct((sum(held), 2, 2 * size, 2 * LANES), BF16)
    return pl.pallas_call(
        functools.partial(build_kernel, first, held),
        out_shape=out,
        in_specs=[whole(x.shape) for x in (own, *got)]
        + [pl.BlockSpec(memory_space=pl.ANY)] * len(after),
        out_specs=whole(out.shape),
        compiler_params=params(),
        cost_estimate=pl.CostEstimate(
            flops=8 * out.size, bytes_accessed=4 * out.size, transcendentals=0
        ),
        name="build",
    )(own, *got, *after)


def product_kernel(pieces, kept, after, *refs):
    parts, op = refs[:pieces], refs[pieces]
    refs = refs[pieces + 1 + after :]
    outs, full = refs[:pieces], refs[pieces]
    tiles = op.shape[0]
    rows = parts[0].shape[0]
    for i, part in enumerate(parts):
        full[i * rows : (i + 1) * rows, :] = part[...]
    tails = {q: jnp.zeros((TAIL, LANES), F32) for q in range(pieces) if q not in kept}
    for t in range(tiles):
        x = full[...]
        acc = jnp.dot(x, op[t, 0], preferred_element_type=F32)
        acc += jnp.dot(x, op[t, 1], preferred_element_type=F32)
        for q in range(pieces):
            block = acc[q * rows : (q + 1) * rows]
            if q in kept:
                outs[q][t] = block
                continue
            for part in range(2):
                strip = 2 * t + part
                code, step = encode(block[:, part * LANES : (part + 1) * LANES])
                outs[q][strip * rows : (strip + 1) * rows, :] = code
                tails[q] = put_row(tails[q], strip, step)
    for q, tail in tails.items():
        outs[q][2 * tiles * rows :, :] = tail.astype(I32).astype(I16)


def product(parts, op, kept, after):
    tiles = op.shape[0]
    rows, width = parts[0].shape
    count = len(parts)
    plain = jax.ShapeDtypeStruct((tiles, rows, 2 * LANES), F32)
    send = message(2 * tiles, rows)
    return pl.pallas_call(
        functools.partial(product_kernel, count, kept, len(after)),
        out_shape=[plain if q in kept else send for q in range(count)],
        in_specs=[whole(x.shape) for x in (*parts, op)]
        + [pl.BlockSpec(memory_space=pl.ANY)] * len(after),
        out_specs=[whole(send.shape)] * count,
        scratch_shapes=[pltpu.VMEM((count * rows, width), BF16)],
        compiler_params=params(),
        cost_estimate=pl.CostEstimate(
            flops=8 * count * rows * width * tiles * LANES,
            bytes_accessed=2 * op.size + 2 * count * rows * width,
            transcendentals=0,
        ),
        name="product",
    )(*parts, op, *after)


def fold_kernel(own, got, *refs):
    out = refs[-1]
    tail = jnp.zeros((TAIL, LANES), F32)
    sums = {}

    def write(tile, part, total):
        sums[2 * tile + part] = total

    add_up([own], [[got]], write)
    rows = own.shape[1]
    for strip, total in sums.items():
        code, step = encode(total)
        out[strip * rows : (strip + 1) * rows, :] = code
        tail = put_row(tail, strip, step)
    out[out.shape[0] - TAIL :, :] = tail.astype(I32).astype(I16)


def fold(own, got, after):
    return pl.pallas_call(
        fold_kernel,
        out_shape=jax.ShapeDtypeStruct(got.shape, got.dtype),
        in_specs=[whole(own.shape), whole(got.shape)]
        + [pl.BlockSpec(memory_space=pl.ANY)] * len(after),
        out_specs=whole(got.shape),
        compiler_params=params(),
        cost_estimate=pl.CostEstimate(
            flops=12 * own.size, bytes_accessed=8 * own.size, transcendentals=0
        ),
        name="fold",
    )(own, got, *after)


def add_up(near, got, write):
    base = 0
    for own, parts in zip(near, got):
        tiles, rows, _ = own.shape
        tables = [scales(part[2 * tiles * rows :, :]) for part in parts]
        for t in range(tiles):
            for part in range(2):
                strip = 2 * t + part
                total = own[t, :, part * LANES : (part + 1) * LANES]
                for ref, table in zip(parts, tables):
                    code = ref[strip * rows : (strip + 1) * rows, :]
                    total += code.astype(I32).astype(F32) * table[strip : strip + 1, :]
                write(base + t, part, total)
        base += tiles


def unpack(refs, counts):
    near, refs, got = refs[: len(counts)], refs[len(counts) :], []
    for count in counts:
        got.append(refs[:count])
        refs = refs[count:]
    return near, got, refs


def synthesis_kernel(bands, counts, where, *refs):
    near, got, rest = unpack(refs, counts)
    table, outs, values = rest[0], rest[1:-1], rest[-1]
    rows = near[0].shape[1]
    quarter = rows // 4
    band = table.shape[1] // bands

    def write(tile, part, total):
        for level, value in enumerate(split(total)):
            values[
                level, part * rows : (part + 1) * rows, tile * LANES : (tile + 1) * LANES
            ] = value

    add_up(near, got, write)
    for d in reversed(range(bands)):
        start = pl.multiple_of((where[4] ^ d) * band, LANES)
        columns = table[:, pl.ds(start, band)]
        grid = jnp.dot(values[0], columns, preferred_element_type=F32)
        grid += jnp.dot(values[1], columns, preferred_element_type=F32)
        for side in range(4):
            out = outs[4 * d + side]
            if len(out.shape) == 3:
                for part in range(2):
                    start = part * rows + side * quarter
                    out[part] = grid[start : start + quarter]
                continue
            tail = jnp.zeros((TAIL, LANES), F32)
            for part in range(2):
                start = part * rows + side * quarter
                for k in range(band // LANES):
                    strip = 2 * k + part
                    code, step = encode(
                        grid[start : start + quarter, k * LANES : (k + 1) * LANES]
                    )
                    out[strip * quarter : (strip + 1) * quarter, :] = code
                    tail = put_row(tail, strip, step)
            out[out.shape[0] - TAIL :, :] = tail.astype(I32).astype(I16)


def synthesis(where, near, got, table, bands):
    rows = near[0].shape[1]
    size, nlat = table.shape
    band = nlat // bands
    send = message(2 * band // LANES, rows // 4)
    outs = [jax.ShapeDtypeStruct((2, rows // 4, band), F32)] + [send] * (4 * bands - 1)
    operands = [*near, *[part for parts in got for part in parts], table]
    return pl.pallas_call(
        functools.partial(synthesis_kernel, bands, [len(parts) for parts in got]),
        out_shape=outs,
        in_specs=[pl.BlockSpec(memory_space=pltpu.SMEM)] + [whole(x.shape) for x in operands],
        out_specs=[whole(out.shape) for out in outs],
        scratch_shapes=[pltpu.VMEM((2, 2 * rows, size), BF16)],
        compiler_params=params(),
        cost_estimate=pl.CostEstimate(
            flops=8 * rows * size * nlat,
            bytes_accessed=2 * size * nlat + 8 * rows * nlat,
            transcendentals=0,
        ),
        name="synthesis",
    )(where, *operands)


def total_kernel(counts, *refs):
    near, got, (out,) = unpack(refs, counts)

    def write(tile, part, total):
        out[part, :, tile * LANES : (tile + 1) * LANES] = total

    add_up(near, got, write)


def plain_synthesis(where, near, got, table, bands):
    rows = near[0].shape[1]
    size, nlat = table.shape
    total = pl.pallas_call(
        functools.partial(total_kernel, [len(parts) for parts in got]),
        out_shape=jax.ShapeDtypeStruct((2, rows, size), F32),
        compiler_params=params(),
        name="total",
    )(*near, *[part for parts in got for part in parts])
    grid = sum(
        jnp.einsum("pcn,nl->pcl", v, table, preferred_element_type=F32) for v in split(total)
    )
    quarter, band = rows // 4, nlat // bands
    return [
        lax.dynamic_slice(grid, (0, side * quarter, (where[4] ^ d) * band), (2, quarter, band))
        for d in range(bands)
        for side in range(4)
    ]


def place_kernel(count, slots, order, where, column, *refs):
    pieces, out, full, sems = refs[:count], refs[count], refs[count + 1], refs[count + 2]
    _, _, rows, lanes = full.shape
    copies = []
    for i, piece in enumerate(pieces):
        if len(piece.shape) == 3:
            full[i] = piece[...]
        else:
            strips = 2 * lanes // LANES
            table = scales(piece[strips * rows :, :])
            for strip in range(strips):
                code = piece[strip * rows : (strip + 1) * rows, :]
                at = strip // 2 * LANES
                full[i, strip % 2, :, at : at + LANES] = (
                    code.astype(I32).astype(F32) * table[strip : strip + 1, :]
                )
        d, bits = order[i]
        slot = column[(where[4] ^ d) * slots + where[bits]]
        copies.append(pltpu.make_async_copy(full.at[i], out.at[slot], sems.at[i]))
        copies[-1].start()
    for copy in copies:
        copy.wait()


def place(where, column, slots, order, pieces):
    count = len(pieces)
    shape = (count,) + pieces[order.index((0, 0))].shape
    smem = pl.BlockSpec(memory_space=pltpu.SMEM)
    return pl.pallas_call(
        functools.partial(place_kernel, count, slots, order),
        out_shape=jax.ShapeDtypeStruct(shape, F32),
        in_specs=[smem, smem] + [whole(piece.shape) for piece in pieces],
        out_specs=pl.BlockSpec(memory_space=pl.ANY),
        scratch_shapes=[pltpu.VMEM(shape, F32), pltpu.SemaphoreType.DMA((count,))],
        compiler_params=params(),
        name="place",
    )(where, column, *pieces)


def pick_kernel(where, *refs):
    count = len(refs) // 2
    for i in range(count):
        refs[count + i][...] = refs[i][0]


def pick(where, state):
    shape = state.shape[1:]
    block = lambda i: pl.BlockSpec((1,) + shape, lambda _, where: (where[i], 0, 0))
    return pl.pallas_call(
        pick_kernel,
        out_shape=[jax.ShapeDtypeStruct(shape, state.dtype)] * 4,
        grid_spec=pltpu.PrefetchScalarGridSpec(
            num_scalar_prefetch=1,
            grid=(1,),
            in_specs=[block(i) for i in range(4)],
            out_specs=[whole(shape)] * 4,
        ),
        compiler_params=params(),
        name="pick",
    )(where, *[state] * 4)


def join_kernel(*refs):
    *parts, _, out = refs
    rows = parts[0].shape[0]
    for i, part in enumerate(parts):
        out[i * rows : (i + 1) * rows, :] = part[...]


def join(parts, after):
    rows, width = parts[0].shape
    return pl.pallas_call(
        join_kernel,
        out_shape=jax.ShapeDtypeStruct((len(parts) * rows, width), parts[0].dtype),
        in_specs=[whole(part.shape) for part in parts] + [pl.BlockSpec(memory_space=pl.ANY)],
        out_specs=whole(None),
        compiler_params=params(),
        name="join",
    )(*parts, after)


def shards(mesh, spectral_state, inverse, term_weights, legendre, slot_column):
    terms, waves = mesh.shape["term"], mesh.shape["wave"]
    slots, cols, width = spectral_state.shape
    size = width // 2
    outer = terms // 4
    me, wave = lax.axis_index("term"), lax.axis_index("wave")
    place_of = me % 4

    def swap(x, term_bits, wave_bits=0):
        pairs = [
            (t * waves + w, (t ^ term_bits) * waves + (w ^ wave_bits))
            for t in range(terms)
            for w in range(waves)
        ]
        return lax.ppermute(x, ("term", "wave"), pairs)

    tiles = size // LANES
    assert slots == 4
    where = jnp.stack([place_of ^ bits for bits in range(4)] + [wave]).astype(I32)
    states = pick(where, spectral_state)
    received = [swap(states[bits], bits) for bits in range(1, 4)]
    turned, received[0] = lax.optimization_barrier((place_of, received[0]))
    w_got = swap(term_weights, 1)
    far, own = (
        swap(lax.dynamic_index_in_dim(inverse, turned ^ bits, 1, keepdims=False), 1)
        for bits in (3, 1)
    )
    last = max(1, 2 * tiles // 5)
    counts = [n for n in (last, tiles - 2 * last, last) if n]
    shares, messages = [], []
    for at, n in enumerate(counts):
        first = sum(counts[:at])
        after = () if not shares else (shares[-1], mine)[: at]
        shares.append(share(where, term_weights, w_got, inverse, far, first, n, after))
        messages.append(swap(shares[-1], 2))
        if at == 0:
            mine = operator(where, term_weights, w_got, inverse, own)
            block = join([states[0]] + received, shares[0])
            steps = [3, 1] + list(range(4, outer)) + [2]
            parts = [block] + [swap(block, q * 4) for q in steps[:-1]]
            parts.append(swap(parts[1], 1 * 4))
    near, got = [], []
    ends = [0, len(counts) - 1, len(counts)]
    for start, end in zip(ends, ends[1:]):
        after = [near[-1], got[-1][1]] if near else []
        held = counts[start:end]
        folded = sends[:1] if near else []
        op = build(mine, messages[start:end], sum(counts[:start]), held, folded)
        made = product(parts, op, (0, 1), after)
        relayed = swap(made[-1], 1 * 4)
        sends = [fold(made[1], relayed, got[-1] if got else []), *made[2:-1]]
        near.append(made[0])
        got.append([swap(send, q * 4) for send, q in zip(sends, steps)])
    make = synthesis if legendre.shape[2] // waves % LANES == 0 else plain_synthesis
    table = slot_table(where, legendre, near[-1])
    grid = make(where, near, got, table, waves)
    order = [(d, bits) for d in reversed(range(waves)) for bits in (2, 3, 0, 1)]
    order.append(order.pop(order.index((0, 0))))
    pieces = [
        swap(grid[4 * d + bits], bits, d) if d or bits else grid[0] for d, bits in order
    ]
    return place(where, slot_column, slots, order, pieces)


def solution(mesh):
    return jax.shard_map(
        functools.partial(shards, mesh),
        mesh=mesh,
        in_specs=(
            P("wave", "term", None),
            P("term", "wave", None, None, None),
            P("term", None),
            P("wave", None, None),
            P(),
        ),
        out_specs=P(None, None, "term", "wave"),
        check_vma=False,
    )
```

```python
import functools

import jax
import jax.numpy as jnp
from jax import lax
from jax.experimental import pallas as pl
from jax.experimental.pallas import tpu as pltpu
from jax.sharding import PartitionSpec as P

F32, BF16, I16, I32 = jnp.float32, jnp.bfloat16, jnp.int16, jnp.int32
LANES = 128
TAIL = 16
STEPS = 64.0
TOP = 32000.0
TINY = 1e-30


def params(mib=8):
    return pltpu.CompilerParams(vmem_limit_bytes=mib * 2**20)


def split(x):
    hi = x.astype(BF16)
    return hi, (x - hi.astype(F32)).astype(BF16)


def encode(x):
    top = jnp.maximum(jnp.max(jnp.abs(x), axis=0, keepdims=True), TINY)
    step = jnp.ceil(jnp.log2(top * (1.0 / TOP)) * STEPS)
    code = jnp.round(x * jnp.exp2(step * (-1.0 / STEPS)))
    return code.astype(I32).astype(I16), step


def put_row(tail, row, values):
    at = lax.broadcasted_iota(I32, tail.shape, 0)
    return jnp.where(at == row, values, tail)


def scales(tail):
    return jnp.exp2(tail.astype(I32).astype(F32) * (1.0 / STEPS))


def message(strips, rows):
    return jax.ShapeDtypeStruct((strips * rows + TAIL, LANES), I16)


def whole(shape):
    return pl.BlockSpec(memory_space=pltpu.VMEM)


def weighted(w_own, w_got, own, got):
    real = imag = 0.0
    for k in range(own.shape[0]):
        for w, block in ((w_own, own[k, 0]), (w_got, got[k])):
            r, j = block[0].astype(F32), block[1].astype(F32)
            real += w[k, 0] * r - w[k, 1] * j
            imag += w[k, 0] * j + w[k, 1] * r
    return real, imag


def share_kernel(after, where, w_own, w_got, own, got, *refs):
    out, tail = refs[after:]
    t = pl.program_id(0)
    size = own.shape[3]
    end = out.shape[0] - TAIL

    @pl.when(t == 0)
    def _():
        tail[...] = jnp.zeros_like(tail)

    for part, value in enumerate(weighted(w_own, w_got, own, got)):
        strip = 2 * t + part
        code, step = encode(value)
        out[pl.ds(pl.multiple_of(strip * size, TAIL), size), :] = code
        tail[...] = put_row(tail[...], strip, step)

    @pl.when(t == pl.num_programs(0) - 1)
    def _():
        out[end:, :] = tail[...].astype(I32).astype(I16)


def own_kernel(where, w_own, w_got, own, got, out):
    for part, value in enumerate(weighted(w_own, w_got, own, got)):
        out[0, part] = value


def share(where, w_own, w_got, inverse, got, first, count, after):
    terms, _, _, size, _ = inverse.shape
    smem = pl.BlockSpec(memory_space=pltpu.SMEM)
    out = message(2 * count, size)
    return pl.pallas_call(
        functools.partial(share_kernel, len(after)),
        out_shape=out,
        grid_spec=pltpu.PrefetchScalarGridSpec(
            num_scalar_prefetch=1,
            grid=(count,),
            in_specs=[smem, smem]
            + operator_specs(terms, size, 2, first)
            + [pl.BlockSpec(memory_space=pl.ANY)] * len(after),
            out_specs=whole(out.shape),
            scratch_shapes=[pltpu.VMEM((TAIL, LANES), F32)],
        ),
        compiler_params=params(),
        cost_estimate=pl.CostEstimate(
            flops=32 * terms * size * LANES * count,
            bytes_accessed=16 * size * LANES * count,
            transcendentals=0,
        ),
        name="share",
    )(where, w_own, w_got, inverse, got, *after)


def operator_specs(terms, size, bits, first):
    return [
        pl.BlockSpec(
            (terms, 1, 2, size, LANES), lambda t, where: (0, where[bits], 0, 0, t + first)
        ),
        pl.BlockSpec((terms, 2, size, LANES), lambda t, where: (0, 0, 0, t + first)),
    ]


def operator(where, w_own, w_got, inverse, got):
    terms, _, _, size, _ = inverse.shape
    tiles = size // LANES
    smem = pl.BlockSpec(memory_space=pltpu.SMEM)
    return pl.pallas_call(
        own_kernel,
        out_shape=jax.ShapeDtypeStruct((tiles, 2, size, LANES), F32),
        grid_spec=pltpu.PrefetchScalarGridSpec(
            num_scalar_prefetch=1,
            grid=(tiles,),
            in_specs=[smem, smem] + operator_specs(terms, size, 0, 0),
            out_specs=pl.BlockSpec((1, 2, size, LANES), lambda t, where: (t, 0, 0, 0)),
        ),
        compiler_params=params(),
        cost_estimate=pl.CostEstimate(
            flops=32 * terms * size * size,
            bytes_accessed=16 * size * size,
            transcendentals=0,
        ),
        name="operator",
    )(where, w_own, w_got, inverse, got)


def table_kernel(where, legendre, after, out):
    out[...] = legendre[0]


def slot_table(where, legendre, after):
    _, size, nlat = legendre.shape
    return pl.pallas_call(
        table_kernel,
        out_shape=jax.ShapeDtypeStruct((size, nlat), legendre.dtype),
        grid_spec=pltpu.PrefetchScalarGridSpec(
            num_scalar_prefetch=1,
            grid=(size // LANES,),
            in_specs=[
                pl.BlockSpec((1, LANES, nlat), lambda i, where: (where[0], i, 0)),
                pl.BlockSpec(memory_space=pl.ANY),
            ],
            out_specs=pl.BlockSpec((LANES, nlat), lambda i, where: (i, 0)),
        ),
        compiler_params=params(),
        name="table",
    )(where, legendre, after)


def build_kernel(first, held, own, *refs):
    got, op = refs[: len(held)], refs[-1]
    size = own.shape[2]
    sources = [(ref, i) for ref, n in zip(got, held) for i in range(n)]
    for t, (ref, i) in enumerate(sources):
        table = scales(ref[ref.shape[0] - TAIL :, :])
        real, imag = (
            own[first + t, strip % 2]
            + ref[strip * size : (strip + 1) * size, :].astype(I32).astype(F32)
            * table[strip : strip + 1, :]
            for strip in (2 * i, 2 * i + 1)
        )
        for level, (r, j) in enumerate(zip(split(real), split(imag))):
            op[t, level, :size, :LANES] = r
            op[t, level, :size, LANES:] = j
            op[t, level, size:, :LANES] = -j
            op[t, level, size:, LANES:] = r


def build(own, got, first, held, after):
    size = own.shape[2]
    out = jax.ShapeDtypeStruct((sum(held), 2, 2 * size, 2 * LANES), BF16)
    return pl.pallas_call(
        functools.partial(build_kernel, first, held),
        out_shape=out,
        in_specs=[whole(x.shape) for x in (own, *got)]
        + [pl.BlockSpec(memory_space=pl.ANY)] * len(after),
        out_specs=whole(out.shape),
        compiler_params=params(),
        cost_estimate=pl.CostEstimate(
            flops=8 * out.size, bytes_accessed=4 * out.size, transcendentals=0
        ),
        name="build",
    )(own, *got, *after)


def product_kernel(pieces, kept, after, *refs):
    parts, op = refs[:pieces], refs[pieces]
    refs = refs[pieces + 1 + after :]
    outs, full = refs[:pieces], refs[pieces]
    tiles = op.shape[0]
    rows = parts[0].shape[0]
    for i, part in enumerate(parts):
        full[i * rows : (i + 1) * rows, :] = part[...]
    tails = {q: jnp.zeros((TAIL, LANES), F32) for q in range(pieces) if q not in kept}
    for t in range(tiles):
        x = full[...]
        acc = jnp.dot(x, op[t, 0], preferred_element_type=F32)
        acc += jnp.dot(x, op[t, 1], preferred_element_type=F32)
        for q in range(pieces):
            block = acc[q * rows : (q + 1) * rows]
            if q in kept:
                outs[q][t] = block
                continue
            for part in range(2):
                strip = 2 * t + part
                code, step = encode(block[:, part * LANES : (part + 1) * LANES])
                outs[q][strip * rows : (strip + 1) * rows, :] = code
                tails[q] = put_row(tails[q], strip, step)
    for q, tail in tails.items():
        outs[q][2 * tiles * rows :, :] = tail.astype(I32).astype(I16)


def product(parts, op, kept, after):
    tiles = op.shape[0]
    rows, width = parts[0].shape
    count = len(parts)
    plain = jax.ShapeDtypeStruct((tiles, rows, 2 * LANES), F32)
    send = message(2 * tiles, rows)
    return pl.pallas_call(
        functools.partial(product_kernel, count, kept, len(after)),
        out_shape=[plain if q in kept else send for q in range(count)],
        in_specs=[whole(x.shape) for x in (*parts, op)]
        + [pl.BlockSpec(memory_space=pl.ANY)] * len(after),
        out_specs=[whole(send.shape)] * count,
        scratch_shapes=[pltpu.VMEM((count * rows, width), BF16)],
        compiler_params=params(),
        cost_estimate=pl.CostEstimate(
            flops=8 * count * rows * width * tiles * LANES,
            bytes_accessed=2 * op.size + 2 * count * rows * width,
            transcendentals=0,
        ),
        name="product",
    )(*parts, op, *after)


def fold_kernel(own, got, *refs):
    out = refs[-1]
    tail = jnp.zeros((TAIL, LANES), F32)
    sums = {}

    def write(tile, part, total):
        sums[2 * tile + part] = total

    add_up([own], [[got]], write)
    rows = own.shape[1]
    for strip, total in sums.items():
        code, step = encode(total)
        out[strip * rows : (strip + 1) * rows, :] = code
        tail = put_row(tail, strip, step)
    out[out.shape[0] - TAIL :, :] = tail.astype(I32).astype(I16)


def fold(own, got, after):
    return pl.pallas_call(
        fold_kernel,
        out_shape=jax.ShapeDtypeStruct(got.shape, got.dtype),
        in_specs=[whole(own.shape), whole(got.shape)]
        + [pl.BlockSpec(memory_space=pl.ANY)] * len(after),
        out_specs=whole(got.shape),
        compiler_params=params(),
        cost_estimate=pl.CostEstimate(
            flops=12 * own.size, bytes_accessed=8 * own.size, transcendentals=0
        ),
        name="fold",
    )(own, got, *after)


def add_up(near, got, write):
    base = 0
    for own, parts in zip(near, got):
        tiles, rows, _ = own.shape
        tables = [scales(part[2 * tiles * rows :, :]) for part in parts]
        for t in range(tiles):
            for part in range(2):
                strip = 2 * t + part
                total = own[t, :, part * LANES : (part + 1) * LANES]
                for ref, table in zip(parts, tables):
                    code = ref[strip * rows : (strip + 1) * rows, :]
                    total += code.astype(I32).astype(F32) * table[strip : strip + 1, :]
                write(base + t, part, total)
        base += tiles


def unpack(refs, counts):
    near, refs, got = refs[: len(counts)], refs[len(counts) :], []
    for count in counts:
        got.append(refs[:count])
        refs = refs[count:]
    return near, got, refs


def synthesis_kernel(bands, counts, where, *refs):
    near, got, rest = unpack(refs, counts)
    table, outs, values = rest[0], rest[1:-1], rest[-1]
    rows = near[0].shape[1]
    quarter = rows // 4
    band = table.shape[1] // bands

    def write(tile, part, total):
        for level, value in enumerate(split(total)):
            values[
                level, part * rows : (part + 1) * rows, tile * LANES : (tile + 1) * LANES
            ] = value

    add_up(near, got, write)
    for d in reversed(range(bands)):
        start = pl.multiple_of((where[4] ^ d) * band, LANES)
        columns = table[:, pl.ds(start, band)]
        grid = jnp.dot(values[0], columns, preferred_element_type=F32)
        grid += jnp.dot(values[1], columns, preferred_element_type=F32)
        for side in range(4):
            out = outs[4 * d + side]
            if len(out.shape) == 3:
                for part in range(2):
                    start = part * rows + side * quarter
                    out[part] = grid[start : start + quarter]
                continue
            tail = jnp.zeros((TAIL, LANES), F32)
            for part in range(2):
                start = part * rows + side * quarter
                for k in range(band // LANES):
                    strip = 2 * k + part
                    code, step = encode(
                        grid[start : start + quarter, k * LANES : (k + 1) * LANES]
                    )
                    out[strip * quarter : (strip + 1) * quarter, :] = code
                    tail = put_row(tail, strip, step)
            out[out.shape[0] - TAIL :, :] = tail.astype(I32).astype(I16)


def synthesis(where, near, got, table, bands):
    rows = near[0].shape[1]
    size, nlat = table.shape
    band = nlat // bands
    send = message(2 * band // LANES, rows // 4)
    outs = [jax.ShapeDtypeStruct((2, rows // 4, band), F32)] + [send] * (4 * bands - 1)
    operands = [*near, *[part for parts in got for part in parts], table]
    return pl.pallas_call(
        functools.partial(synthesis_kernel, bands, [len(parts) for parts in got]),
        out_shape=outs,
        in_specs=[pl.BlockSpec(memory_space=pltpu.SMEM)] + [whole(x.shape) for x in operands],
        out_specs=[whole(out.shape) for out in outs],
        scratch_shapes=[pltpu.VMEM((2, 2 * rows, size), BF16)],
        compiler_params=params(),
        cost_estimate=pl.CostEstimate(
            flops=8 * rows * size * nlat,
            bytes_accessed=2 * size * nlat + 8 * rows * nlat,
            transcendentals=0,
        ),
        name="synthesis",
    )(where, *operands)


def total_kernel(counts, *refs):
    near, got, (out,) = unpack(refs, counts)

    def write(tile, part, total):
        out[part, :, tile * LANES : (tile + 1) * LANES] = total

    add_up(near, got, write)


def plain_synthesis(where, near, got, table, bands):
    rows = near[0].shape[1]
    size, nlat = table.shape
    total = pl.pallas_call(
        functools.partial(total_kernel, [len(parts) for parts in got]),
        out_shape=jax.ShapeDtypeStruct((2, rows, size), F32),
        compiler_params=params(),
        name="total",
    )(*near, *[part for parts in got for part in parts])
    grid = sum(
        jnp.einsum("pcn,nl->pcl", v, table, preferred_element_type=F32) for v in split(total)
    )
    quarter, band = rows // 4, nlat // bands
    return [
        lax.dynamic_slice(grid, (0, side * quarter, (where[4] ^ d) * band), (2, quarter, band))
        for d in range(bands)
        for side in range(4)
    ]


def place_kernel(count, slots, order, where, column, *refs):
    pieces, out, full, sems = refs[:count], refs[count], refs[count + 1], refs[count + 2]
    _, _, rows, lanes = full.shape
    copies = []
    for i, piece in enumerate(pieces):
        if len(piece.shape) == 3:
            full[i] = piece[...]
        else:
            strips = 2 * lanes // LANES
            table = scales(piece[strips * rows :, :])
            for strip in range(strips):
                code = piece[strip * rows : (strip + 1) * rows, :]
                at = strip // 2 * LANES
                full[i, strip % 2, :, at : at + LANES] = (
                    code.astype(I32).astype(F32) * table[strip : strip + 1, :]
                )
        d, bits = order[i]
        slot = column[(where[4] ^ d) * slots + where[bits]]
        copies.append(pltpu.make_async_copy(full.at[i], out.at[slot], sems.at[i]))
        copies[-1].start()
    for copy in copies:
        copy.wait()


def place(where, column, slots, order, pieces):
    count = len(pieces)
    shape = (count,) + pieces[order.index((0, 0))].shape
    smem = pl.BlockSpec(memory_space=pltpu.SMEM)
    return pl.pallas_call(
        functools.partial(place_kernel, count, slots, order),
        out_shape=jax.ShapeDtypeStruct(shape, F32),
        in_specs=[smem, smem] + [whole(piece.shape) for piece in pieces],
        out_specs=pl.BlockSpec(memory_space=pl.ANY),
        scratch_shapes=[pltpu.VMEM(shape, F32), pltpu.SemaphoreType.DMA((count,))],
        compiler_params=params(),
        name="place",
    )(where, column, *pieces)


def pick_kernel(where, *refs):
    count = len(refs) // 2
    for i in range(count):
        refs[count + i][...] = refs[i][0]


def pick(where, state):
    shape = state.shape[1:]
    block = lambda i: pl.BlockSpec((1,) + shape, lambda _, where: (where[i], 0, 0))
    return pl.pallas_call(
        pick_kernel,
        out_shape=[jax.ShapeDtypeStruct(shape, state.dtype)] * 4,
        grid_spec=pltpu.PrefetchScalarGridSpec(
            num_scalar_prefetch=1,
            grid=(1,),
            in_specs=[block(i) for i in range(4)],
            out_specs=[whole(shape)] * 4,
        ),
        compiler_params=params(),
        name="pick",
    )(where, *[state] * 4)


def join_kernel(*refs):
    *parts, _, out = refs
    rows = parts[0].shape[0]
    for i, part in enumerate(parts):
        out[i * rows : (i + 1) * rows, :] = part[...]


def join(parts, after):
    rows, width = parts[0].shape
    return pl.pallas_call(
        join_kernel,
        out_shape=jax.ShapeDtypeStruct((len(parts) * rows, width), parts[0].dtype),
        in_specs=[whole(part.shape) for part in parts] + [pl.BlockSpec(memory_space=pl.ANY)],
        out_specs=whole(None),
        compiler_params=params(),
        name="join",
    )(*parts, after)


def shards(mesh, spectral_state, inverse, term_weights, legendre, slot_column):
    terms, waves = mesh.shape["term"], mesh.shape["wave"]
    slots, cols, width = spectral_state.shape
    size = width // 2
    outer = terms // 4
    me, wave = lax.axis_index("term"), lax.axis_index("wave")
    place_of = me % 4

    def swap(x, term_bits, wave_bits=0):
        pairs = [
            (t * waves + w, (t ^ term_bits) * waves + (w ^ wave_bits))
            for t in range(terms)
            for w in range(waves)
        ]
        return lax.ppermute(x, ("term", "wave"), pairs)

    tiles = size // LANES
    assert slots == 4
    where = jnp.stack([place_of ^ bits for bits in range(4)] + [wave]).astype(I32)
    states = pick(where, spectral_state)
    turned, w_got, *states = lax.optimization_barrier(
        (place_of, swap(term_weights, 1), *states)
    )
    received = [swap(states[bits], bits) for bits in range(1, 4)]
    far, own = (
        swap(lax.dynamic_index_in_dim(inverse, turned ^ bits, 1, keepdims=False), 1)
        for bits in (3, 1)
    )
    last = max(1, 2 * tiles // 5)
    counts = [n for n in (last, tiles - 2 * last, last) if n]
    shares, messages = [], []
    for at, n in enumerate(counts):
        first = sum(counts[:at])
        after = (shares[-1], mine) if shares else ()
        shares.append(share(where, term_weights, w_got, inverse, far, first, n, after))
        messages.append(swap(shares[-1], 2))
        if at == 0:
            mine = operator(where, term_weights, w_got, inverse, own)
            block = join([states[0]] + received, shares[0])
            steps = [3, 1] + list(range(4, outer)) + [2]
            parts = [block] + [swap(block, q * 4) for q in steps[:-1]]
            parts.append(swap(parts[1], 1 * 4))
    near, got = [], []
    ends = [0, len(counts) - 1, len(counts)]
    for start, end in zip(ends, ends[1:]):
        after = [near[-1], got[-1][1]] if near else []
        held = counts[start:end]
        folded = sends[:1] if near else []
        op = build(mine, messages[start:end], sum(counts[:start]), held, folded)
        made = product(parts, op, (0, 1), after)
        relayed = swap(made[-1], 1 * 4)
        sends = [fold(made[1], relayed, got[-1] if got else []), *made[2:-1]]
        near.append(made[0])
        got.append([swap(send, q * 4) for send, q in zip(sends, steps)])
    make = synthesis if legendre.shape[2] // waves % LANES == 0 else plain_synthesis
    table = slot_table(where, legendre, near[-1])
    grid = make(where, near, got, table, waves)
    order = [(d, bits) for d in reversed(range(waves)) for bits in (2, 3, 0, 1)]
    order.append(order.pop(order.index((0, 0))))
    pieces = [
        swap(grid[4 * d + bits], bits, d) if d or bits else grid[0] for d, bits in order
    ]
    return place(where, slot_column, slots, order, pieces)


def solution(mesh):
    return jax.shard_map(
        functools.partial(shards, mesh),
        mesh=mesh,
        in_specs=(
            P("wave", "term", None),
            P("term", "wave", None, None, None),
            P("term", None),
            P("wave", None, None),
            P(),
        ),
        out_specs=P(None, None, "term", "wave"),
        check_vma=False,
    )
```

```python
import functools

import jax
import jax.numpy as jnp
from jax import lax
from jax.experimental import pallas as pl
from jax.experimental.pallas import tpu as pltpu
from jax.sharding import PartitionSpec as P

F32, BF16, I16, I32 = jnp.float32, jnp.bfloat16, jnp.int16, jnp.int32
LANES = 128
TAIL = 16
STEPS = 64.0
TOP = 32000.0
TINY = 1e-30


def params(mib=8):
    return pltpu.CompilerParams(vmem_limit_bytes=mib * 2**20)


def split(x):
    hi = x.astype(BF16)
    return hi, (x - hi.astype(F32)).astype(BF16)


def encode(x):
    top = jnp.maximum(jnp.max(jnp.abs(x), axis=0, keepdims=True), TINY)
    step = jnp.ceil(jnp.log2(top * (1.0 / TOP)) * STEPS)
    code = jnp.round(x * jnp.exp2(step * (-1.0 / STEPS)))
    return code.astype(I32).astype(I16), step


def put_row(tail, row, values):
    at = lax.broadcasted_iota(I32, tail.shape, 0)
    return jnp.where(at == row, values, tail)


def scales(tail):
    return jnp.exp2(tail.astype(I32).astype(F32) * (1.0 / STEPS))


def message(strips, rows):
    return jax.ShapeDtypeStruct((strips * rows + TAIL, LANES), I16)


def whole(shape):
    return pl.BlockSpec(memory_space=pltpu.VMEM)


def weighted(w_own, w_got, own, got):
    real = imag = 0.0
    for k in range(own.shape[0]):
        for w, block in ((w_own, own[k, 0]), (w_got, got[k])):
            r, j = block[0].astype(F32), block[1].astype(F32)
            real += w[k, 0] * r - w[k, 1] * j
            imag += w[k, 0] * j + w[k, 1] * r
    return real, imag


def share_kernel(after, where, w_own, w_got, own, got, *refs):
    out, tail = refs[after:]
    t = pl.program_id(0)
    size = own.shape[3]
    end = out.shape[0] - TAIL

    @pl.when(t == 0)
    def _():
        tail[...] = jnp.zeros_like(tail)

    for part, value in enumerate(weighted(w_own, w_got, own, got)):
        strip = 2 * t + part
        code, step = encode(value)
        out[pl.ds(pl.multiple_of(strip * size, TAIL), size), :] = code
        tail[...] = put_row(tail[...], strip, step)

    @pl.when(t == pl.num_programs(0) - 1)
    def _():
        out[end:, :] = tail[...].astype(I32).astype(I16)


def own_kernel(where, w_own, w_got, own, got, out):
    for part, value in enumerate(weighted(w_own, w_got, own, got)):
        out[0, part] = value


def share(where, w_own, w_got, inverse, got, first, count, after):
    terms, _, _, size, _ = inverse.shape
    smem = pl.BlockSpec(memory_space=pltpu.SMEM)
    out = message(2 * count, size)
    return pl.pallas_call(
        functools.partial(share_kernel, len(after)),
        out_shape=out,
        grid_spec=pltpu.PrefetchScalarGridSpec(
            num_scalar_prefetch=1,
            grid=(count,),
            in_specs=[smem, smem]
            + operator_specs(terms, size, 2, first)
            + [pl.BlockSpec(memory_space=pl.ANY)] * len(after),
            out_specs=whole(out.shape),
            scratch_shapes=[pltpu.VMEM((TAIL, LANES), F32)],
        ),
        compiler_params=params(),
        cost_estimate=pl.CostEstimate(
            flops=32 * terms * size * LANES * count,
            bytes_accessed=16 * size * LANES * count,
            transcendentals=0,
        ),
        name="share",
    )(where, w_own, w_got, inverse, got, *after)


def operator_specs(terms, size, bits, first):
    return [
        pl.BlockSpec(
            (terms, 1, 2, size, LANES), lambda t, where: (0, where[bits], 0, 0, t + first)
        ),
        pl.BlockSpec((terms, 2, size, LANES), lambda t, where: (0, 0, 0, t + first)),
    ]


def operator(where, w_own, w_got, inverse, got):
    terms, _, _, size, _ = inverse.shape
    tiles = size // LANES
    smem = pl.BlockSpec(memory_space=pltpu.SMEM)
    return pl.pallas_call(
        own_kernel,
        out_shape=jax.ShapeDtypeStruct((tiles, 2, size, LANES), F32),
        grid_spec=pltpu.PrefetchScalarGridSpec(
            num_scalar_prefetch=1,
            grid=(tiles,),
            in_specs=[smem, smem] + operator_specs(terms, size, 0, 0),
            out_specs=pl.BlockSpec((1, 2, size, LANES), lambda t, where: (t, 0, 0, 0)),
        ),
        compiler_params=params(),
        cost_estimate=pl.CostEstimate(
            flops=32 * terms * size * size,
            bytes_accessed=16 * size * size,
            transcendentals=0,
        ),
        name="operator",
    )(where, w_own, w_got, inverse, got)


def table_kernel(where, legendre, after, out):
    out[...] = legendre[0]


def slot_table(where, legendre, after):
    _, size, nlat = legendre.shape
    return pl.pallas_call(
        table_kernel,
        out_shape=jax.ShapeDtypeStruct((size, nlat), legendre.dtype),
        grid_spec=pltpu.PrefetchScalarGridSpec(
            num_scalar_prefetch=1,
            grid=(size // LANES,),
            in_specs=[
                pl.BlockSpec((1, LANES, nlat), lambda i, where: (where[0], i, 0)),
                pl.BlockSpec(memory_space=pl.ANY),
            ],
            out_specs=pl.BlockSpec((LANES, nlat), lambda i, where: (i, 0)),
        ),
        compiler_params=params(),
        name="table",
    )(where, legendre, after)


def build_kernel(first, held, own, *refs):
    got, op = refs[: len(held)], refs[-1]
    size = own.shape[2]
    sources = [(ref, i) for ref, n in zip(got, held) for i in range(n)]
    for t, (ref, i) in enumerate(sources):
        table = scales(ref[ref.shape[0] - TAIL :, :])
        real, imag = (
            own[first + t, strip % 2]
            + ref[strip * size : (strip + 1) * size, :].astype(I32).astype(F32)
            * table[strip : strip + 1, :]
            for strip in (2 * i, 2 * i + 1)
        )
        for level, (r, j) in enumerate(zip(split(real), split(imag))):
            op[t, level, :size, :LANES] = r
            op[t, level, :size, LANES:] = j
            op[t, level, size:, :LANES] = -j
            op[t, level, size:, LANES:] = r


def build(own, got, first, held, after):
    size = own.shape[2]
    out = jax.ShapeDtypeStruct((sum(held), 2, 2 * size, 2 * LANES), BF16)
    return pl.pallas_call(
        functools.partial(build_kernel, first, held),
        out_shape=out,
        in_specs=[whole(x.shape) for x in (own, *got)]
        + [pl.BlockSpec(memory_space=pl.ANY)] * len(after),
        out_specs=whole(out.shape),
        compiler_params=params(),
        cost_estimate=pl.CostEstimate(
            flops=8 * out.size, bytes_accessed=4 * out.size, transcendentals=0
        ),
        name="build",
    )(own, *got, *after)


def product_kernel(pieces, kept, after, *refs):
    parts, op = refs[:pieces], refs[pieces]
    refs = refs[pieces + 1 + after :]
    outs, full = refs[:pieces], refs[pieces]
    tiles = op.shape[0]
    rows = parts[0].shape[0]
    for i, part in enumerate(parts):
        full[i * rows : (i + 1) * rows, :] = part[...]
    tails = {q: jnp.zeros((TAIL, LANES), F32) for q in range(pieces) if q not in kept}
    for t in range(tiles):
        x = full[...]
        acc = jnp.dot(x, op[t, 0], preferred_element_type=F32)
        acc += jnp.dot(x, op[t, 1], preferred_element_type=F32)
        for q in range(pieces):
            block = acc[q * rows : (q + 1) * rows]
            if q in kept:
                outs[q][t] = block
                continue
            for part in range(2):
                strip = 2 * t + part
                code, step = encode(block[:, part * LANES : (part + 1) * LANES])
                outs[q][strip * rows : (strip + 1) * rows, :] = code
                tails[q] = put_row(tails[q], strip, step)
    for q, tail in tails.items():
        outs[q][2 * tiles * rows :, :] = tail.astype(I32).astype(I16)


def product(parts, op, kept, after):
    tiles = op.shape[0]
    rows, width = parts[0].shape
    count = len(parts)
    plain = jax.ShapeDtypeStruct((tiles, rows, 2 * LANES), F32)
    send = message(2 * tiles, rows)
    return pl.pallas_call(
        functools.partial(product_kernel, count, kept, len(after)),
        out_shape=[plain if q in kept else send for q in range(count)],
        in_specs=[whole(x.shape) for x in (*parts, op)]
        + [pl.BlockSpec(memory_space=pl.ANY)] * len(after),
        out_specs=[whole(send.shape)] * count,
        scratch_shapes=[pltpu.VMEM((count * rows, width), BF16)],
        compiler_params=params(),
        cost_estimate=pl.CostEstimate(
            flops=8 * count * rows * width * tiles * LANES,
            bytes_accessed=2 * op.size + 2 * count * rows * width,
            transcendentals=0,
        ),
        name="product",
    )(*parts, op, *after)


def fold_kernel(own, got, *refs):
    out = refs[-1]
    tail = jnp.zeros((TAIL, LANES), F32)
    sums = {}

    def write(tile, part, total):
        sums[2 * tile + part] = total

    add_up([own], [[got]], write)
    rows = own.shape[1]
    for strip, total in sums.items():
        code, step = encode(total)
        out[strip * rows : (strip + 1) * rows, :] = code
        tail = put_row(tail, strip, step)
    out[out.shape[0] - TAIL :, :] = tail.astype(I32).astype(I16)


def fold(own, got, after):
    return pl.pallas_call(
        fold_kernel,
        out_shape=jax.ShapeDtypeStruct(got.shape, got.dtype),
        in_specs=[whole(own.shape), whole(got.shape)]
        + [pl.BlockSpec(memory_space=pl.ANY)] * len(after),
        out_specs=whole(got.shape),
        compiler_params=params(),
        cost_estimate=pl.CostEstimate(
            flops=12 * own.size, bytes_accessed=8 * own.size, transcendentals=0
        ),
        name="fold",
    )(own, got, *after)


def add_up(near, got, write):
    base = 0
    for own, parts in zip(near, got):
        tiles, rows, _ = own.shape
        tables = [scales(part[2 * tiles * rows :, :]) for part in parts]
        for t in range(tiles):
            for part in range(2):
                strip = 2 * t + part
                total = own[t, :, part * LANES : (part + 1) * LANES]
                for ref, table in zip(parts, tables):
                    code = ref[strip * rows : (strip + 1) * rows, :]
                    total += code.astype(I32).astype(F32) * table[strip : strip + 1, :]
                write(base + t, part, total)
        base += tiles


def unpack(refs, counts):
    near, refs, got = refs[: len(counts)], refs[len(counts) :], []
    for count in counts:
        got.append(refs[:count])
        refs = refs[count:]
    return near, got, refs


def synthesis_kernel(bands, counts, where, *refs):
    near, got, rest = unpack(refs, counts)
    table, outs, values = rest[0], rest[1:-1], rest[-1]
    rows = near[0].shape[1]
    quarter = rows // 4
    band = table.shape[1] // bands

    def write(tile, part, total):
        for level, value in enumerate(split(total)):
            values[
                level, part * rows : (part + 1) * rows, tile * LANES : (tile + 1) * LANES
            ] = value

    add_up(near, got, write)
    for d in reversed(range(bands)):
        start = pl.multiple_of((where[4] ^ d) * band, LANES)
        columns = table[:, pl.ds(start, band)]
        grid = jnp.dot(values[0], columns, preferred_element_type=F32)
        grid += jnp.dot(values[1], columns, preferred_element_type=F32)
        for side in range(4):
            out = outs[4 * d + side]
            if len(out.shape) == 3:
                for part in range(2):
                    start = part * rows + side * quarter
                    out[part] = grid[start : start + quarter]
                continue
            tail = jnp.zeros((TAIL, LANES), F32)
            for part in range(2):
                start = part * rows + side * quarter
                for k in range(band // LANES):
                    strip = 2 * k + part
                    code, step = encode(
                        grid[start : start + quarter, k * LANES : (k + 1) * LANES]
                    )
                    out[strip * quarter : (strip + 1) * quarter, :] = code
                    tail = put_row(tail, strip, step)
            out[out.shape[0] - TAIL :, :] = tail.astype(I32).astype(I16)


def synthesis(where, near, got, table, bands):
    rows = near[0].shape[1]
    size, nlat = table.shape
    band = nlat // bands
    send = message(2 * band // LANES, rows // 4)
    outs = [jax.ShapeDtypeStruct((2, rows // 4, band), F32)] + [send] * (4 * bands - 1)
    operands = [*near, *[part for parts in got for part in parts], table]
    return pl.pallas_call(
        functools.partial(synthesis_kernel, bands, [len(parts) for parts in got]),
        out_shape=outs,
        in_specs=[pl.BlockSpec(memory_space=pltpu.SMEM)] + [whole(x.shape) for x in operands],
        out_specs=[whole(out.shape) for out in outs],
        scratch_shapes=[pltpu.VMEM((2, 2 * rows, size), BF16)],
        compiler_params=params(),
        cost_estimate=pl.CostEstimate(
            flops=8 * rows * size * nlat,
            bytes_accessed=2 * size * nlat + 8 * rows * nlat,
            transcendentals=0,
        ),
        name="synthesis",
    )(where, *operands)


def total_kernel(counts, *refs):
    near, got, (out,) = unpack(refs, counts)

    def write(tile, part, total):
        out[part, :, tile * LANES : (tile + 1) * LANES] = total

    add_up(near, got, write)


def plain_synthesis(where, near, got, table, bands):
    rows = near[0].shape[1]
    size, nlat = table.shape
    total = pl.pallas_call(
        functools.partial(total_kernel, [len(parts) for parts in got]),
        out_shape=jax.ShapeDtypeStruct((2, rows, size), F32),
        compiler_params=params(),
        name="total",
    )(*near, *[part for parts in got for part in parts])
    grid = sum(
        jnp.einsum("pcn,nl->pcl", v, table, preferred_element_type=F32) for v in split(total)
    )
    quarter, band = rows // 4, nlat // bands
    return [
        lax.dynamic_slice(grid, (0, side * quarter, (where[4] ^ d) * band), (2, quarter, band))
        for d in range(bands)
        for side in range(4)
    ]


def place_kernel(count, slots, order, where, column, *refs):
    pieces, out, full, sems = refs[:count], refs[count], refs[count + 1], refs[count + 2]
    _, _, rows, lanes = full.shape
    copies = []
    for i, piece in sorted(enumerate(pieces), key=lambda at: len(at[1].shape) != 3):
        source = piece
        if len(piece.shape) != 3:
            source = full.at[i]
            strips = 2 * lanes // LANES
            table = scales(piece[strips * rows :, :])
            for strip in range(strips):
                code = piece[strip * rows : (strip + 1) * rows, :]
                at = strip // 2 * LANES
                full[i, strip % 2, :, at : at + LANES] = (
                    code.astype(I32).astype(F32) * table[strip : strip + 1, :]
                )
        d, bits = order[i]
        slot = column[(where[4] ^ d) * slots + where[bits]]
        copies.append(pltpu.make_async_copy(source, out.at[slot], sems.at[i]))
        copies[-1].start()
    for copy in copies:
        copy.wait()


def place(where, column, slots, order, pieces):
    count = len(pieces)
    shape = (count,) + pieces[order.index((0, 0))].shape
    smem = pl.BlockSpec(memory_space=pltpu.SMEM)
    return pl.pallas_call(
        functools.partial(place_kernel, count, slots, order),
        out_shape=jax.ShapeDtypeStruct(shape, F32),
        in_specs=[smem, smem] + [whole(piece.shape) for piece in pieces],
        out_specs=pl.BlockSpec(memory_space=pl.ANY),
        scratch_shapes=[pltpu.VMEM(shape, F32), pltpu.SemaphoreType.DMA((count,))],
        compiler_params=params(),
        name="place",
    )(where, column, *pieces)


def pick_kernel(where, *refs):
    count = len(refs) // 2
    for i in range(count):
        refs[count + i][...] = refs[i][0]


def pick(where, state):
    shape = state.shape[1:]
    block = lambda i: pl.BlockSpec((1,) + shape, lambda _, where: (where[i], 0, 0))
    return pl.pallas_call(
        pick_kernel,
        out_shape=[jax.ShapeDtypeStruct(shape, state.dtype)] * 4,
        grid_spec=pltpu.PrefetchScalarGridSpec(
            num_scalar_prefetch=1,
            grid=(1,),
            in_specs=[block(i) for i in range(4)],
            out_specs=[whole(shape)] * 4,
        ),
        compiler_params=params(),
        name="pick",
    )(where, *[state] * 4)


def join_kernel(*refs):
    *parts, _, out = refs
    rows = parts[0].shape[0]
    for i, part in enumerate(parts):
        out[i * rows : (i + 1) * rows, :] = part[...]


def join(parts, after):
    rows, width = parts[0].shape
    return pl.pallas_call(
        join_kernel,
        out_shape=jax.ShapeDtypeStruct((len(parts) * rows, width), parts[0].dtype),
        in_specs=[whole(part.shape) for part in parts] + [pl.BlockSpec(memory_space=pl.ANY)],
        out_specs=whole(None),
        compiler_params=params(),
        name="join",
    )(*parts, after)


def shards(mesh, spectral_state, inverse, term_weights, legendre, slot_column):
    terms, waves = mesh.shape["term"], mesh.shape["wave"]
    slots, cols, width = spectral_state.shape
    size = width // 2
    outer = terms // 4
    me, wave = lax.axis_index("term"), lax.axis_index("wave")
    place_of = me % 4

    def swap(x, term_bits, wave_bits=0):
        pairs = [
            (t * waves + w, (t ^ term_bits) * waves + (w ^ wave_bits))
            for t in range(terms)
            for w in range(waves)
        ]
        return lax.ppermute(x, ("term", "wave"), pairs)

    tiles = size // LANES
    assert slots == 4
    where = jnp.stack([place_of ^ bits for bits in range(4)] + [wave]).astype(I32)
    states = pick(where, spectral_state)
    turned, w_got, *states = lax.optimization_barrier(
        (place_of, swap(term_weights, 1), *states)
    )
    received = [swap(states[bits], bits) for bits in range(1, 4)]
    far, own = (
        swap(lax.dynamic_index_in_dim(inverse, turned ^ bits, 1, keepdims=False), 1)
        for bits in (3, 1)
    )
    last = max(1, 2 * tiles // 5)
    counts = [n for n in (last, tiles - 2 * last, last) if n]
    shares, messages = [], []
    for at, n in enumerate(counts):
        first = sum(counts[:at])
        after = (shares[-1], mine) if shares else ()
        shares.append(share(where, term_weights, w_got, inverse, far, first, n, after))
        messages.append(swap(shares[-1], 2))
        if at == 0:
            mine = operator(where, term_weights, w_got, inverse, own)
            block = join([states[0]] + received, shares[0])
            steps = [3, 1] + list(range(4, outer)) + [2]
            parts = [block] + [swap(block, q * 4) for q in steps[:-1]]
            parts.append(swap(parts[1], 1 * 4))
    near, got = [], []
    ends = [0, len(counts) - 1, len(counts)]
    for start, end in zip(ends, ends[1:]):
        after = [near[-1], got[-1][1]] if near else []
        held = counts[start:end]
        folded = sends[:1] if near else []
        op = build(mine, messages[start:end], sum(counts[:start]), held, folded)
        made = product(parts, op, (0, 1), after)
        relayed = swap(made[-1], 1 * 4)
        sends = [fold(made[1], relayed, got[-1] if got else []), *made[2:-1]]
        near.append(made[0])
        got.append([swap(send, q * 4) for send, q in zip(sends, steps)])
    make = synthesis if legendre.shape[2] // waves % LANES == 0 else plain_synthesis
    table = slot_table(where, legendre, near[-1])
    grid = make(where, near, got, table, waves)
    order = [(d, bits) for d in reversed(range(waves)) for bits in (2, 3, 0, 1)]
    order.append(order.pop(order.index((0, 0))))
    pieces = [
        swap(grid[4 * d + bits], bits, d) if d or bits else grid[0] for d, bits in order
    ]
    return place(where, slot_column, slots, order, pieces)


def solution(mesh):
    return jax.shard_map(
        functools.partial(shards, mesh),
        mesh=mesh,
        in_specs=(
            P("wave", "term", None),
            P("term", "wave", None, None, None),
            P("term", None),
            P("wave", None, None),
            P(),
        ),
        out_specs=P(None, None, "term", "wave"),
        check_vma=False,
    )
```

```python
import functools

import jax
import jax.numpy as jnp
from jax import lax
from jax.experimental import pallas as pl
from jax.experimental.pallas import tpu as pltpu
from jax.sharding import PartitionSpec as P

F32, BF16, I16, I32 = jnp.float32, jnp.bfloat16, jnp.int16, jnp.int32
LANES = 128
TAIL = 16
STEPS = 64.0
TOP = 32000.0
TINY = 1e-30


def params(mib=8):
    return pltpu.CompilerParams(vmem_limit_bytes=mib * 2**20)


def split(x):
    hi = x.astype(BF16)
    return hi, (x - hi.astype(F32)).astype(BF16)


def encode(x):
    top = jnp.maximum(jnp.max(jnp.abs(x), axis=0, keepdims=True), TINY)
    step = jnp.ceil(jnp.log2(top * (1.0 / TOP)) * STEPS)
    code = jnp.round(x * jnp.exp2(step * (-1.0 / STEPS)))
    return code.astype(I32).astype(I16), step


def put_row(tail, row, values):
    at = lax.broadcasted_iota(I32, tail.shape, 0)
    return jnp.where(at == row, values, tail)


def scales(tail):
    return jnp.exp2(tail.astype(I32).astype(F32) * (1.0 / STEPS))


def message(strips, rows):
    return jax.ShapeDtypeStruct((strips * rows + TAIL, LANES), I16)


def whole(shape):
    return pl.BlockSpec(memory_space=pltpu.VMEM)


def weighted(w_own, w_got, own, got):
    real = imag = 0.0
    for k in range(own.shape[0]):
        for w, block in ((w_own, own[k, 0]), (w_got, got[k])):
            r, j = block[0].astype(F32), block[1].astype(F32)
            real += w[k, 0] * r - w[k, 1] * j
            imag += w[k, 0] * j + w[k, 1] * r
    return real, imag


def share_kernel(after, where, w_own, w_got, own, got, *refs):
    out, tail = refs[after:]
    t = pl.program_id(0)
    size = own.shape[3]
    end = out.shape[0] - TAIL

    @pl.when(t == 0)
    def _():
        tail[...] = jnp.zeros_like(tail)

    for part, value in enumerate(weighted(w_own, w_got, own, got)):
        strip = 2 * t + part
        code, step = encode(value)
        out[pl.ds(pl.multiple_of(strip * size, TAIL), size), :] = code
        tail[...] = put_row(tail[...], strip, step)

    @pl.when(t == pl.num_programs(0) - 1)
    def _():
        out[end:, :] = tail[...].astype(I32).astype(I16)


def own_kernel(where, w_own, w_got, own, got, out):
    for part, value in enumerate(weighted(w_own, w_got, own, got)):
        out[0, part] = value


def share(where, w_own, w_got, inverse, got, first, count, after):
    terms, _, _, size, _ = inverse.shape
    smem = pl.BlockSpec(memory_space=pltpu.SMEM)
    out = message(2 * count, size)
    return pl.pallas_call(
        functools.partial(share_kernel, len(after)),
        out_shape=out,
        grid_spec=pltpu.PrefetchScalarGridSpec(
            num_scalar_prefetch=1,
            grid=(count,),
            in_specs=[smem, smem]
            + operator_specs(terms, size, 2, first)
            + [pl.BlockSpec(memory_space=pl.ANY)] * len(after),
            out_specs=whole(out.shape),
            scratch_shapes=[pltpu.VMEM((TAIL, LANES), F32)],
        ),
        compiler_params=params(),
        cost_estimate=pl.CostEstimate(
            flops=32 * terms * size * LANES * count,
            bytes_accessed=16 * size * LANES * count,
            transcendentals=0,
        ),
        name="share",
    )(where, w_own, w_got, inverse, got, *after)


def operator_specs(terms, size, bits, first):
    return [
        pl.BlockSpec(
            (terms, 1, 2, size, LANES), lambda t, where: (0, where[bits], 0, 0, t + first)
        ),
        pl.BlockSpec((terms, 2, size, LANES), lambda t, where: (0, 0, 0, t + first)),
    ]


def operator(where, w_own, w_got, inverse, got):
    terms, _, _, size, _ = inverse.shape
    tiles = size // LANES
    smem = pl.BlockSpec(memory_space=pltpu.SMEM)
    return pl.pallas_call(
        own_kernel,
        out_shape=jax.ShapeDtypeStruct((tiles, 2, size, LANES), F32),
        grid_spec=pltpu.PrefetchScalarGridSpec(
            num_scalar_prefetch=1,
            grid=(tiles,),
            in_specs=[smem, smem] + operator_specs(terms, size, 0, 0),
            out_specs=pl.BlockSpec((1, 2, size, LANES), lambda t, where: (t, 0, 0, 0)),
        ),
        compiler_params=params(),
        cost_estimate=pl.CostEstimate(
            flops=32 * terms * size * size,
            bytes_accessed=16 * size * size,
            transcendentals=0,
        ),
        name="operator",
    )(where, w_own, w_got, inverse, got)


def table_kernel(where, legendre, after, out):
    out[...] = legendre[0]


def slot_table(where, legendre, after):
    _, size, nlat = legendre.shape
    return pl.pallas_call(
        table_kernel,
        out_shape=jax.ShapeDtypeStruct((size, nlat), legendre.dtype),
        grid_spec=pltpu.PrefetchScalarGridSpec(
            num_scalar_prefetch=1,
            grid=(size // LANES,),
            in_specs=[
                pl.BlockSpec((1, LANES, nlat), lambda i, where: (where[0], i, 0)),
                pl.BlockSpec(memory_space=pl.ANY),
            ],
            out_specs=pl.BlockSpec((LANES, nlat), lambda i, where: (i, 0)),
        ),
        compiler_params=params(),
        name="table",
    )(where, legendre, after)


def build_kernel(first, held, own, *refs):
    got, op = refs[: len(held)], refs[-1]
    size = own.shape[2]
    sources = [(ref, i) for ref, n in zip(got, held) for i in range(n)]
    for t, (ref, i) in enumerate(sources):
        table = scales(ref[ref.shape[0] - TAIL :, :])
        real, imag = (
            own[first + t, strip % 2]
            + ref[strip * size : (strip + 1) * size, :].astype(I32).astype(F32)
            * table[strip : strip + 1, :]
            for strip in (2 * i, 2 * i + 1)
        )
        for level, (r, j) in enumerate(zip(split(real), split(imag))):
            op[t, level, :size, :LANES] = r
            op[t, level, :size, LANES:] = j
            op[t, level, size:, :LANES] = -j
            op[t, level, size:, LANES:] = r


def build(own, got, first, held, after):
    size = own.shape[2]
    out = jax.ShapeDtypeStruct((sum(held), 2, 2 * size, 2 * LANES), BF16)
    return pl.pallas_call(
        functools.partial(build_kernel, first, held),
        out_shape=out,
        in_specs=[whole(x.shape) for x in (own, *got)]
        + [pl.BlockSpec(memory_space=pl.ANY)] * len(after),
        out_specs=whole(out.shape),
        compiler_params=params(),
        cost_estimate=pl.CostEstimate(
            flops=8 * out.size, bytes_accessed=4 * out.size, transcendentals=0
        ),
        name="build",
    )(own, *got, *after)


def product_kernel(pieces, kept, after, *refs):
    parts, op = refs[:pieces], refs[pieces]
    refs = refs[pieces + 1 + after :]
    outs, full = refs[:pieces], refs[pieces]
    tiles = op.shape[0]
    rows = parts[0].shape[0]
    for i, part in enumerate(parts):
        full[i * rows : (i + 1) * rows, :] = part[...]
    tails = {q: jnp.zeros((TAIL, LANES), F32) for q in range(pieces) if q not in kept}
    for t in range(tiles):
        x = full[...]
        acc = jnp.dot(x, op[t, 0], preferred_element_type=F32)
        acc += jnp.dot(x, op[t, 1], preferred_element_type=F32)
        for q in range(pieces):
            block = acc[q * rows : (q + 1) * rows]
            if q in kept:
                outs[q][t] = block
                continue
            for part in range(2):
                strip = 2 * t + part
                code, step = encode(block[:, part * LANES : (part + 1) * LANES])
                outs[q][strip * rows : (strip + 1) * rows, :] = code
                tails[q] = put_row(tails[q], strip, step)
    for q, tail in tails.items():
        outs[q][2 * tiles * rows :, :] = tail.astype(I32).astype(I16)


def product(parts, op, kept, after):
    tiles = op.shape[0]
    rows, width = parts[0].shape
    count = len(parts)
    plain = jax.ShapeDtypeStruct((tiles, rows, 2 * LANES), F32)
    send = message(2 * tiles, rows)
    return pl.pallas_call(
        functools.partial(product_kernel, count, kept, len(after)),
        out_shape=[plain if q in kept else send for q in range(count)],
        in_specs=[whole(x.shape) for x in (*parts, op)]
        + [pl.BlockSpec(memory_space=pl.ANY)] * len(after),
        out_specs=[whole(send.shape)] * count,
        scratch_shapes=[pltpu.VMEM((count * rows, width), BF16)],
        compiler_params=params(),
        cost_estimate=pl.CostEstimate(
            flops=8 * count * rows * width * tiles * LANES,
            bytes_accessed=2 * op.size + 2 * count * rows * width,
            transcendentals=0,
        ),
        name="product",
    )(*parts, op, *after)


def fold_kernel(own, got, *refs):
    out = refs[-1]
    tail = jnp.zeros((TAIL, LANES), F32)
    sums = {}

    def write(tile, part, total):
        sums[2 * tile + part] = total

    add_up([own], [[got]], write)
    rows = own.shape[1]
    for strip, total in sums.items():
        code, step = encode(total)
        out[strip * rows : (strip + 1) * rows, :] = code
        tail = put_row(tail, strip, step)
    out[out.shape[0] - TAIL :, :] = tail.astype(I32).astype(I16)


def fold(own, got, after):
    return pl.pallas_call(
        fold_kernel,
        out_shape=jax.ShapeDtypeStruct(got.shape, got.dtype),
        in_specs=[whole(own.shape), whole(got.shape)]
        + [pl.BlockSpec(memory_space=pl.ANY)] * len(after),
        out_specs=whole(got.shape),
        compiler_params=params(),
        cost_estimate=pl.CostEstimate(
            flops=12 * own.size, bytes_accessed=8 * own.size, transcendentals=0
        ),
        name="fold",
    )(own, got, *after)


def add_up(near, got, write):
    base = 0
    for own, parts in zip(near, got):
        tiles, rows, _ = own.shape
        tables = [scales(part[2 * tiles * rows :, :]) for part in parts]
        for t in range(tiles):
            for part in range(2):
                strip = 2 * t + part
                total = own[t, :, part * LANES : (part + 1) * LANES]
                for ref, table in zip(parts, tables):
                    code = ref[strip * rows : (strip + 1) * rows, :]
                    total += code.astype(I32).astype(F32) * table[strip : strip + 1, :]
                write(base + t, part, total)
        base += tiles


def unpack(refs, counts):
    near, refs, got = refs[: len(counts)], refs[len(counts) :], []
    for count in counts:
        got.append(refs[:count])
        refs = refs[count:]
    return near, got, refs


def synthesis_kernel(bands, counts, where, *refs):
    near, got, rest = unpack(refs, counts)
    table, outs, values = rest[0], rest[1:-1], rest[-1]
    rows = near[0].shape[1]
    quarter = rows // 4
    band = table.shape[1] // bands

    def write(tile, part, total):
        for level, value in enumerate(split(total)):
            values[
                level, part * rows : (part + 1) * rows, tile * LANES : (tile + 1) * LANES
            ] = value

    add_up(near, got, write)
    for d in reversed(range(bands)):
        start = pl.multiple_of((where[4] ^ d) * band, LANES)
        columns = table[:, pl.ds(start, band)]
        levels = values[...].reshape(4 * rows, values.shape[2])
        grid = jnp.dot(levels, columns, preferred_element_type=F32)
        grid = grid[: 2 * rows] + grid[2 * rows :]
        for side in range(4):
            out = outs[4 * d + side]
            if len(out.shape) == 3:
                for part in range(2):
                    start = part * rows + side * quarter
                    out[part] = grid[start : start + quarter]
                continue
            tail = jnp.zeros((TAIL, LANES), F32)
            for part in range(2):
                start = part * rows + side * quarter
                for k in range(band // LANES):
                    strip = 2 * k + part
                    code, step = encode(
                        grid[start : start + quarter, k * LANES : (k + 1) * LANES]
                    )
                    out[strip * quarter : (strip + 1) * quarter, :] = code
                    tail = put_row(tail, strip, step)
            out[out.shape[0] - TAIL :, :] = tail.astype(I32).astype(I16)


def synthesis(where, near, got, table, bands):
    rows = near[0].shape[1]
    size, nlat = table.shape
    band = nlat // bands
    send = message(2 * band // LANES, rows // 4)
    outs = [jax.ShapeDtypeStruct((2, rows // 4, band), F32)] + [send] * (4 * bands - 1)
    operands = [*near, *[part for parts in got for part in parts], table]
    return pl.pallas_call(
        functools.partial(synthesis_kernel, bands, [len(parts) for parts in got]),
        out_shape=outs,
        in_specs=[pl.BlockSpec(memory_space=pltpu.SMEM)] + [whole(x.shape) for x in operands],
        out_specs=[whole(out.shape) for out in outs],
        scratch_shapes=[pltpu.VMEM((2, 2 * rows, size), BF16)],
        compiler_params=params(),
        cost_estimate=pl.CostEstimate(
            flops=8 * rows * size * nlat,
            bytes_accessed=2 * size * nlat + 8 * rows * nlat,
            transcendentals=0,
        ),
        name="synthesis",
    )(where, *operands)


def total_kernel(counts, *refs):
    near, got, (out,) = unpack(refs, counts)

    def write(tile, part, total):
        out[part, :, tile * LANES : (tile + 1) * LANES] = total

    add_up(near, got, write)


def plain_synthesis(where, near, got, table, bands):
    rows = near[0].shape[1]
    size, nlat = table.shape
    total = pl.pallas_call(
        functools.partial(total_kernel, [len(parts) for parts in got]),
        out_shape=jax.ShapeDtypeStruct((2, rows, size), F32),
        compiler_params=params(),
        name="total",
    )(*near, *[part for parts in got for part in parts])
    grid = sum(
        jnp.einsum("pcn,nl->pcl", v, table, preferred_element_type=F32) for v in split(total)
    )
    quarter, band = rows // 4, nlat // bands
    return [
        lax.dynamic_slice(grid, (0, side * quarter, (where[4] ^ d) * band), (2, quarter, band))
        for d in range(bands)
        for side in range(4)
    ]


def place_kernel(count, slots, order, where, column, *refs):
    pieces, out, full, sems = refs[:count], refs[count], refs[count + 1], refs[count + 2]
    _, _, rows, lanes = full.shape
    copies = []
    for i, piece in sorted(enumerate(pieces), key=lambda at: len(at[1].shape) != 3):
        source = piece
        if len(piece.shape) != 3:
            source = full.at[i]
            strips = 2 * lanes // LANES
            table = scales(piece[strips * rows :, :])
            for strip in range(strips):
                code = piece[strip * rows : (strip + 1) * rows, :]
                at = strip // 2 * LANES
                full[i, strip % 2, :, at : at + LANES] = (
                    code.astype(I32).astype(F32) * table[strip : strip + 1, :]
                )
        d, bits = order[i]
        slot = column[(where[4] ^ d) * slots + where[bits]]
        copies.append(pltpu.make_async_copy(source, out.at[slot], sems.at[i]))
        copies[-1].start()
    for copy in copies:
        copy.wait()


def place(where, column, slots, order, pieces):
    count = len(pieces)
    shape = (count,) + pieces[order.index((0, 0))].shape
    smem = pl.BlockSpec(memory_space=pltpu.SMEM)
    return pl.pallas_call(
        functools.partial(place_kernel, count, slots, order),
        out_shape=jax.ShapeDtypeStruct(shape, F32),
        in_specs=[smem, smem] + [whole(piece.shape) for piece in pieces],
        out_specs=pl.BlockSpec(memory_space=pl.ANY),
        scratch_shapes=[pltpu.VMEM(shape, F32), pltpu.SemaphoreType.DMA((count,))],
        compiler_params=params(),
        name="place",
    )(where, column, *pieces)


def pick_kernel(where, *refs):
    count = len(refs) // 2
    for i in range(count):
        refs[count + i][...] = refs[i][0]


def pick(where, state):
    shape = state.shape[1:]
    block = lambda i: pl.BlockSpec((1,) + shape, lambda _, where: (where[i], 0, 0))
    return pl.pallas_call(
        pick_kernel,
        out_shape=[jax.ShapeDtypeStruct(shape, state.dtype)] * 4,
        grid_spec=pltpu.PrefetchScalarGridSpec(
            num_scalar_prefetch=1,
            grid=(1,),
            in_specs=[block(i) for i in range(4)],
            out_specs=[whole(shape)] * 4,
        ),
        compiler_params=params(),
        name="pick",
    )(where, *[state] * 4)


def join_kernel(*refs):
    *parts, _, out = refs
    rows = parts[0].shape[0]
    for i, part in enumerate(parts):
        out[i * rows : (i + 1) * rows, :] = part[...]


def join(parts, after):
    rows, width = parts[0].shape
    return pl.pallas_call(
        join_kernel,
        out_shape=jax.ShapeDtypeStruct((len(parts) * rows, width), parts[0].dtype),
        in_specs=[whole(part.shape) for part in parts] + [pl.BlockSpec(memory_space=pl.ANY)],
        out_specs=whole(None),
        compiler_params=params(),
        name="join",
    )(*parts, after)


def shards(mesh, spectral_state, inverse, term_weights, legendre, slot_column):
    terms, waves = mesh.shape["term"], mesh.shape["wave"]
    slots, cols, width = spectral_state.shape
    size = width // 2
    outer = terms // 4
    me, wave = lax.axis_index("term"), lax.axis_index("wave")
    place_of = me % 4

    def swap(x, term_bits, wave_bits=0):
        pairs = [
            (t * waves + w, (t ^ term_bits) * waves + (w ^ wave_bits))
            for t in range(terms)
            for w in range(waves)
        ]
        return lax.ppermute(x, ("term", "wave"), pairs)

    tiles = size // LANES
    assert slots == 4
    where = jnp.stack([place_of ^ bits for bits in range(4)] + [wave]).astype(I32)
    states = pick(where, spectral_state)
    turned, w_got, *states = lax.optimization_barrier(
        (place_of, swap(term_weights, 1), *states)
    )
    received = [swap(states[bits], bits) for bits in range(1, 4)]
    far, own = (
        swap(lax.dynamic_index_in_dim(inverse, turned ^ bits, 1, keepdims=False), 1)
        for bits in (3, 1)
    )
    last = max(1, 2 * tiles // 5)
    counts = [n for n in (last, tiles - 2 * last, last) if n]
    shares, messages = [], []
    for at, n in enumerate(counts):
        first = sum(counts[:at])
        after = (shares[-1], mine) if shares else ()
        shares.append(share(where, term_weights, w_got, inverse, far, first, n, after))
        messages.append(swap(shares[-1], 2))
        if at == 0:
            mine = operator(where, term_weights, w_got, inverse, own)
            block = join([states[0]] + received, shares[0])
            steps = [3, 1] + list(range(4, outer)) + [2]
            parts = [block] + [swap(block, q * 4) for q in steps[:-1]]
            parts.append(swap(parts[1], 1 * 4))
    near, got = [], []
    ends = [0, len(counts) - 1, len(counts)]
    for start, end in zip(ends, ends[1:]):
        after = [near[-1], got[-1][1]] if near else []
        held = counts[start:end]
        folded = sends[:1] if near else []
        op = build(mine, messages[start:end], sum(counts[:start]), held, folded)
        made = product(parts, op, (0, 1), after)
        relayed = swap(made[-1], 1 * 4)
        sends = [fold(made[1], relayed, got[-1] if got else []), *made[2:-1]]
        near.append(made[0])
        got.append([swap(send, q * 4) for send, q in zip(sends, steps)])
    make = synthesis if legendre.shape[2] // waves % LANES == 0 else plain_synthesis
    table = slot_table(where, legendre, near[-1])
    grid = make(where, near, got, table, waves)
    order = [(d, bits) for d in reversed(range(waves)) for bits in (2, 3, 0, 1)]
    order.append(order.pop(order.index((0, 0))))
    pieces = [
        swap(grid[4 * d + bits], bits, d) if d or bits else grid[0] for d, bits in order
    ]
    return place(where, slot_column, slots, order, pieces)


def solution(mesh):
    return jax.shard_map(
        functools.partial(shards, mesh),
        mesh=mesh,
        in_specs=(
            P("wave", "term", None),
            P("term", "wave", None, None, None),
            P("term", None),
            P("wave", None, None),
            P(),
        ),
        out_specs=P(None, None, "term", "wave"),
        check_vma=False,
    )
```
